32 devices in a mesh: groups: 2 (over y), feat: 4 (over z), layer: 2 (over x), tok: 2 (over core).
Axes of the slice: x: 2, y: 2, z: 4, core: 2. Of those that a mesh axis runs over, the one named last changes fastest.
Arguments:
- residual_in: float32 [256, 2, 1792], P('groups', 'tok', 'feat'), parts along dimension 0, may hold values from -6 to 6
- attn_scale: float32 [2, 256], P('layer', 'groups'), parts along dimension 1, may hold values from 0.4 to 2.5
- mlp_scale: float32 [2, 256], P('layer', 'groups'), parts along dimension 1, may hold values from 0.4 to 2.5
- patterns: bfloat16 [2, 8, 4, 64, 64], P('layer', None, 'groups'), parts along dimension 2, may hold values from 0.0029907227 to 0.059814453
- lengths: int32 [4], P('groups'), parts along dimension 0, may hold values from 16 to 64
- value_proj: bfloat16 [2, 2, 1792, 1024], P('layer', 'tok', None, 'feat'), may hold values from -0.09375 to 0.09375
- out_proj: bfloat16 [2, 4, 256, 2, 2, 1792], P('layer', None, None, None, 'tok', 'feat'), may hold values from -0.125 to 0.125
- enc_weight: bfloat16 [2, 2, 1792, 512], P('layer', 'tok', None, 'feat'), may hold values from -0.09375 to 0.09375
- enc_bias: float32 [2, 512], P('layer', 'feat'), may hold values from -3 to 3
- dec_weight: bfloat16 [2, 2, 512, 2, 1792], P('layer', None, None, 'tok', 'feat'), may hold values from -0.25 to 0.25
- errors: float32 [2, 256, 2, 1792], P('layer', 'groups', 'tok', 'feat'), parts along dimension 1, may hold values from -4 to 4
- clamp_mode: int32 [2, 16384], P('layer', 'feat'), may hold values from 0 to 2
- clamp_index: int32 [2, 16384], P('layer', 'feat'), may hold values from 0 to 63
- clamp_values: float32 [64], replicated, may hold values from 0.25 to 3
- active_blocks: int32 [2, 4], P('layer', 'feat'), may hold values from 0 to 31
Outputs:
- residual_out: float32 [2, 256, 2, 1792], P('layer', 'groups', 'tok', 'feat'), parts along dimension 1
- features: bfloat16 [2, 256, 512], P('layer', 'groups', 'feat'), parts along dimension 1
The draws below stay inside these ranges and needn't reach their ends.
There are 2 independent parts, one for each index of `groups`. The reference program is written for one: setup_inputs(seed, part) draws one part's arguments, and reference() takes and returns one part's arrays. A program takes and returns all parts, laid end to end along the dimension named above; an argument that names none is the same for every part. Nothing has to cross between parts.
Inputs may be any that keep to these rules, and one draw needn't show every extreme that they name: `clamp_mode`: 0 leaves a feature free, 1 sets it to its table value, 2 multiplies it by its table value. `lengths`: positions at or past a prompt's length are padding.
All inputs are finite; a program needn't handle non-finite values.
Results may differ from the reference program's by a relative error of at most 0.018.
Values may be sent and summed in bfloat16 or wider, within the bound.
No kernel may reach another device: no remote copies, remote signals or barrier semaphores. Data moves between devices by JAX's collectives and lax.ppermute only.
A program may use at most 64 MiB of HBM per device.

```python
import math
import jax
import jax.numpy as jnp

D = 3584
HD = 256
HEADS = 8
KVH = 4
FEATURES = 16384
BLOCK = 128
VALUES = 64
SEQ = 64
PROMPTS = 2
QPK = 2
LAYERS = 2
RANGES = 4
ACT = 512
SHARD_BLOCKS = 32
SLABS = 2
SLAB = 1792
ROWS = 128


def place_ends(values, stream_key, low, high):
    spot = [jax.random.randint(jax.random.fold_in(stream_key, axis), (), 0, length) for axis, length in enumerate(values.shape)]
    widest = values.shape.index(max(values.shape))
    neighbour = spot[:widest] + [(spot[widest] + 1) % values.shape[widest]] + spot[widest + 1:]
    return values.at[tuple(spot)].set(low).at[tuple(neighbour)].set(high)


def level_of(key, shape, pieces, smallest, top_value):
    def one(axis_at, shards_of):
        draws = jax.random.uniform(jax.random.fold_in(jax.random.fold_in(key, 6), axis_at), (shards_of,), jnp.float32, smallest / len(pieces), top_value / len(pieces))
        return jnp.repeat(jnp.exp(draws), shape[axis_at] // shards_of).reshape((-1,) + (1,) * (len(shape) - axis_at - 1))

    factor_of = one(*pieces[0])
    for cut in pieces[1:]:
        factor_of = factor_of * one(*cut)
    return factor_of


def normal_values(own_key, shape, scale, limit, cuts=(), kind=jnp.bfloat16):
    values = jax.random.normal(own_key, shape, jnp.float32) * scale
    if len(cuts) > 0:
        values = level_of(own_key, shape, cuts, -0.22, 0.18) * values
    return jnp.clip(values, min=-limit, max=limit).astype(kind)


def setup_inputs(seed: int = 0, part: int = 0) -> dict:
    keys = jax.random.split(jax.random.key(seed), 16)
    own_keys = jax.random.split(jax.random.fold_in(keys[15], part), 16)
    return {
        "residual_in": normal_values(own_keys[0], (ROWS, SLABS, SLAB), 1.0, 6.0, ((1, 2), (2, 4)), jnp.float32),
        "attn_scale": jnp.clip(jnp.exp(math.log(2.5) - 1.8325814 * jax.random.uniform(own_keys[1], (LAYERS, ROWS), jnp.float32) ** level_of(own_keys[1], (LAYERS, ROWS), ((0, 2),), -0.2, 0.2)), 0.4, 2.5),
        "mlp_scale": jnp.clip(jnp.exp(math.log(2.5) - 1.8325814 * jax.random.uniform(own_keys[2], (LAYERS, ROWS), jnp.float32) ** level_of(own_keys[2], (LAYERS, ROWS), ((0, 2),), -0.2, 0.2)), 0.4, 2.5),
        "patterns": jnp.clip(jnp.exp(math.log(0.059814453) - 2.9957323 * jax.random.uniform(own_keys[3], (LAYERS, HEADS, PROMPTS, SEQ, SEQ), jnp.float32) ** level_of(own_keys[3], (LAYERS, HEADS, PROMPTS, SEQ, SEQ), ((0, 2),), -0.2, 0.2)), 0.0029907227, 0.059814453).astype(jnp.bfloat16),
        "lengths": jax.random.randint(own_keys[4], (PROMPTS,), SEQ // 4, SEQ + 1).astype(jnp.int32),
        "value_proj": normal_values(keys[5], (LAYERS, SLABS, SLAB, KVH * HD), D ** -0.5, 0.09375, ((0, 2), (1, 2), (3, 4))),
        "out_proj": normal_values(keys[6], (LAYERS, KVH, HD, QPK, SLABS, SLAB), (HEADS * HD) ** -0.5, 0.125, ((0, 2), (4, 2), (5, 4))),
        "enc_weight": normal_values(keys[7], (LAYERS, SLABS, SLAB, ACT), D ** -0.5, 0.09375, ((0, 2), (1, 2), (3, 4))),
        "enc_bias": normal_values(keys[8], (LAYERS, ACT), 0.5, 3.0, ((0, 2), (1, 4)), jnp.float32),
        "dec_weight": normal_values(keys[9], (LAYERS, LAYERS, ACT, SLABS, SLAB), ACT ** -0.5, 0.25, ((0, 2), (3, 2), (4, 4))),
        "errors": normal_values(own_keys[10], (LAYERS, ROWS, SLABS, SLAB), 0.5, 4.0, ((0, 2), (2, 2), (3, 4)), jnp.float32),
        "clamp_mode": place_ends(jax.random.randint(keys[11], (LAYERS, FEATURES), 0, 3), jax.random.fold_in(keys[11], 1), 0, 2).astype(jnp.int32),
        "clamp_index": place_ends(jax.random.randint(keys[12], (LAYERS, FEATURES), 0, VALUES), jax.random.fold_in(keys[12], 1), 0, VALUES - 1).astype(jnp.int32),
        "clamp_values": jnp.clip(jax.random.uniform(keys[13], (VALUES,), jnp.float32, 0.25, 3.0), 0.25, 3.0),
        "active_blocks": place_ends(jax.random.randint(keys[14], (LAYERS, RANGES), 0, SHARD_BLOCKS), jax.random.fold_in(keys[14], 1), 0, SHARD_BLOCKS - 1).astype(jnp.int32),
    }


def pick_block(lookup_table, chosen):
    shaped = lookup_table.reshape(RANGES, SHARD_BLOCKS, BLOCK)
    taken = jnp.take_along_axis(shaped, chosen.astype(jnp.int32)[:, None, None], axis=1)
    return taken[:, 0, :].reshape(ACT)


def reference(residual_in, attn_scale, mlp_scale, patterns, lengths, value_proj, out_proj, enc_weight, enc_bias, dec_weight, errors, clamp_mode, clamp_index, clamp_values, active_blocks):
    positions = jnp.arange(SEQ, dtype=jnp.int32)
    live_rows = (positions[None, :] < lengths[:, None]).reshape(ROWS)
    keep_keys = (positions[None, None, :] <= positions[None, :, None]) & (positions[None, None, :] < lengths[:, None, None])
    state = residual_in.reshape(ROWS, D)
    feature_list = []
    state_list = []
    for layer_num in range(LAYERS):
        normed = (state * attn_scale[layer_num][:, None]).astype(jnp.bfloat16)
        values = jnp.dot(normed, value_proj[layer_num].reshape(D, KVH * HD), preferred_element_type=jnp.float32).astype(jnp.bfloat16)
        value_grid = values.reshape(PROMPTS, SEQ, KVH, HD).astype(jnp.float32)
        pattern_grid = jnp.where(keep_keys[None], patterns[layer_num].astype(jnp.float32), 0.0).reshape(KVH, QPK, PROMPTS, SEQ, SEQ)
        head_out = jnp.einsum("gupqk,pkgd->pqgdu", pattern_grid, value_grid).astype(jnp.bfloat16).reshape(ROWS, KVH * HD * QPK)
        attention = jnp.dot(head_out, out_proj[layer_num].reshape(KVH * HD * QPK, D), preferred_element_type=jnp.float32)
        middle = state + attention
        normed_mlp = (middle * mlp_scale[layer_num][:, None]).astype(jnp.bfloat16)
        preact = jnp.dot(normed_mlp, enc_weight[layer_num].reshape(D, ACT), preferred_element_type=jnp.float32) + enc_bias[layer_num]
        active = jnp.maximum(preact, 0.0)
        modes = pick_block(clamp_mode[layer_num], active_blocks[layer_num])
        levels = clamp_values[pick_block(clamp_index[layer_num], active_blocks[layer_num])]
        clamped = jnp.where(modes == 1, levels, jnp.where(modes == 2, active * levels, active))
        features = jnp.where(live_rows[:, None], clamped, 0.0).astype(jnp.bfloat16)
        feature_list.append(features)
        recon = jnp.zeros((ROWS, D), jnp.float32)
        for source_num in range(layer_num + 1):
            recon = recon + jnp.dot(feature_list[source_num], dec_weight[source_num, layer_num].reshape(ACT, D), preferred_element_type=jnp.float32)
        state = middle + recon + errors[layer_num].reshape(ROWS, D)
        state_list.append(state)
    return jnp.stack(state_list).reshape(LAYERS, ROWS, SLABS, SLAB), jnp.stack(feature_list)
```

```python
import jax
import jax.numpy as jnp
from jax import lax
from jax.sharding import PartitionSpec as P

BF16 = jnp.bfloat16
F32 = jnp.float32


def peers(axis):
    count = lax.axis_size(axis)
    return range(1, count)


def partner(index, step, count):
    if count & (count - 1) == 0:
        return index ^ step
    return (step - index) % count


def swap(value, axis, step, first_layer=0):
    count = lax.axis_size(axis)
    if first_layer == 0:
        return lax.ppermute(value, axis, [(s, partner(s, step, count)) for s in range(count)])
    layers = lax.axis_size("layer")
    pairs = [
        (s * layers + n, partner(s, step, count) * layers + n)
        for s in range(count)
        for n in range(first_layer, layers)
    ]
    return lax.ppermute(value, (axis, "layer"), pairs)


def spread(value, axis="feat"):
    return [value] + [swap(value, axis, step) for step in peers(axis)]


def total(blocks):
    result = blocks[0].astype(F32)
    for block in blocks[1:]:
        result = result + block.astype(F32)
    return result


def dot_tn(left, right):
    return lax.dot_general(left, right, (((0,), (0,)), ((), ())), preferred_element_type=F32)


def dot_nt(left, right):
    return lax.dot_general(left, right, (((1,), (1,)), ((), ())), preferred_element_type=F32)


def pick(array, index):
    return lax.dynamic_index_in_dim(array, index, 0, keepdims=False)


def redistribute(weight, ranges, my_range, first_layer):
    blocks = weight.reshape(ranges, -1, weight.shape[1])
    got = [pick(blocks, my_range)]
    for step in peers("feat"):
        other = partner(my_range, step, ranges)
        got.append(swap(pick(blocks, other), "feat", step, first_layer))
    got = jnp.stack(got)
    return [pick(got, partner(my_range, n, ranges)) for n in range(ranges)]


def local(
    residual_in,
    attn_scale,
    mlp_scale,
    patterns,
    lengths,
    value_proj,
    out_proj,
    enc_weight,
    enc_bias,
    dec_weight,
    errors,
    clamp_mode,
    clamp_index,
    clamp_values,
    active_blocks,
):
    layers = lax.axis_size("layer")
    ranges = lax.axis_size("feat")
    my_layer = lax.axis_index("layer")
    my_range = lax.axis_index("feat")
    my_slab = lax.axis_index("tok")
    prompts, seq = patterns.shape[2:4]
    head_dim, per_group = out_proj.shape[2:4]
    kv_cols = value_proj.shape[3]
    half = kv_cols // 2
    width = residual_in.shape[2]
    block_len = enc_bias.shape[1]
    act = block_len * ranges
    rows = residual_in.shape[0]

    source = residual_in[:, 0, :].T
    error_cols = errors[0, :, 0, :].T
    scale_attn = attn_scale[0]
    scale_mlp = mlp_scale[0]

    chosen = active_blocks[0, 0]
    modes = pick(clamp_mode[0].reshape(-1, block_len), chosen)
    entries = pick(clamp_index[0].reshape(-1, block_len), chosen)
    table_ids = jnp.arange(clamp_values.shape[0], dtype=jnp.int32)
    levels = jnp.sum(jnp.where(entries[:, None] == table_ids[None, :], clamp_values[None, :], 0.0), axis=1)
    gain = jnp.where(modes == 1, 0.0, jnp.where(modes == 2, levels, 1.0))
    shift = jnp.where(modes == 1, levels, 0.0)
    mine = jnp.stack([enc_bias[0], gain, shift])
    got = jnp.stack(spread(mine))
    clamp_all = jnp.stack([pick(got, partner(my_range, n, ranges)) for n in range(ranges)], axis=1).reshape(3, act)
    clamp_half = lax.dynamic_slice_in_dim(clamp_all, my_slab * (act // 2), act // 2, 1)

    positions = jnp.arange(seq, dtype=jnp.int32)
    keep = (positions[None, None, :] <= positions[None, :, None]) & (positions[None, None, :] < lengths[:, None, None])
    masked = jnp.where(keep[None], patterns[0], jnp.zeros_like(patterns[0]))
    zero = jnp.zeros_like(masked[:, 0])
    mixing = jnp.concatenate(
        [
            jnp.concatenate([masked[:, p] if q == p else zero for q in range(prompts)], axis=2)
            for p in range(prompts)
        ],
        axis=1,
    ).reshape(-1, per_group * rows, rows)
    live = (positions[None, :] < lengths[:, None]).reshape(rows)

    value_rows = value_proj[0, 0]
    own_value, other_value = (
        lax.dynamic_slice_in_dim(value_rows, n * half, half, 1) for n in (my_slab, 1 - my_slab)
    )
    shares = kv_cols * ranges // head_dim
    out_cols = out_proj[0, :, :, :, 0, :].reshape(shares, head_dim // kv_cols if kv_cols < head_dim else 1, 2, half, per_group, width)
    out_cols = out_cols.reshape(ranges, 2, half, per_group, width).transpose(1, 0, 4, 3, 2).reshape(2, ranges, width, per_group * half)
    out_own, out_other = (pick(out_cols, n) for n in (my_slab, 1 - my_slab))
    group_of = [n * kv_cols // head_dim for n in range(ranges)]

    enc_blocks = jnp.concatenate(redistribute(enc_weight[0, 0], ranges, my_range, 0), axis=1)
    enc_own, enc_other = (
        lax.dynamic_slice_in_dim(enc_blocks, n * (act // 2), act // 2, 1) for n in (my_slab, 1 - my_slab)
    )
    value_blocks = redistribute(value_rows, ranges, my_range, 1)
    spread_own, spread_other = (
        jnp.concatenate([lax.dynamic_slice_in_dim(b, n * half, half, 1) for b in value_blocks], axis=1)
        for n in (my_slab, 1 - my_slab)
    )
    dec_cols = dec_weight[0, :, :, 0, :].transpose(0, 2, 1)

    def over_slabs(own, other):
        return own + swap(other, "tok", 1).astype(F32)

    def heads(values, group):
        mixed = jnp.dot(mixing[group] if isinstance(group, int) else pick(mixing, group), values, preferred_element_type=F32)
        return mixed.astype(BF16).reshape(per_group, rows, -1).transpose(1, 0, 2).reshape(rows, -1)

    def first_attention(state):
        normed = (state * scale_attn[None, :]).astype(BF16)
        blocks = spread(normed)
        own_rows, other_rows = (w.reshape(ranges, width, half) for w in (own_value, other_value))
        order = [partner(my_range, n, ranges) if n else my_range for n in range(ranges)]
        other = sum(dot_tn(b, pick(other_rows, n)) for b, n in zip(blocks, order))
        own = sum(dot_tn(b, pick(own_rows, n)) for b, n in zip(blocks, order))
        values = over_slabs(own, other).astype(BF16)
        mine = heads(values, my_range * kv_cols // head_dim)
        got = spread(mine)
        also = [swap(b, "tok", 1) for b in got]
        return sum(
            dot_nt(pick(out_own, n), b) + dot_nt(pick(out_other, n), c) for n, b, c in zip(order, got, also)
        )

    def later_attention(state_low):
        other = dot_tn(state_low, spread_other).astype(BF16)
        own = dot_tn(state_low, spread_own)
        part = over_slabs(own, other).astype(BF16)
        mine = (total(spread(part)) * scale_attn[:, None]).astype(BF16)
        also = swap(mine, "tok", 1)
        result = 0.0
        for n in range(ranges):
            cols = slice(n * half, (n + 1) * half)
            result = (
                result
                + dot_nt(out_own[n], heads(mine[:, cols], group_of[n]))
                + dot_nt(out_other[n], heads(also[:, cols], group_of[n]))
            )
        return result

    def code(middle):
        normed = (middle * scale_mlp[None, :]).astype(BF16)
        other = dot_tn(normed, enc_other).astype(BF16)
        own = dot_tn(normed, enc_own)
        part = over_slabs(own, other).astype(BF16)
        preact = total(spread(part)) + clamp_half[0][None, :]
        clamped = jnp.maximum(preact, 0.0) * clamp_half[1][None, :] + clamp_half[2][None, :]
        mine = jnp.where(live[:, None], clamped, 0.0).astype(BF16)
        also = swap(mine, "tok", 1)
        return jnp.concatenate(
            [jnp.where(my_slab == 0, mine, also), jnp.where(my_slab == 0, also, mine)], axis=1
        )

    def handed_on(value, layer):
        return lax.ppermute(value, "layer", [(layer, layer + 1)])

    states = jnp.zeros_like(source)
    feats = jnp.zeros((rows, block_len), BF16)
    state, links = source, None
    for layer in range(layers):
        if layer == 0:
            middle = state + first_attention(state)
        else:
            middle = low.astype(F32) + later_attention(low) + rest.astype(F32)
        kept = code(middle)
        recon = dot_nt(dec_cols[layer], kept)
        base = middle + error_cols
        if layer > 0:
            base = base + links[0]
        state = base + recon
        states = jnp.where(my_layer == layer, state, states)
        feats = jnp.where(
            my_layer == layer, lax.dynamic_slice_in_dim(kept, my_range * block_len, block_len, 1), feats
        )
        if layer + 1 < layers:
            low = state.astype(BF16)
            left = (state - low.astype(F32)).astype(BF16)
            low = handed_on(low, layer)
            writes = jnp.stack([dot_nt(dec_cols[n], kept) for n in range(layer + 1, layers)])
            if layer > 0:
                writes = writes + links[1:]
            rest = handed_on(left, layer)
            links = handed_on(writes, layer)
    return states.T[None, :, None, :], feats[None]


def solution(mesh):
    return jax.shard_map(
        local,
        mesh=mesh,
        in_specs=(
            P("groups", "tok", "feat"),
            P("layer", "groups"),
            P("layer", "groups"),
            P("layer", None, "groups", None, None),
            P("groups"),
            P("layer", "tok", None, "feat"),
            P("layer", None, None, None, "tok", "feat"),
            P("layer", "tok", None, "feat"),
            P("layer", "feat"),
            P("layer", None, None, "tok", "feat"),
            P("layer", "groups", "tok", "feat"),
            P("layer", "feat"),
            P("layer", "feat"),
            P(),
            P("layer", "feat"),
        ),
        out_specs=(P("layer", "groups", "tok", "feat"), P("layer", "groups", "feat")),
        check_vma=False,
    )
```

```python
import functools

import jax
import jax.numpy as jnp
from jax import lax
from jax.experimental import pallas as pl
from jax.experimental.pallas import tpu as pltpu
from jax.sharding import PartitionSpec as P

BF16 = jnp.bfloat16
F32 = jnp.float32


def peers(axis):
    count = lax.axis_size(axis)
    return range(1, count)


def partner(index, step, count):
    if count & (count - 1) == 0:
        return index ^ step
    return (step - index) % count


def swap(value, axis, step, first_layer=0):
    count = lax.axis_size(axis)
    if first_layer == 0:
        return lax.ppermute(value, axis, [(s, partner(s, step, count)) for s in range(count)])
    layers = lax.axis_size("layer")
    pairs = [
        (s * layers + n, partner(s, step, count) * layers + n)
        for s in range(count)
        for n in range(first_layer, layers)
    ]
    return lax.ppermute(value, (axis, "layer"), pairs)


def spread(value, axis="feat"):
    return [value] + [swap(value, axis, step) for step in peers(axis)]


def total(blocks):
    result = blocks[0].astype(F32)
    for block in blocks[1:]:
        result = result + block.astype(F32)
    return result


def dot_tn(left, right):
    return lax.dot_general(left, right, (((0,), (0,)), ((), ())), preferred_element_type=F32)


def dot_nt(left, right):
    return lax.dot_general(left, right, (((1,), (1,)), ((), ())), preferred_element_type=F32)


def pick(array, index):
    return lax.dynamic_index_in_dim(array, index, 0, keepdims=False)


def redistribute(weight, ranges, my_range, first_layer):
    blocks = weight.reshape(ranges, -1, weight.shape[1])
    got = [pick(blocks, my_range)]
    for step in peers("feat"):
        other = partner(my_range, step, ranges)
        got.append(swap(pick(blocks, other), "feat", step, first_layer))
    got = jnp.stack(got)
    return [pick(got, partner(my_range, n, ranges)) for n in range(ranges)]


def plain(
    residual_in,
    attn_scale,
    mlp_scale,
    patterns,
    lengths,
    value_proj,
    out_proj,
    enc_weight,
    enc_bias,
    dec_weight,
    errors,
    clamp_mode,
    clamp_index,
    clamp_values,
    active_blocks,
):
    layers = lax.axis_size("layer")
    ranges = lax.axis_size("feat")
    my_layer = lax.axis_index("layer")
    my_range = lax.axis_index("feat")
    my_slab = lax.axis_index("tok")
    prompts, seq = patterns.shape[2:4]
    head_dim, per_group = out_proj.shape[2:4]
    kv_cols = value_proj.shape[3]
    half = kv_cols // 2
    width = residual_in.shape[2]
    block_len = enc_bias.shape[1]
    act = block_len * ranges
    rows = residual_in.shape[0]

    source = residual_in[:, 0, :].T
    error_cols = errors[0, :, 0, :].T
    scale_attn = attn_scale[0]
    scale_mlp = mlp_scale[0]

    chosen = active_blocks[0, 0]
    modes = pick(clamp_mode[0].reshape(-1, block_len), chosen)
    entries = pick(clamp_index[0].reshape(-1, block_len), chosen)
    table_ids = jnp.arange(clamp_values.shape[0], dtype=jnp.int32)
    levels = jnp.sum(jnp.where(entries[:, None] == table_ids[None, :], clamp_values[None, :], 0.0), axis=1)
    gain = jnp.where(modes == 1, 0.0, jnp.where(modes == 2, levels, 1.0))
    shift = jnp.where(modes == 1, levels, 0.0)
    mine = jnp.stack([enc_bias[0], gain, shift])
    got = jnp.stack(spread(mine))
    clamp_all = jnp.stack([pick(got, partner(my_range, n, ranges)) for n in range(ranges)], axis=1).reshape(3, act)
    clamp_half = lax.dynamic_slice_in_dim(clamp_all, my_slab * (act // 2), act // 2, 1)

    positions = jnp.arange(seq, dtype=jnp.int32)
    keep = (positions[None, None, :] <= positions[None, :, None]) & (positions[None, None, :] < lengths[:, None, None])
    masked = jnp.where(keep[None], patterns[0], jnp.zeros_like(patterns[0]))
    zero = jnp.zeros_like(masked[:, 0])
    mixing = jnp.concatenate(
        [
            jnp.concatenate([masked[:, p] if q == p else zero for q in range(prompts)], axis=2)
            for p in range(prompts)
        ],
        axis=1,
    ).reshape(-1, per_group * rows, rows)
    live = (positions[None, :] < lengths[:, None]).reshape(rows)

    value_rows = value_proj[0, 0]
    own_value, other_value = (
        lax.dynamic_slice_in_dim(value_rows, n * half, half, 1) for n in (my_slab, 1 - my_slab)
    )
    out_cols = out_proj[0, :, :, :, 0, :].reshape(ranges, 2, half, per_group, width).transpose(1, 0, 4, 3, 2).reshape(2, ranges, width, per_group * half)
    out_own, out_other = (pick(out_cols, n) for n in (my_slab, 1 - my_slab))
    group_of = [n * kv_cols // head_dim for n in range(ranges)]

    enc_blocks = jnp.concatenate(redistribute(enc_weight[0, 0], ranges, my_range, 0), axis=1)
    enc_own, enc_other = (
        lax.dynamic_slice_in_dim(enc_blocks, n * (act // 2), act // 2, 1) for n in (my_slab, 1 - my_slab)
    )
    value_blocks = redistribute(value_rows, ranges, my_range, 1)
    spread_own, spread_other = (
        jnp.concatenate([lax.dynamic_slice_in_dim(b, n * half, half, 1) for b in value_blocks], axis=1)
        for n in (my_slab, 1 - my_slab)
    )
    dec_cols = dec_weight[0, :, :, 0, :].transpose(0, 2, 1)

    def over_slabs(own, other):
        return own + swap(other, "tok", 1).astype(F32)

    def heads(values, group):
        mixed = jnp.dot(mixing[group] if isinstance(group, int) else pick(mixing, group), values, preferred_element_type=F32)
        return mixed.astype(BF16).reshape(per_group, rows, -1).transpose(1, 0, 2).reshape(rows, -1)

    def first_attention(state):
        normed = (state * scale_attn[None, :]).astype(BF16)
        blocks = spread(normed)
        own_rows, other_rows = (w.reshape(ranges, width, half) for w in (own_value, other_value))
        order = [partner(my_range, n, ranges) if n else my_range for n in range(ranges)]
        other = sum(dot_tn(b, pick(other_rows, n)) for b, n in zip(blocks, order))
        own = sum(dot_tn(b, pick(own_rows, n)) for b, n in zip(blocks, order))
        values = over_slabs(own, other).astype(BF16)
        mine = heads(values, my_range * kv_cols // head_dim)
        got = spread(mine)
        also = [swap(b, "tok", 1) for b in got]
        return sum(
            dot_nt(pick(out_own, n), b) + dot_nt(pick(out_other, n), c) for n, b, c in zip(order, got, also)
        )

    def later_attention(state_low):
        other = dot_tn(state_low, spread_other).astype(BF16)
        own = dot_tn(state_low, spread_own)
        part = over_slabs(own, other).astype(BF16)
        mine = (total(spread(part)) * scale_attn[:, None]).astype(BF16)
        also = swap(mine, "tok", 1)
        result = 0.0
        for n in range(ranges):
            cols = slice(n * half, (n + 1) * half)
            result = (
                result
                + dot_nt(out_own[n], heads(mine[:, cols], group_of[n]))
                + dot_nt(out_other[n], heads(also[:, cols], group_of[n]))
            )
        return result

    def code(middle):
        normed = (middle * scale_mlp[None, :]).astype(BF16)
        other = dot_tn(normed, enc_other).astype(BF16)
        own = dot_tn(normed, enc_own)
        part = over_slabs(own, other).astype(BF16)
        preact = total(spread(part)) + clamp_half[0][None, :]
        clamped = jnp.maximum(preact, 0.0) * clamp_half[1][None, :] + clamp_half[2][None, :]
        mine = jnp.where(live[:, None], clamped, 0.0).astype(BF16)
        also = swap(mine, "tok", 1)
        return jnp.concatenate(
            [jnp.where(my_slab == 0, mine, also), jnp.where(my_slab == 0, also, mine)], axis=1
        )

    def handed_on(value, layer):
        return lax.ppermute(value, "layer", [(layer, layer + 1)])

    states = jnp.zeros_like(source)
    feats = jnp.zeros((rows, block_len), BF16)
    state, links = source, None
    for layer in range(layers):
        if layer == 0:
            middle = state + first_attention(state)
        else:
            middle = low.astype(F32) + later_attention(low) + rest.astype(F32)
        kept = code(middle)
        recon = dot_nt(dec_cols[layer], kept)
        base = middle + error_cols
        if layer > 0:
            base = base + links[0]
        state = base + recon
        states = jnp.where(my_layer == layer, state, states)
        feats = jnp.where(
            my_layer == layer, lax.dynamic_slice_in_dim(kept, my_range * block_len, block_len, 1), feats
        )
        if layer + 1 < layers:
            low = state.astype(BF16)
            left = (state - low.astype(F32)).astype(BF16)
            low = handed_on(low, layer)
            writes = jnp.stack([dot_nt(dec_cols[n], kept) for n in range(layer + 1, layers)])
            if layer > 0:
                writes = writes + links[1:]
            rest = handed_on(left, layer)
            links = handed_on(writes, layer)
    return states.T[None, :, None, :], feats[None]


LANES = 128
INFO = 16


def shape(*sizes, dtype=F32):
    return jax.ShapeDtypeStruct(sizes, dtype)


def kernel_call(body, outs, scalars, arrays, scratch=(), flops=0):
    many = isinstance(outs, (list, tuple))
    kept = list(outs) if many else [outs]
    size = sum(a.size * a.dtype.itemsize for a in arrays) + sum(a.size * a.dtype.itemsize for a in kept)
    return pl.pallas_call(
        body,
        out_shape=tuple(kept) if many else outs,
        in_specs=[pl.BlockSpec(memory_space=pltpu.SMEM)] * len(scalars) + [pl.BlockSpec(memory_space=pltpu.VMEM)] * len(arrays),
        out_specs=tuple(pl.BlockSpec(memory_space=pltpu.VMEM) for _ in kept) if many else pl.BlockSpec(memory_space=pltpu.VMEM),
        scratch_shapes=list(scratch),
        compiler_params=pltpu.CompilerParams(vmem_limit_bytes=16 * 1024 * 1024),
        cost_estimate=pl.CostEstimate(flops=int(flops), bytes_accessed=int(size), transcendentals=0),
    )(*scalars, *arrays)


def split_terms(value):
    high = value.astype(BF16)
    left = value - high.astype(F32)
    middle = left.astype(BF16)
    low = (left - middle.astype(F32)).astype(BF16)
    return [high, middle, low]


def pack_body(ranges, place, chosen, table, mode, index, bias, enc, *sends):
    width = enc.shape[0] // ranges
    block = chosen[0, 0]
    modes = mode[pl.ds(block, 1), :]
    entries = index[pl.ds(block, 1), :]
    levels = jnp.zeros(entries.shape, F32)
    for n in range(table.shape[0]):
        levels = jnp.where(entries == n, table[n], levels)
    gain = jnp.where(modes == 1, 0.0, jnp.where(modes == 2, levels, 1.0))
    shift = jnp.where(modes == 1, levels, 0.0)
    terms = [t.astype(F32) for v in (bias[...], gain, shift) for t in split_terms(v)]
    info = jnp.concatenate(terms + [jnp.zeros((INFO - len(terms), bias.shape[1]), F32)], axis=0).astype(BF16)
    for step, send in enumerate(sends):
        other = partner(place[0], step, ranges) if step else place[0]
        send[0:width, :] = enc[pl.ds(pl.multiple_of(other * width, 16), width), :]
        send[width:, :] = info


def values_body(ranges, place, *refs):
    blocks, (weight, own, other) = refs[:ranges], refs[ranges:]
    width, half = blocks[0].shape[0], own.shape[1]
    acc = None
    for step, block in enumerate(blocks):
        n = partner(place[0], step, ranges) if step else place[0]
        part = dot_tn(block[...], weight[pl.ds(pl.multiple_of(n * width, 16), width), :])
        acc = part if acc is None else acc + part
    first = place[1] == 0
    own[...] = jnp.where(first, acc[:, :half], acc[:, half:])
    other[...] = jnp.where(first, acc[:, half:], acc[:, :half])


def heads_body(kv_cols, head_dim, place, lengths, own, got, scale, patterns, out):
    per_group, seq, prompts = out.shape[0], patterns.shape[2], patterns.shape[1]
    values = ((own[...] + got[...]) * scale[...]).astype(BF16)
    first = (place[0] * kv_cols // head_dim) * per_group
    query = lax.broadcasted_iota(jnp.int32, (seq, seq), 0)
    key = lax.broadcasted_iota(jnp.int32, (seq, seq), 1)
    for p in range(prompts):
        keep = (key <= query) & (key < lengths[p])
        for u in range(per_group):
            pattern = jnp.where(keep, patterns[first + u, p].astype(F32), 0.0).astype(BF16)
            mixed = jnp.dot(pattern, values[p * seq : (p + 1) * seq, :], preferred_element_type=F32)
            out[u, p * seq : (p + 1) * seq, :] = mixed.astype(BF16)


def code_body(ranges, states, kv_cols, head_dim, place, *refs):
    refs = list(refs)
    got, also, state, packed = (
        [refs.pop(0) for _ in range(count)] for count in (ranges, ranges, states, ranges)
    )
    weight, scale, middle, own, other, info, parts = refs
    width = middle.shape[0]
    per_group = got[0].shape[0]
    first = place[1] == 0
    acc = state[0][...].astype(F32)
    for piece in state[1:]:
        acc = acc + piece[...].astype(F32)
    for step in range(ranges):
        n = partner(place[0], step, ranges) if step else place[0]
        group = n * kv_cols // head_dim
        for u in range(per_group):
            mine, theirs = got[step][u], also[step][u]
            head = jnp.concatenate([jnp.where(first, mine, theirs), jnp.where(first, theirs, mine)], axis=1)
            acc = acc + dot_nt(weight[group * per_group + u], head)
    middle[...] = acc
    normed = (acc * scale[...]).astype(BF16)
    for step in range(ranges):
        n = partner(place[0], step, ranges) if step else place[0]
        parts[n] = dot_tn(normed, packed[step][0:width, :])
        terms = packed[step][width:, :].astype(F32)
        info[n] = jnp.concatenate(
            [terms[3 * i : 3 * i + 1] + terms[3 * i + 1 : 3 * i + 2] + terms[3 * i + 2 : 3 * i + 3] for i in range(3)]
            + [jnp.zeros((5, terms.shape[1]), F32)],
            axis=0,
        )
    share = ranges // 2
    own[...] = parts[pl.ds(place[1] * share, share)]
    other[...] = parts[pl.ds((1 - place[1]) * share, share)].astype(BF16)


def clamp_body(seq, place, lengths, *refs):
    *blocks, info, out = refs
    share, rows, _ = out.shape
    row = lax.broadcasted_iota(jnp.int32, out.shape[1:], 0)
    end = jnp.full(row.shape, lengths[0], jnp.int32)
    for p in range(1, rows // seq):
        end = jnp.where(row >= p * seq, p * seq + lengths[p], end)
    live = row < end
    for n in range(share):
        facts = info[place[1] * share + n]
        preact = total([b[n] for b in blocks]) + facts[0:1]
        clamped = jnp.maximum(preact, 0.0) * facts[1:2] + facts[2:3]
        out[n] = jnp.where(live, clamped, 0.0).astype(BF16)


def ordered(place, mine, also):
    first = place[1] == 0
    share = mine.shape[0]
    return [jnp.where(first, mine[n], also[n]) for n in range(share)] + [
        jnp.where(first, also[n], mine[n]) for n in range(share)
    ]


def decode_body(layer, adds, sends, keeps, place, *refs):
    refs = list(refs)
    mine, also, dec = refs[:3]
    added = refs[3 : 3 + adds]
    refs = refs[3 + adds :]
    before = refs[:2] if keeps else None
    if keeps:
        refs = refs[2:]
    state_out, feats_out = refs[:2]
    feats = ordered(place, mine, also)
    acc = added[0][...]
    for piece in added[1:]:
        acc = acc + piece[...]
    acc = acc + dot_nt(dec[layer], jnp.concatenate(feats, axis=1))
    block = feats[0]
    for n in range(1, len(feats)):
        block = jnp.where(place[0] == n, feats[n], block)
    if sends:
        low = acc.astype(BF16)
        refs[2][...] = low
        refs[3][...] = (acc - low.astype(F32)).astype(BF16)
    if keeps:
        here = place[2] == layer
        state_out[...] = jnp.where(here, acc, before[0][...])
        feats_out[...] = jnp.where(here, block, before[1][...])
    else:
        state_out[...] = acc
        feats_out[...] = block


def writes_body(layer, has_links, place, mine, also, dec, *refs):
    out = refs[-1]
    feats = jnp.concatenate(ordered(place, mine, also), axis=1)
    for n in range(out.shape[0]):
        made = dot_nt(dec[layer + 1 + n], feats)
        out[n] = made + refs[0][n + 1] if has_links else made


def after(value, *others):
    return lax.optimization_barrier((value, *others))[0]


def tiled(
    residual_in,
    attn_scale,
    mlp_scale,
    patterns,
    lengths,
    value_proj,
    out_proj,
    enc_weight,
    enc_bias,
    dec_weight,
    errors,
    clamp_mode,
    clamp_index,
    clamp_values,
    active_blocks,
):
    layers = lax.axis_size("layer")
    ranges = lax.axis_size("feat")
    seq = patterns.shape[3]
    head_dim, per_group = out_proj.shape[2:4]
    kv_cols = value_proj.shape[3]
    half = kv_cols // 2
    width = residual_in.shape[2]
    block_len = enc_bias.shape[1]
    rows = residual_in.shape[0]
    share = ranges // 2
    place = jnp.stack([lax.axis_index("feat"), lax.axis_index("tok"), lax.axis_index("layer")]).astype(jnp.int32)

    source = residual_in[:, 0, :].T
    error_cols = errors[0, :, 0, :].T
    out_weight = out_proj[0, :, :, :, 0, :].transpose(0, 2, 3, 1).reshape(-1, width, head_dim)
    dec_cols = dec_weight[0, :, :, 0, :].transpose(0, 2, 1)
    value_rows = value_proj[0, 0]
    scale_attn = attn_scale.reshape(rows, 1)

    def handed_on(value, layer):
        return lax.ppermute(value, "layer", [(layer, layer + 1)])

    packed = None
    low, links, kept = source.astype(BF16), None, None
    state = [source]
    for layer in range(layers):
        blocks = spread(low)
        if packed is None:
            sends = kernel_call(
                functools.partial(pack_body, ranges),
                [shape(width + INFO, block_len, dtype=BF16)] * ranges,
                [place, active_blocks, clamp_values],
                [clamp_mode.reshape(-1, block_len), clamp_index.reshape(-1, block_len), enc_bias, enc_weight[0, 0]],
            )
            packed = [sends[0]] + [
                swap(after(sends[step], *blocks), "feat", step) for step in peers("feat")
            ]
        own, other = kernel_call(
            functools.partial(values_body, ranges),
            [shape(rows, half)] * 2,
            [place],
            [*blocks, value_rows],
            flops=4 * rows * value_rows.size,
        )
        mine = kernel_call(
            functools.partial(heads_body, kv_cols, head_dim),
            shape(per_group, rows, half, dtype=BF16),
            [place, lengths],
            [own, swap(other, "tok", 1), scale_attn, patterns[0]],
        )
        got = spread(mine)
        also = [swap(b, "tok", 1) for b in got]
        middle, own, other, info = kernel_call(
            functools.partial(code_body, ranges, len(state), kv_cols, head_dim),
            [
                shape(width, rows),
                shape(share, rows, block_len),
                shape(share, rows, block_len, dtype=BF16),
                shape(ranges, 8, block_len),
            ],
            [place],
            [*got, *also, *state, *packed, out_weight, mlp_scale],
            scratch=[pltpu.VMEM((ranges, rows, block_len), F32)],
            flops=2 * rows * (out_weight.size + width * block_len * ranges),
        )
        part = (own + swap(other, "tok", 1).astype(F32)).astype(BF16)
        mine = kernel_call(
            functools.partial(clamp_body, seq),
            shape(share, rows, block_len, dtype=BF16),
            [place, lengths],
            [*spread(part), info],
        )
        also = swap(mine, "tok", 1)
        more = layer + 1 < layers
        added = [middle, error_cols] + ([links[0]] if links is not None else [])
        outs = [shape(width, rows), shape(rows, block_len, dtype=BF16)]
        if more:
            outs += [shape(width, rows, dtype=BF16)] * 2
        made = kernel_call(
            functools.partial(decode_body, layer, len(added), more, kept is not None),
            outs,
            [place],
            [mine, also, dec_cols, *added, *(kept or ())],
            flops=2 * rows * dec_cols.size // layers,
        )
        kept = made[:2]
        if more:
            low = handed_on(made[2], layer)
            rest = handed_on(after(made[3], low), layer)
            writes = kernel_call(
                functools.partial(writes_body, layer, links is not None),
                shape(layers - 1 - layer, width, rows),
                [place],
                [mine, also, dec_cols, *([links] if links is not None else [])],
                flops=2 * rows * dec_cols.size,
            )
            links = handed_on(after(writes, rest), layer)
            state = [low, rest]
    return kept[0].T[None, :, None, :], kept[1][None]


def local(residual_in, attn_scale, mlp_scale, patterns, lengths, value_proj, out_proj, enc_weight, enc_bias, *others):
    whole = (
        residual_in.shape[0] % LANES == 0
        and residual_in.shape[2] % 16 == 0
        and value_proj.shape[3] == out_proj.shape[2]
        and value_proj.shape[3] % (2 * LANES) == 0
        and enc_bias.shape[1] % LANES == 0
        and lax.axis_size("feat") % 2 == 0
        and lax.axis_size("tok") == 2
    )
    run = tiled if whole else plain
    return run(
        residual_in, attn_scale, mlp_scale, patterns, lengths, value_proj, out_proj, enc_weight, enc_bias, *others
    )


def solution(mesh):
    return jax.shard_map(
        local,
        mesh=mesh,
        in_specs=(
            P("groups", "tok", "feat"),
            P("layer", "groups"),
            P("layer", "groups"),
            P("layer", None, "groups", None, None),
            P("groups"),
            P("layer", "tok", None, "feat"),
            P("layer", None, None, None, "tok", "feat"),
            P("layer", "tok", None, "feat"),
            P("layer", "feat"),
            P("layer", None, None, "tok", "feat"),
            P("layer", "groups", "tok", "feat"),
            P("layer", "feat"),
            P("layer", "feat"),
            P(),
            P("layer", "feat"),
        ),
        out_specs=(P("layer", "groups", "tok", "feat"), P("layer", "groups", "feat")),
        check_vma=False,
    )
```

```python
import functools

import jax
import jax.numpy as jnp
from jax import lax
from jax.experimental import pallas as pl
from jax.experimental.pallas import tpu as pltpu
from jax.sharding import PartitionSpec as P

BF16 = jnp.bfloat16
F32 = jnp.float32


def peers(axis):
    count = lax.axis_size(axis)
    return range(1, count)


def partner(index, step, count):
    if count & (count - 1) == 0:
        return index ^ step
    return (step - index) % count


def swap(value, axis, step, first_layer=0):
    count = lax.axis_size(axis)
    if first_layer == 0:
        return lax.ppermute(value, axis, [(s, partner(s, step, count)) for s in range(count)])
    layers = lax.axis_size("layer")
    pairs = [
        (s * layers + n, partner(s, step, count) * layers + n)
        for s in range(count)
        for n in range(first_layer, layers)
    ]
    return lax.ppermute(value, (axis, "layer"), pairs)


def spread(value, axis="feat"):
    return [value] + [swap(value, axis, step) for step in peers(axis)]


def exchange(sends):
    return [sends[0]] + [swap(sends[step], "feat", step) for step in peers("feat")]


def total(blocks):
    result = blocks[0].astype(F32)
    for block in blocks[1:]:
        result = result + block.astype(F32)
    return result


def dot_tn(left, right):
    return lax.dot_general(left, right, (((0,), (0,)), ((), ())), preferred_element_type=F32)


def dot_nt(left, right):
    return lax.dot_general(left, right, (((1,), (1,)), ((), ())), preferred_element_type=F32)


def pick(array, index):
    return lax.dynamic_index_in_dim(array, index, 0, keepdims=False)


def redistribute(weight, ranges, my_range, first_layer):
    blocks = weight.reshape(ranges, -1, weight.shape[1])
    got = [pick(blocks, my_range)]
    for step in peers("feat"):
        other = partner(my_range, step, ranges)
        got.append(swap(pick(blocks, other), "feat", step, first_layer))
    got = jnp.stack(got)
    return [pick(got, partner(my_range, n, ranges)) for n in range(ranges)]


def plain(
    residual_in,
    attn_scale,
    mlp_scale,
    patterns,
    lengths,
    value_proj,
    out_proj,
    enc_weight,
    enc_bias,
    dec_weight,
    errors,
    clamp_mode,
    clamp_index,
    clamp_values,
    active_blocks,
):
    layers = lax.axis_size("layer")
    ranges = lax.axis_size("feat")
    my_layer = lax.axis_index("layer")
    my_range = lax.axis_index("feat")
    my_slab = lax.axis_index("tok")
    prompts, seq = patterns.shape[2:4]
    head_dim, per_group = out_proj.shape[2:4]
    kv_cols = value_proj.shape[3]
    half = kv_cols // 2
    width = residual_in.shape[2]
    block_len = enc_bias.shape[1]
    act = block_len * ranges
    rows = residual_in.shape[0]

    source = residual_in[:, 0, :].T
    error_cols = errors[0, :, 0, :].T
    scale_attn = attn_scale[0]
    scale_mlp = mlp_scale[0]

    chosen = active_blocks[0, 0]
    modes = pick(clamp_mode[0].reshape(-1, block_len), chosen)
    entries = pick(clamp_index[0].reshape(-1, block_len), chosen)
    table_ids = jnp.arange(clamp_values.shape[0], dtype=jnp.int32)
    levels = jnp.sum(jnp.where(entries[:, None] == table_ids[None, :], clamp_values[None, :], 0.0), axis=1)
    gain = jnp.where(modes == 1, 0.0, jnp.where(modes == 2, levels, 1.0))
    shift = jnp.where(modes == 1, levels, 0.0)
    mine = jnp.stack([enc_bias[0], gain, shift])
    got = jnp.stack(spread(mine))
    clamp_all = jnp.stack([pick(got, partner(my_range, n, ranges)) for n in range(ranges)], axis=1).reshape(3, act)
    clamp_half = lax.dynamic_slice_in_dim(clamp_all, my_slab * (act // 2), act // 2, 1)

    positions = jnp.arange(seq, dtype=jnp.int32)
    keep = (positions[None, None, :] <= positions[None, :, None]) & (positions[None, None, :] < lengths[:, None, None])
    masked = jnp.where(keep[None], patterns[0], jnp.zeros_like(patterns[0]))
    zero = jnp.zeros_like(masked[:, 0])
    mixing = jnp.concatenate(
        [
            jnp.concatenate([masked[:, p] if q == p else zero for q in range(prompts)], axis=2)
            for p in range(prompts)
        ],
        axis=1,
    ).reshape(-1, per_group * rows, rows)
    live = (positions[None, :] < lengths[:, None]).reshape(rows)

    value_rows = value_proj[0, 0]
    own_value, other_value = (
        lax.dynamic_slice_in_dim(value_rows, n * half, half, 1) for n in (my_slab, 1 - my_slab)
    )
    out_cols = out_proj[0, :, :, :, 0, :].reshape(ranges, 2, half, per_group, width).transpose(1, 0, 4, 3, 2).reshape(2, ranges, width, per_group * half)
    out_own, out_other = (pick(out_cols, n) for n in (my_slab, 1 - my_slab))
    group_of = [n * kv_cols // head_dim for n in range(ranges)]

    enc_blocks = jnp.concatenate(redistribute(enc_weight[0, 0], ranges, my_range, 0), axis=1)
    enc_own, enc_other = (
        lax.dynamic_slice_in_dim(enc_blocks, n * (act // 2), act // 2, 1) for n in (my_slab, 1 - my_slab)
    )
    value_blocks = redistribute(value_rows, ranges, my_range, 1)
    spread_own, spread_other = (
        jnp.concatenate([lax.dynamic_slice_in_dim(b, n * half, half, 1) for b in value_blocks], axis=1)
        for n in (my_slab, 1 - my_slab)
    )
    dec_cols = dec_weight[0, :, :, 0, :].transpose(0, 2, 1)

    def over_slabs(own, other):
        return own + swap(other, "tok", 1).astype(F32)

    def heads(values, group):
        mixed = jnp.dot(mixing[group] if isinstance(group, int) else pick(mixing, group), values, preferred_element_type=F32)
        return mixed.astype(BF16).reshape(per_group, rows, -1).transpose(1, 0, 2).reshape(rows, -1)

    def first_attention(state):
        normed = (state * scale_attn[None, :]).astype(BF16)
        blocks = spread(normed)
        own_rows, other_rows = (w.reshape(ranges, width, half) for w in (own_value, other_value))
        order = [partner(my_range, n, ranges) if n else my_range for n in range(ranges)]
        other = sum(dot_tn(b, pick(other_rows, n)) for b, n in zip(blocks, order))
        own = sum(dot_tn(b, pick(own_rows, n)) for b, n in zip(blocks, order))
        values = over_slabs(own, other).astype(BF16)
        mine = heads(values, my_range * kv_cols // head_dim)
        got = spread(mine)
        also = [swap(b, "tok", 1) for b in got]
        return sum(
            dot_nt(pick(out_own, n), b) + dot_nt(pick(out_other, n), c) for n, b, c in zip(order, got, also)
        )

    def later_attention(state_low):
        other = dot_tn(state_low, spread_other).astype(BF16)
        own = dot_tn(state_low, spread_own)
        part = over_slabs(own, other).astype(BF16)
        mine = (total(spread(part)) * scale_attn[:, None]).astype(BF16)
        also = swap(mine, "tok", 1)
        result = 0.0
        for n in range(ranges):
            cols = slice(n * half, (n + 1) * half)
            result = (
                result
                + dot_nt(out_own[n], heads(mine[:, cols], group_of[n]))
                + dot_nt(out_other[n], heads(also[:, cols], group_of[n]))
            )
        return result

    def code(middle):
        normed = (middle * scale_mlp[None, :]).astype(BF16)
        other = dot_tn(normed, enc_other).astype(BF16)
        own = dot_tn(normed, enc_own)
        part = over_slabs(own, other).astype(BF16)
        preact = total(spread(part)) + clamp_half[0][None, :]
        clamped = jnp.maximum(preact, 0.0) * clamp_half[1][None, :] + clamp_half[2][None, :]
        mine = jnp.where(live[:, None], clamped, 0.0).astype(BF16)
        also = swap(mine, "tok", 1)
        return jnp.concatenate(
            [jnp.where(my_slab == 0, mine, also), jnp.where(my_slab == 0, also, mine)], axis=1
        )

    def handed_on(value, layer):
        return lax.ppermute(value, "layer", [(layer, layer + 1)])

    states = jnp.zeros_like(source)
    feats = jnp.zeros((rows, block_len), BF16)
    state, links = source, None
    for layer in range(layers):
        if layer == 0:
            middle = state + first_attention(state)
        else:
            middle = low.astype(F32) + later_attention(low) + rest.astype(F32)
        kept = code(middle)
        recon = dot_nt(dec_cols[layer], kept)
        base = middle + error_cols
        if layer > 0:
            base = base + links[0]
        state = base + recon
        states = jnp.where(my_layer == layer, state, states)
        feats = jnp.where(
            my_layer == layer, lax.dynamic_slice_in_dim(kept, my_range * block_len, block_len, 1), feats
        )
        if layer + 1 < layers:
            low = state.astype(BF16)
            left = (state - low.astype(F32)).astype(BF16)
            low = handed_on(low, layer)
            writes = jnp.stack([dot_nt(dec_cols[n], kept) for n in range(layer + 1, layers)])
            if layer > 0:
                writes = writes + links[1:]
            rest = handed_on(left, layer)
            links = handed_on(writes, layer)
    return states.T[None, :, None, :], feats[None]


LANES = 128
INFO = 16


def shape(*sizes, dtype=F32):
    return jax.ShapeDtypeStruct(sizes, dtype)


def kernel_call(body, outs, scalars, arrays, left=(), scratch=(), flops=0):
    many = isinstance(outs, (list, tuple))
    kept = list(outs) if many else [outs]
    size = sum(a.size * a.dtype.itemsize for a in arrays) + sum(a.size * a.dtype.itemsize for a in kept)
    return pl.pallas_call(
        body,
        out_shape=tuple(kept) if many else outs,
        in_specs=[pl.BlockSpec(memory_space=pltpu.SMEM)] * len(scalars) + [pl.BlockSpec(memory_space=pltpu.VMEM)] * len(arrays) + [pl.BlockSpec(memory_space=pltpu.HBM)] * len(left),
        out_specs=tuple(pl.BlockSpec(memory_space=pltpu.VMEM) for _ in kept) if many else pl.BlockSpec(memory_space=pltpu.VMEM),
        scratch_shapes=list(scratch),
        compiler_params=pltpu.CompilerParams(vmem_limit_bytes=16 * 1024 * 1024),
        cost_estimate=pl.CostEstimate(flops=int(flops), bytes_accessed=int(size), transcendentals=0),
    )(*scalars, *arrays, *left)


def split_terms(value):
    high = value.astype(BF16)
    left = value - high.astype(F32)
    middle = left.astype(BF16)
    low = (left - middle.astype(F32)).astype(BF16)
    return [high, middle, low]


def facts_body(place, lengths, chosen, table, mode, index, bias, scale, patterns, info, mixing, scales):
    block = chosen[0, 0]
    modes = mode[pl.ds(block, 1), :]
    entries = index[pl.ds(block, 1), :]
    levels = jnp.zeros(entries.shape, F32)
    for n in range(table.shape[0]):
        levels = jnp.where(entries == n, table[n], levels)
    gain = jnp.where(modes == 1, 0.0, jnp.where(modes == 2, levels, 1.0))
    shift = jnp.where(modes == 1, levels, 0.0)
    terms = [t.astype(F32) for v in (bias[...], gain, shift) for t in split_terms(v)]
    info[...] = jnp.concatenate(terms + [jnp.zeros((INFO - len(terms), bias.shape[1]), F32)], axis=0).astype(BF16)
    heads, prompts, seq, _ = patterns.shape
    query = lax.broadcasted_iota(jnp.int32, (seq, seq), 0)
    key = lax.broadcasted_iota(jnp.int32, (seq, seq), 1)
    for p in range(prompts):
        keep = (key <= query) & (key < lengths[p])
        for head in range(heads):
            pattern = jnp.where(keep, patterns[head, p].astype(F32), 0.0)
            zero = jnp.zeros_like(pattern)
            row = jnp.concatenate([pattern if q == p else zero for q in range(prompts)], axis=1)
            mixing[head, p * seq : (p + 1) * seq, :] = row.astype(BF16)
    rows = scale.shape[1]
    scales[...] = jnp.broadcast_to(scale[...], (rows, rows)).T


def start_body(ranges, place, state, weight, enc, *refs):
    sends, sems = refs[:-1], refs[-1]
    width, rows = state.shape
    part = width // 2
    low = state[...].astype(BF16)
    sends[0][...] = low

    def copies(source, first, size, at, group):
        made = []
        for step in range(1, ranges):
            start = pl.multiple_of(partner(place[0], step, ranges) * width + first, 16)
            made.append(
                pltpu.make_async_copy(
                    source.at[pl.ds(start, size), pl.ds(0, rows)],
                    sends[step].at[pl.ds(at, size)],
                    sems.at[group, step - 1],
                )
            )
        return made

    rest = copies(enc, place[3] * part, part, width, 0)
    for copy in rest:
        copy.start()

    @pl.when(place[2] == 0)
    def _():
        for send in sends[1:]:
            send[0:width] = low

    @pl.when(place[2] > 0)
    def _():
        carried = copies(weight, 0, width, 0, 1)
        for copy in carried:
            copy.start()
        for copy in carried:
            copy.wait()

    for copy in rest:
        copy.wait()


def carry(place, ranges, weight, width, first, count, made, sends):
    rows, half = made[0].shape
    for n, block in enumerate(made):
        sends[0][n * rows : (n + 1) * rows] = block
    for step in range(1, ranges):
        other = partner(place[0], step, ranges)
        for n, block in enumerate(made):
            at, size = n * rows, min(max(count - n * rows, 0), rows)
            if size > 0:
                start = pl.multiple_of(other * width + first + at, 16)
                carried = weight[pl.ds(start, size), half:]
                sends[step][at : at + size] = jnp.where(place[2] == 0, block[0:size], carried)
            if size < rows:
                sends[step][at + size : at + rows] = block[size:]


def values_body(ranges, place, *refs):
    blocks, (weight, own, other, passed) = refs[:ranges], refs[ranges:]
    width, half = blocks[0].shape[0], own.shape[1]
    acc = None
    for step, block in enumerate(blocks):
        n = partner(place[0], step, ranges) if step else place[0]
        if step:
            size = block.shape[0] - width
            passed[(step - 1) * size : step * size] = block[width:]
        part = dot_tn(block[0:width], weight[pl.ds(pl.multiple_of(n * width, 16), width), :])
        acc = part if acc is None else acc + part
    first = place[1] == 0
    own[...] = jnp.where(first, acc[:, :half], acc[:, half:])
    other[...] = jnp.where(first, acc[:, half:], acc[:, :half])


def mix(mixing, head, values):
    return jnp.dot(mixing[head], values, preferred_element_type=F32).astype(BF16)


def heads_body(ranges, per_group, width, place, own, got, scales, mixing, weight, *sends):
    values = ((own[...] + got[...]) * scales[...]).astype(BF16)
    made = [mix(mixing, place[0] * per_group + u, values) for u in range(per_group)]
    carry(place, ranges, weight, width, 0, sends[0].shape[0], made, sends)


def sums_body(ranges, width, done, place, own, got, weight, info, *sends):
    made = [(own[n] + got[n].astype(F32)).astype(BF16) for n in range(own.shape[0])]
    carry(place, ranges, weight, width, done, width - done, made, sends)
    for send in sends:
        send[send.shape[0] - INFO :] = info[...]


def halves_of(first, mine, theirs):
    return jnp.concatenate([jnp.where(first, mine, theirs), jnp.where(first, theirs, mine)], axis=1)


def spread_values_body(ranges, carried, place, low, weight, *refs):
    others = ranges - 1
    firsts, seconds, thirds = (refs[i * others : (i + 1) * others] for i in range(3))
    own, other = refs[3 * others :]
    width, rows = low.shape
    first = place[1] == 0
    state = low[...]
    for step in range(ranges):
        if step == 0:
            n = place[0]
            both = dot_tn(state, weight[pl.ds(pl.multiple_of(n * width, 16), width), :])
            even, odd = both[:, : own.shape[2]], both[:, own.shape[2] :]
        else:
            n = partner(place[0], step, ranges)
            even = dot_tn(state, firsts[step - 1][0:width])
            odd, at = None, 0
            for piece in (seconds[step - 1], thirds[step - 1]):
                size = min(carried, width - at)
                part = dot_tn(state[at : at + size], piece[0:size])
                odd = part if odd is None else odd + part
                at += size
        own[n] = jnp.where(first, even, odd)
        other[n] = jnp.where(first, odd, even).astype(BF16)


def scaled_body(scales, *refs):
    *blocks, out = refs
    for n in range(out.shape[0]):
        out[n] = (total([b[n] for b in blocks]) * scales[...]).astype(BF16)


def finish(ranges, place, acc, blocks, passed, enc, weight_scale, middle, own, other, parts):
    width = middle.shape[0]
    size = width // 2
    middle[...] = acc
    normed = (acc * weight_scale[...]).astype(BF16)
    here = place[3] == 0
    mine = jnp.where(here, normed[:size], normed[size:])
    theirs = jnp.where(here, normed[size:], normed[:size])
    parts[place[0]] = dot_tn(normed, enc[pl.ds(pl.multiple_of(place[0] * width, 16), width), :])
    for step in range(1, ranges):
        parts[partner(place[0], step, ranges)] = dot_tn(mine, blocks[step - 1][width:]) + dot_tn(
            theirs, passed[(step - 1) * size : step * size]
        )
    share = ranges // 2
    own[...] = parts[pl.ds(place[1] * share, share)]
    other[...] = parts[pl.ds((1 - place[1]) * share, share)].astype(BF16)


def first_code_body(ranges, per_group, place, *refs):
    got, also = (refs[i * ranges : (i + 1) * ranges] for i in range(2))
    blocks = refs[2 * ranges : 3 * ranges - 1]
    passed, state, weight, *ends = refs[3 * ranges - 1 :]
    rows = state.shape[1]
    first = place[1] == 0
    acc = state[...]
    for step in range(ranges):
        n = partner(place[0], step, ranges) if step else place[0]
        for u in range(per_group):
            span = slice(u * rows, (u + 1) * rows)
            acc = acc + dot_nt(weight[n * per_group + u], halves_of(first, got[step][span], also[step][span]))
    finish(ranges, place, acc, blocks, passed, *ends)


def later_code_body(ranges, per_group, place, mine, also, low, rest, mixing, *refs):
    blocks = refs[: ranges - 1]
    passed, weight, *ends = refs[ranges - 1 :]
    first = place[1] == 0
    acc = low[...].astype(F32) + rest[0].astype(F32)
    for n in range(ranges):
        values = halves_of(first, mine[n], also[n])
        for u in range(per_group):
            acc = acc + dot_nt(weight[n * per_group + u], mix(mixing, n * per_group + u, values))
    finish(ranges, place, acc, blocks, passed, *ends)


def clamp_body(seq, place, lengths, *refs):
    *refs, out = refs
    blocks, facts = refs[: len(refs) // 2], refs[len(refs) // 2 :]
    share, rows, cols = out.shape
    ranges = len(blocks)
    row = lax.broadcasted_iota(jnp.int32, out.shape[1:], 0)
    end = jnp.full(row.shape, lengths[0], jnp.int32)
    for p in range(1, rows // seq):
        end = jnp.where(row >= p * seq, p * seq + lengths[p], end)
    live = row < end
    terms = [f[f.shape[0] - INFO :].astype(F32) for f in facts]
    terms = [
        [t[3 * i : 3 * i + 1] + t[3 * i + 1 : 3 * i + 2] + t[3 * i + 2 : 3 * i + 3] for i in range(3)] for t in terms
    ]
    for n in range(share):
        number = place[1] * share + n
        bias, gain, shift = terms[0]
        for step in range(1, ranges):
            here = partner(place[0], step, ranges) == number
            bias, gain, shift = (jnp.where(here, b, a) for a, b in zip((bias, gain, shift), terms[step]))
        preact = total([b[n * rows : (n + 1) * rows] for b in blocks]) + bias
        clamped = jnp.maximum(preact, 0.0) * gain + shift
        out[n] = jnp.where(live, clamped, 0.0).astype(BF16)


def ordered(place, mine, also):
    first = place[1] == 0
    share = mine.shape[0]
    return [jnp.where(first, mine[n], also[n]) for n in range(share)] + [
        jnp.where(first, also[n], mine[n]) for n in range(share)
    ]


def decode_body(layer, adds, linked, sends, keeps, place, *refs):
    refs = list(refs)
    take = lambda count: [refs.pop(0) for _ in range(count)]
    (mine, also, dec), added, links, before = take(3), take(adds), take(linked), take(2 if keeps else 0)
    state_out, feats_out = take(2)
    feats = ordered(place, mine, also)
    acc = added[0][...]
    for piece in added[1:]:
        acc = acc + piece[...]
    for piece in links:
        acc = acc + piece[1].astype(F32)
    acc = acc + dot_nt(dec[layer], jnp.concatenate(feats, axis=1))
    block = feats[0]
    for n in range(1, len(feats)):
        block = jnp.where(place[0] == n, feats[n], block)
    if sends:
        low = acc.astype(BF16)
        refs[0][...] = low
        refs[1][...] = (acc - low.astype(F32)).astype(BF16)
    if keeps:
        here = place[2] == layer
        state_out[...] = jnp.where(here, acc, before[0][...])
        feats_out[...] = jnp.where(here, block, before[1][...])
    else:
        state_out[...] = acc
        feats_out[...] = block


def writes_body(layer, linked, place, mine, also, dec, left, *refs):
    out = refs[-1]
    feats = jnp.concatenate(ordered(place, mine, also), axis=1)
    out[0] = left[...]
    for n in range(1, out.shape[0]):
        made = dot_nt(dec[layer + n], feats)
        out[n] = (made + refs[0][n + 1].astype(F32) if linked else made).astype(BF16)


def after(value, *others):
    return lax.optimization_barrier((value, *others))[0]


def tiled(
    residual_in,
    attn_scale,
    mlp_scale,
    patterns,
    lengths,
    value_proj,
    out_proj,
    enc_weight,
    enc_bias,
    dec_weight,
    errors,
    clamp_mode,
    clamp_index,
    clamp_values,
    active_blocks,
):
    layers = lax.axis_size("layer")
    ranges = lax.axis_size("feat")
    seq = patterns.shape[3]
    head_dim, per_group = out_proj.shape[2:4]
    kv_cols = value_proj.shape[3]
    half = kv_cols // 2
    width = residual_in.shape[2]
    block_len = enc_bias.shape[1]
    rows = residual_in.shape[0]
    share = ranges // 2
    place = jnp.stack([lax.axis_index("feat"), lax.axis_index("tok"), lax.axis_index("layer"), lax.axis_index("groups")]).astype(jnp.int32)

    source = residual_in[:, 0, :].T
    error_cols = errors[0, :, 0, :].T
    out_weight = out_proj[0, :, :, :, 0, :].transpose(0, 2, 3, 1).reshape(-1, width, head_dim)
    dec_cols = dec_weight[0, :, :, 0, :].transpose(0, 2, 1)
    value_rows = value_proj[0, 0]
    enc_rows = enc_weight[0, 0]

    def handed_on(value):
        return lax.ppermute(value, "layer", [(n, (n + 1) % layers) for n in range(layers)])

    packed = carried = rest = low = kept = None
    for layer in range(layers):
        if layer == 0:
            sends = kernel_call(
                functools.partial(start_body, ranges),
                [shape(width, rows, dtype=BF16)] + [shape(width + width // 2, rows, dtype=BF16)] * (ranges - 1),
                [place],
                [source],
                left=[value_rows, enc_rows],
                scratch=[pltpu.SemaphoreType.DMA((2, ranges - 1))],
            )
            blocks = exchange(sends)
            info, mixing, scales = kernel_call(
                facts_body,
                [
                    shape(INFO, block_len, dtype=BF16),
                    shape(patterns.shape[1], rows, rows, dtype=BF16),
                    shape(rows, half),
                ],
                [place, lengths, active_blocks, clamp_values],
                [
                    clamp_mode.reshape(-1, block_len),
                    clamp_index.reshape(-1, block_len),
                    enc_bias,
                    attn_scale,
                    patterns[0],
                ],
            )
            blocks[0], info, mixing, scales = lax.optimization_barrier((blocks[0], info, mixing, scales))
            own, other, passed = kernel_call(
                functools.partial(values_body, ranges),
                [shape(rows, half)] * 2 + [shape((ranges - 1) * (width // 2), rows, dtype=BF16)],
                [place],
                [*blocks, value_rows],
                flops=4 * rows * value_rows.size,
            )
            got = swap(other, "tok", 1)
            passed = swap(passed, "groups", 1)
            packed = [*blocks[1:], passed]
            sends = kernel_call(
                functools.partial(heads_body, ranges, per_group, width),
                [shape(per_group * rows, half, dtype=BF16)] * ranges,
                [place],
                [own, got, scales, mixing, value_rows],
            )
            got = exchange(sends)
            also = [swap(b, "tok", 1) for b in got]
            carried = [*blocks[1:], *got[1:]]
            code = functools.partial(first_code_body, ranges, per_group)
            scalars, given = [place], [*got, *also, *packed, source]
        else:
            own, other = kernel_call(
                functools.partial(spread_values_body, ranges, per_group * rows),
                [shape(ranges, rows, half), shape(ranges, rows, half, dtype=BF16)],
                [place],
                [low, value_rows, *carried],
                flops=2 * rows * value_rows.size,
            )
            part = (own + swap(other, "tok", 1).astype(F32)).astype(BF16)
            blocks = spread(part)
            rest = handed_on(after(rest, low))
            mine = kernel_call(scaled_body, shape(ranges, rows, half, dtype=BF16), [], [scales, *blocks])
            code = functools.partial(later_code_body, ranges, per_group)
            scalars, given = [place], [mine, swap(mine, "tok", 1), low, rest, mixing, *packed]
        middle, own, other = kernel_call(
            code,
            [
                shape(width, rows),
                shape(share, rows, block_len),
                shape(share, rows, block_len, dtype=BF16),
            ],
            scalars,
            [*given, out_weight, enc_rows, mlp_scale],
            scratch=[pltpu.VMEM((ranges, rows, block_len), F32)],
            flops=2 * rows * (out_weight.size + width * block_len * ranges),
        )
        got = swap(other, "tok", 1)
        if layer == 0:
            sends = kernel_call(
                functools.partial(sums_body, ranges, width, per_group * rows),
                [shape(share * rows + INFO, block_len, dtype=BF16)] * ranges,
                [place],
                [own, got, value_rows, info],
            )
            blocks = facts = exchange(sends)
            carried += blocks[1:]
        else:
            blocks = spread((own + got.astype(F32)).astype(BF16).reshape(-1, block_len))
        mine = kernel_call(
            functools.partial(clamp_body, seq),
            shape(share, rows, block_len, dtype=BF16),
            [place, lengths],
            [*blocks, *facts],
        )
        also = swap(mine, "tok", 1)
        more = layer + 1 < layers
        added = [middle, error_cols]
        links = [rest] if layer > 0 else []
        outs = [shape(width, rows), shape(rows, block_len, dtype=BF16)]
        if more:
            outs += [shape(width, rows, dtype=BF16)] * 2
        made = kernel_call(
            functools.partial(decode_body, layer, len(added), len(links), more, kept is not None),
            outs,
            [place],
            [mine, also, dec_cols, *added, *links, *(kept or ())],
            flops=2 * rows * dec_cols.size // layers,
        )
        kept = made[:2]
        if more:
            low = handed_on(made[2])
            rest = kernel_call(
                functools.partial(writes_body, layer, len(links)),
                shape(layers - layer, width, rows, dtype=BF16),
                [place],
                [mine, also, dec_cols, made[3], *links],
                flops=2 * rows * dec_cols.size,
            )
    return kept[0].T[None, :, None, :], kept[1][None]


def local(residual_in, attn_scale, mlp_scale, patterns, lengths, value_proj, out_proj, enc_weight, enc_bias, *others):
    whole = (
        residual_in.shape[0] % LANES == 0
        and residual_in.shape[2] % 32 == 0
        and value_proj.shape[3] == out_proj.shape[2]
        and value_proj.shape[3] == 2 * enc_bias.shape[1] == 2 * residual_in.shape[0]
        and residual_in.shape[2] <= residual_in.shape[0] * (out_proj.shape[3] + lax.axis_size("feat") // 2)
        and lax.axis_size("feat") % 2 == 0
        and lax.axis_size("tok") == lax.axis_size("groups") == 2
    )
    run = tiled if whole else plain
    return run(
        residual_in, attn_scale, mlp_scale, patterns, lengths, value_proj, out_proj, enc_weight, enc_bias, *others
    )


def solution(mesh):
    return jax.shard_map(
        local,
        mesh=mesh,
        in_specs=(
            P("groups", "tok", "feat"),
            P("layer", "groups"),
            P("layer", "groups"),
            P("layer", None, "groups", None, None),
            P("groups"),
            P("layer", "tok", None, "feat"),
            P("layer", None, None, None, "tok", "feat"),
            P("layer", "tok", None, "feat"),
            P("layer", "feat"),
            P("layer", None, None, "tok", "feat"),
            P("layer", "groups", "tok", "feat"),
            P("layer", "feat"),
            P("layer", "feat"),
            P(),
            P("layer", "feat"),
        ),
        out_specs=(P("layer", "groups", "tok", "feat"), P("layer", "groups", "feat")),
        check_vma=False,
    )
```

```python
import functools

import jax
import jax.numpy as jnp
from jax import lax
from jax.experimental import pallas as pl
from jax.experimental.pallas import tpu as pltpu
from jax.sharding import PartitionSpec as P

BF16 = jnp.bfloat16
F32 = jnp.float32


def peers(axis):
    count = lax.axis_size(axis)
    return range(1, count)


def partner(index, step, count):
    if count & (count - 1) == 0:
        return index ^ step
    return (step - index) % count


def swap(value, axis, step, first_layer=0):
    count = lax.axis_size(axis)
    if first_layer == 0:
        return lax.ppermute(value, axis, [(s, partner(s, step, count)) for s in range(count)])
    layers = lax.axis_size("layer")
    pairs = [
        (s * layers + n, partner(s, step, count) * layers + n)
        for s in range(count)
        for n in range(first_layer, layers)
    ]
    return lax.ppermute(value, (axis, "layer"), pairs)


def spread(value, axis="feat"):
    return [value] + [swap(value, axis, step) for step in peers(axis)]


def exchange(sends):
    got = {step: swap(sends[step], "feat", step) for step in reversed(peers("feat"))}
    return [sends[0]] + [got[step] for step in peers("feat")]


def total(blocks):
    result = blocks[0].astype(F32)
    for block in blocks[1:]:
        result = result + block.astype(F32)
    return result


def dot_tn(left, right):
    return lax.dot_general(left, right, (((0,), (0,)), ((), ())), preferred_element_type=F32)


def dot_nt(left, right):
    return lax.dot_general(left, right, (((1,), (1,)), ((), ())), preferred_element_type=F32)


def pick(array, index):
    return lax.dynamic_index_in_dim(array, index, 0, keepdims=False)


def redistribute(weight, ranges, my_range, first_layer):
    blocks = weight.reshape(ranges, -1, weight.shape[1])
    got = [pick(blocks, my_range)]
    for step in peers("feat"):
        other = partner(my_range, step, ranges)
        got.append(swap(pick(blocks, other), "feat", step, first_layer))
    got = jnp.stack(got)
    return [pick(got, partner(my_range, n, ranges)) for n in range(ranges)]


def plain(
    residual_in,
    attn_scale,
    mlp_scale,
    patterns,
    lengths,
    value_proj,
    out_proj,
    enc_weight,
    enc_bias,
    dec_weight,
    errors,
    clamp_mode,
    clamp_index,
    clamp_values,
    active_blocks,
):
    layers = lax.axis_size("layer")
    ranges = lax.axis_size("feat")
    my_layer = lax.axis_index("layer")
    my_range = lax.axis_index("feat")
    my_slab = lax.axis_index("tok")
    prompts, seq = patterns.shape[2:4]
    head_dim, per_group = out_proj.shape[2:4]
    kv_cols = value_proj.shape[3]
    half = kv_cols // 2
    width = residual_in.shape[2]
    block_len = enc_bias.shape[1]
    act = block_len * ranges
    rows = residual_in.shape[0]

    source = residual_in[:, 0, :].T
    error_cols = errors[0, :, 0, :].T
    scale_attn = attn_scale[0]
    scale_mlp = mlp_scale[0]

    chosen = active_blocks[0, 0]
    modes = pick(clamp_mode[0].reshape(-1, block_len), chosen)
    entries = pick(clamp_index[0].reshape(-1, block_len), chosen)
    table_ids = jnp.arange(clamp_values.shape[0], dtype=jnp.int32)
    levels = jnp.sum(jnp.where(entries[:, None] == table_ids[None, :], clamp_values[None, :], 0.0), axis=1)
    gain = jnp.where(modes == 1, 0.0, jnp.where(modes == 2, levels, 1.0))
    shift = jnp.where(modes == 1, levels, 0.0)
    mine = jnp.stack([enc_bias[0], gain, shift])
    got = jnp.stack(spread(mine))
    clamp_all = jnp.stack([pick(got, partner(my_range, n, ranges)) for n in range(ranges)], axis=1).reshape(3, act)
    clamp_half = lax.dynamic_slice_in_dim(clamp_all, my_slab * (act // 2), act // 2, 1)

    positions = jnp.arange(seq, dtype=jnp.int32)
    keep = (positions[None, None, :] <= positions[None, :, None]) & (positions[None, None, :] < lengths[:, None, None])
    masked = jnp.where(keep[None], patterns[0], jnp.zeros_like(patterns[0]))
    zero = jnp.zeros_like(masked[:, 0])
    mixing = jnp.concatenate(
        [
            jnp.concatenate([masked[:, p] if q == p else zero for q in range(prompts)], axis=2)
            for p in range(prompts)
        ],
        axis=1,
    ).reshape(-1, per_group * rows, rows)
    live = (positions[None, :] < lengths[:, None]).reshape(rows)

    value_rows = value_proj[0, 0]
    own_value, other_value = (
        lax.dynamic_slice_in_dim(value_rows, n * half, half, 1) for n in (my_slab, 1 - my_slab)
    )
    out_cols = out_proj[0, :, :, :, 0, :].reshape(ranges, 2, half, per_group, width).transpose(1, 0, 4, 3, 2).reshape(2, ranges, width, per_group * half)
    out_own, out_other = (pick(out_cols, n) for n in (my_slab, 1 - my_slab))
    group_of = [n * kv_cols // head_dim for n in range(ranges)]

    enc_blocks = jnp.concatenate(redistribute(enc_weight[0, 0], ranges, my_range, 0), axis=1)
    enc_own, enc_other = (
        lax.dynamic_slice_in_dim(enc_blocks, n * (act // 2), act // 2, 1) for n in (my_slab, 1 - my_slab)
    )
    value_blocks = redistribute(value_rows, ranges, my_range, 1)
    spread_own, spread_other = (
        jnp.concatenate([lax.dynamic_slice_in_dim(b, n * half, half, 1) for b in value_blocks], axis=1)
        for n in (my_slab, 1 - my_slab)
    )
    dec_cols = dec_weight[0, :, :, 0, :].transpose(0, 2, 1)

    def over_slabs(own, other):
        return own + swap(other, "tok", 1).astype(F32)

    def heads(values, group):
        mixed = jnp.dot(mixing[group] if isinstance(group, int) else pick(mixing, group), values, preferred_element_type=F32)
        return mixed.astype(BF16).reshape(per_group, rows, -1).transpose(1, 0, 2).reshape(rows, -1)

    def first_attention(state):
        normed = (state * scale_attn[None, :]).astype(BF16)
        blocks = spread(normed)
        own_rows, other_rows = (w.reshape(ranges, width, half) for w in (own_value, other_value))
        order = [partner(my_range, n, ranges) if n else my_range for n in range(ranges)]
        other = sum(dot_tn(b, pick(other_rows, n)) for b, n in zip(blocks, order))
        own = sum(dot_tn(b, pick(own_rows, n)) for b, n in zip(blocks, order))
        values = over_slabs(own, other).astype(BF16)
        mine = heads(values, my_range * kv_cols // head_dim)
        got = spread(mine)
        also = [swap(b, "tok", 1) for b in got]
        return sum(
            dot_nt(pick(out_own, n), b) + dot_nt(pick(out_other, n), c) for n, b, c in zip(order, got, also)
        )

    def later_attention(state_low):
        other = dot_tn(state_low, spread_other).astype(BF16)
        own = dot_tn(state_low, spread_own)
        part = over_slabs(own, other).astype(BF16)
        mine = (total(spread(part)) * scale_attn[:, None]).astype(BF16)
        also = swap(mine, "tok", 1)
        result = 0.0
        for n in range(ranges):
            cols = slice(n * half, (n + 1) * half)
            result = (
                result
                + dot_nt(out_own[n], heads(mine[:, cols], group_of[n]))
                + dot_nt(out_other[n], heads(also[:, cols], group_of[n]))
            )
        return result

    def code(middle):
        normed = (middle * scale_mlp[None, :]).astype(BF16)
        other = dot_tn(normed, enc_other).astype(BF16)
        own = dot_tn(normed, enc_own)
        part = over_slabs(own, other).astype(BF16)
        preact = total(spread(part)) + clamp_half[0][None, :]
        clamped = jnp.maximum(preact, 0.0) * clamp_half[1][None, :] + clamp_half[2][None, :]
        mine = jnp.where(live[:, None], clamped, 0.0).astype(BF16)
        also = swap(mine, "tok", 1)
        return jnp.concatenate(
            [jnp.where(my_slab == 0, mine, also), jnp.where(my_slab == 0, also, mine)], axis=1
        )

    def handed_on(value, layer):
        return lax.ppermute(value, "layer", [(layer, layer + 1)])

    states = jnp.zeros_like(source)
    feats = jnp.zeros((rows, block_len), BF16)
    state, links = source, None
    for layer in range(layers):
        if layer == 0:
            middle = state + first_attention(state)
        else:
            middle = low.astype(F32) + later_attention(low) + rest.astype(F32)
        kept = code(middle)
        recon = dot_nt(dec_cols[layer], kept)
        base = middle + error_cols
        if layer > 0:
            base = base + links[0]
        state = base + recon
        states = jnp.where(my_layer == layer, state, states)
        feats = jnp.where(
            my_layer == layer, lax.dynamic_slice_in_dim(kept, my_range * block_len, block_len, 1), feats
        )
        if layer + 1 < layers:
            low = state.astype(BF16)
            left = (state - low.astype(F32)).astype(BF16)
            low = handed_on(low, layer)
            writes = jnp.stack([dot_nt(dec_cols[n], kept) for n in range(layer + 1, layers)])
            if layer > 0:
                writes = writes + links[1:]
            rest = handed_on(left, layer)
            links = handed_on(writes, layer)
    return states.T[None, :, None, :], feats[None]


LANES = 128
INFO = 16


def shape(*sizes, dtype=F32):
    return jax.ShapeDtypeStruct(sizes, dtype)


def kernel_call(body, outs, scalars, arrays, left=(), scratch=(), flops=0, room=16 * 1024 * 1024):
    many = isinstance(outs, (list, tuple))
    kept = list(outs) if many else [outs]
    size = sum(a.size * a.dtype.itemsize for a in arrays) + sum(a.size * a.dtype.itemsize for a in kept)
    return pl.pallas_call(
        body,
        out_shape=tuple(kept) if many else outs,
        in_specs=[pl.BlockSpec(memory_space=pltpu.SMEM)] * len(scalars) + [pl.BlockSpec(memory_space=pltpu.VMEM)] * len(arrays) + [pl.BlockSpec(memory_space=pltpu.HBM)] * len(left),
        out_specs=tuple(pl.BlockSpec(memory_space=pltpu.VMEM) for _ in kept) if many else pl.BlockSpec(memory_space=pltpu.VMEM),
        scratch_shapes=list(scratch),
        compiler_params=pltpu.CompilerParams(vmem_limit_bytes=room),
        cost_estimate=pl.CostEstimate(flops=int(flops), bytes_accessed=int(size), transcendentals=0),
    )(*scalars, *arrays, *left)


def place_of():
    return [lax.axis_index(axis) for axis in ("feat", "tok", "layer", "groups")]


def split_terms(value):
    high = value.astype(BF16)
    left = value - high.astype(F32)
    middle = left.astype(BF16)
    low = (left - middle.astype(F32)).astype(BF16)
    return [high, middle, low]


def facts_body(lengths, chosen, table, mode, index, bias, scale, patterns, info, mixing, scales, lives):
    block = chosen[0, 0]
    modes = mode[pl.ds(block, 1), :]
    entries = index[pl.ds(block, 1), :]
    levels = jnp.zeros(entries.shape, F32)
    for n in range(table.shape[0]):
        levels = jnp.where(entries == n, table[n], levels)
    gain = jnp.where(modes == 1, 0.0, jnp.where(modes == 2, levels, 1.0))
    shift = jnp.where(modes == 1, levels, 0.0)
    terms = [t.astype(F32) for v in (bias[...], gain, shift) for t in split_terms(v)]
    info[...] = jnp.concatenate(terms + [jnp.zeros((INFO - len(terms), bias.shape[1]), F32)], axis=0).astype(BF16)
    heads, prompts, seq, _ = patterns.shape
    query = lax.broadcasted_iota(jnp.int32, (seq, seq), 0)
    key = lax.broadcasted_iota(jnp.int32, (seq, seq), 1)
    for p in range(prompts):
        keep = (key <= query) & (key < lengths[p])
        for head in range(heads):
            pattern = jnp.where(keep, patterns[head, p].astype(F32), 0.0)
            zero = jnp.zeros_like(pattern)
            row = jnp.concatenate([pattern if q == p else zero for q in range(prompts)], axis=1)
            mixing[head, p * seq : (p + 1) * seq, :] = row.astype(BF16)
    rows = scale.shape[1]
    scales[...] = jnp.broadcast_to(scale[...], (rows, rows)).T
    row = lax.broadcasted_iota(jnp.int32, lives.shape, 0)
    end = jnp.full(row.shape, lengths[0], jnp.int32)
    for p in range(1, prompts):
        end = jnp.where(row >= p * seq, p * seq + lengths[p], end)
    lives[...] = jnp.where(row < end, 1.0, 0.0)


def start_body(ranges, state, weight, enc, *refs):
    place = place_of()
    sends, sems = (None, *refs[:-1]), refs[-1]
    width, rows = state.shape
    part = width // 2
    low = state[...].astype(BF16)

    def copies(source, first, size, at, group):
        made = []
        for step in range(1, ranges):
            start = pl.multiple_of(partner(place[0], step, ranges) * width + first, 16)
            made.append(
                pltpu.make_async_copy(
                    source.at[pl.ds(start, size), pl.ds(0, rows)],
                    sends[step].at[pl.ds(at, size)],
                    sems.at[group, step - 1],
                )
            )
        return made

    rest = copies(enc, place[3] * part, part, width, 0)
    for copy in rest:
        copy.start()

    @pl.when(place[2] == 0)
    def _():
        for send in sends[1:]:
            send[0:width] = low

    @pl.when(place[2] > 0)
    def _():
        carried = copies(weight, 0, width, 0, 1)
        for copy in carried:
            copy.start()
        for copy in carried:
            copy.wait()

    for copy in rest:
        copy.wait()


def carry(place, ranges, weight, width, first, count, made, sends):
    rows, half = made[0].shape
    for n, block in enumerate(made):
        sends[0][n * rows : (n + 1) * rows] = block
    for step in range(1, ranges):
        other = partner(place[0], step, ranges)
        for n, block in enumerate(made):
            at, size = n * rows, min(max(count - n * rows, 0), rows)
            if size > 0:
                start = pl.multiple_of(other * width + first + at, 16)
                carried = weight[pl.ds(start, size), half:]
                sends[step][at : at + size] = jnp.where(place[2] == 0, block[0:size], carried)
            if size < rows:
                sends[step][at + size : at + rows] = block[size:]


def values_body(ranges, *refs):
    blocks, (weight, own, passed) = refs[:ranges], refs[ranges:]
    width = passed.shape[0] // (ranges - 1) * 2
    place = place_of()
    acc = None
    for step, block in enumerate(blocks):
        n = partner(place[0], step, ranges) if step else place[0]
        if step:
            size = block.shape[0] - width
            passed[(step - 1) * size : step * size] = block[width:]
        part = dot_tn(block[0:width].astype(BF16), weight[pl.ds(pl.multiple_of(n * width, 16), width), :])
        acc = part if acc is None else acc + part
    own[...] = acc


def mix(mixing, head, values):
    return jnp.dot(mixing[head], values, preferred_element_type=F32).astype(BF16)


def whole_values_body(ranges, width, own, got, scales, weight, *sends):
    place = place_of()
    rows, half = scales.shape
    made = [
        ((own[:, n * half : (n + 1) * half] + got[:, n * half : (n + 1) * half]) * scales[...]).astype(BF16)
        for n in range(2)
    ]
    carry(place, ranges, weight, width, 0, 2 * rows, made, sends)


def sums_body(ranges, width, done, own, got, weight, info, *sends):
    place = place_of()
    made = [(own[n] + got[n].astype(F32)).astype(BF16) for n in range(own.shape[0])]
    carry(place, ranges, weight, width, done, width - done, made, sends)
    for send in sends:
        send[send.shape[0] - INFO :] = info[...]


def halves_of(first, mine, theirs):
    return jnp.concatenate([jnp.where(first, mine, theirs), jnp.where(first, theirs, mine)], axis=1)


def spread_values_body(ranges, carried, low, weight, *refs):
    place = place_of()
    others = ranges - 1
    firsts, seconds, thirds = (refs[i * others : (i + 1) * others] for i in range(3))
    own, other = refs[3 * others :]
    width, rows = low.shape
    first = place[1] == 0
    state = low[...]
    for step in range(ranges):
        if step == 0:
            n = place[0]
            both = dot_tn(state, weight[pl.ds(pl.multiple_of(n * width, 16), width), :])
            even, odd = both[:, : own.shape[2]], both[:, own.shape[2] :]
        else:
            n = partner(place[0], step, ranges)
            even = dot_tn(state, firsts[step - 1][0:width])
            odd, at = None, 0
            for piece in (seconds[step - 1], thirds[step - 1]):
                size = min(carried, width - at)
                part = dot_tn(state[at : at + size], piece[0:size])
                odd = part if odd is None else odd + part
                at += size
        own[n] = jnp.where(first, even, odd)
        other[n] = jnp.where(first, odd, even).astype(BF16)


def scaled_body(scales, *refs):
    *blocks, out = refs
    for n in range(out.shape[0]):
        out[n] = (total([b[n] for b in blocks]) * scales[...]).astype(BF16)


def finish(ranges, place, acc, blocks, passed, enc, weight_scale, middle, own, other, parts):
    width = middle.shape[0]
    size = width // 2
    middle[...] = acc
    normed = (acc * weight_scale[...]).astype(BF16)
    here = place[3] == 0
    mine = jnp.where(here, normed[:size], normed[size:])
    theirs = jnp.where(here, normed[size:], normed[:size])
    parts[place[0]] = dot_tn(normed, enc[pl.ds(pl.multiple_of(place[0] * width, 16), width), :])
    for step in range(1, ranges):
        parts[partner(place[0], step, ranges)] = dot_tn(mine, blocks[step - 1][width:]) + dot_tn(
            theirs, passed[(step - 1) * size : step * size]
        )
    share = ranges // 2
    own[...] = parts[pl.ds(place[1] * share, share)]
    other[...] = parts[pl.ds((1 - place[1]) * share, share)].astype(BF16)


def first_code_body(ranges, per_group, *refs):
    place = place_of()
    got, blocks = refs[:ranges], refs[ranges : 2 * ranges - 1]
    passed, state, mixing, weight, *ends = refs[2 * ranges - 1 :]
    rows = state.shape[1]
    acc = state[...]
    for step in range(ranges):
        n = partner(place[0], step, ranges) if step else place[0]
        values = jnp.concatenate([got[step][0:rows], got[step][rows:]], axis=1)
        for u in range(per_group):
            acc = acc + dot_nt(weight[n * per_group + u], mix(mixing, n * per_group + u, values))
    finish(ranges, place, acc, blocks, passed, *ends)


def later_code_body(ranges, per_group, mine, also, low, rest, mixing, *refs):
    place = place_of()
    blocks = refs[: ranges - 1]
    passed, weight, *ends = refs[ranges - 1 :]
    first = place[1] == 0
    acc = low[...].astype(F32) + rest[0].astype(F32)
    for n in range(ranges):
        values = halves_of(first, mine[n], also[n])
        for u in range(per_group):
            acc = acc + dot_nt(weight[n * per_group + u], mix(mixing, n * per_group + u, values))
    finish(ranges, place, acc, blocks, passed, *ends)


def clamp_body(*refs):
    place = place_of()
    *refs, lives, out = refs
    blocks, facts = refs[: len(refs) // 2], refs[len(refs) // 2 :]
    share, rows, _ = out.shape
    ranges = len(blocks)
    live = lives[...] > 0.5
    terms = [f[f.shape[0] - INFO :].astype(F32) for f in facts]
    terms = [
        [t[3 * i : 3 * i + 1] + t[3 * i + 1 : 3 * i + 2] + t[3 * i + 2 : 3 * i + 3] for i in range(3)] for t in terms
    ]
    for n in range(share):
        number = place[1] * share + n
        bias, gain, shift = terms[0]
        for step in range(1, ranges):
            here = partner(place[0], step, ranges) == number
            bias, gain, shift = (jnp.where(here, b, a) for a, b in zip((bias, gain, shift), terms[step]))
        preact = total([b[n * rows : (n + 1) * rows] for b in blocks]) + bias
        clamped = jnp.maximum(preact, 0.0) * gain + shift
        out[n] = jnp.where(live, clamped, 0.0).astype(BF16)


def ordered(place, mine, also):
    first = place[1] == 0
    share = mine.shape[0]
    return [jnp.where(first, mine[n], also[n]) for n in range(share)] + [
        jnp.where(first, also[n], mine[n]) for n in range(share)
    ]


def decode_body(layer, adds, linked, sends, keeps, *refs):
    place = place_of()
    refs = list(refs)
    take = lambda count: [refs.pop(0) for _ in range(count)]
    (mine, also, dec), added, links, before = take(3), take(adds), take(linked), take(2 if keeps else 0)
    state_out, feats_out = take(2)
    feats = ordered(place, mine, also)
    acc = added[0][...]
    for piece in added[1:]:
        acc = acc + piece[...]
    for piece in links:
        acc = acc + piece[1].astype(F32)
    acc = acc + dot_nt(dec[layer], jnp.concatenate(feats, axis=1))
    block = feats[0]
    for n in range(1, len(feats)):
        block = jnp.where(place[0] == n, feats[n], block)
    if sends:
        low = acc.astype(BF16)
        refs[0][...] = low
        refs[1][...] = (acc - low.astype(F32)).astype(BF16)
    if keeps:
        here = place[2] == layer
        state_out[...] = jnp.where(here, acc, before[0][...])
        feats_out[...] = jnp.where(here, block, before[1][...])
    else:
        state_out[...] = acc
        feats_out[...] = block


def writes_body(layer, linked, mine, also, dec, left, *refs):
    place = place_of()
    out = refs[-1]
    feats = jnp.concatenate(ordered(place, mine, also), axis=1)
    out[0] = left[...]
    for n in range(1, out.shape[0]):
        made = dot_nt(dec[layer + n], feats)
        out[n] = (made + refs[0][n + 1].astype(F32) if linked else made).astype(BF16)


def after(value, *others):
    return lax.optimization_barrier((value, *others))[0]


def tiled(
    residual_in,
    attn_scale,
    mlp_scale,
    patterns,
    lengths,
    value_proj,
    out_proj,
    enc_weight,
    enc_bias,
    dec_weight,
    errors,
    clamp_mode,
    clamp_index,
    clamp_values,
    active_blocks,
):
    layers = lax.axis_size("layer")
    ranges = lax.axis_size("feat")
    seq = patterns.shape[3]
    head_dim, per_group = out_proj.shape[2:4]
    kv_cols = value_proj.shape[3]
    half = kv_cols // 2
    width = residual_in.shape[2]
    block_len = enc_bias.shape[1]
    rows = residual_in.shape[0]
    share = ranges // 2

    source = residual_in[:, 0, :].T
    error_cols = errors[0, :, 0, :].T
    out_weight = out_proj[0, :, :, :, 0, :].transpose(0, 2, 3, 1).reshape(-1, width, head_dim)
    dec_cols = dec_weight[0, :, :, 0, :].transpose(0, 2, 1)
    value_rows = value_proj[0, 0]
    enc_rows = enc_weight[0, 0]

    def handed_on(value):
        return lax.ppermute(value, "layer", [(n, (n + 1) % layers) for n in range(layers)])

    packed = carried = rest = low = kept = None
    for layer in range(layers):
        if layer == 0:
            sends = kernel_call(
                functools.partial(start_body, ranges),
                [shape(width + width // 2, rows, dtype=BF16)] * (ranges - 1),
                [],
                [source],
                left=[value_rows, enc_rows],
                scratch=[pltpu.SemaphoreType.DMA((2, ranges - 1))],
                room=60 * 1024 * 1024,
            )
            blocks = exchange([source, *sends])
            info, mixing, scales, live = kernel_call(
                facts_body,
                [
                    shape(INFO, block_len, dtype=BF16),
                    shape(patterns.shape[1], rows, rows, dtype=BF16),
                    shape(rows, half),
                    shape(rows, block_len),
                ],
                [lengths, active_blocks, clamp_values],
                [
                    clamp_mode.reshape(-1, block_len),
                    clamp_index.reshape(-1, block_len),
                    enc_bias,
                    attn_scale,
                    patterns[0],
                ],
            )
            blocks[1], info, mixing, scales, live = lax.optimization_barrier((blocks[1], info, mixing, scales, live))
            own, passed = kernel_call(
                functools.partial(values_body, ranges),
                [shape(rows, kv_cols), shape((ranges - 1) * (width // 2), rows, dtype=BF16)],
                [],
                [*blocks, value_rows],
                flops=4 * rows * value_rows.size,
            )
            got = swap(own, "tok", 1)
            passed = swap(passed, "groups", 1)
            packed = [*blocks[1:], passed]
            sends = kernel_call(
                functools.partial(whole_values_body, ranges, width),
                [shape(2 * rows, half, dtype=BF16)] * ranges,
                [],
                [own, got, scales, value_rows],
            )
            got = exchange(sends)
            carried = [*blocks[1:], *got[1:]]
            code = functools.partial(first_code_body, ranges, per_group)
            given = [*got, *packed, source, mixing]
        else:
            own, other = kernel_call(
                functools.partial(spread_values_body, ranges, 2 * rows),
                [shape(ranges, rows, half), shape(ranges, rows, half, dtype=BF16)],
                [],
                [low, value_rows, *carried],
                flops=2 * rows * value_rows.size,
            )
            part = (own + swap(other, "tok", 1).astype(F32)).astype(BF16)
            blocks = spread(part)
            rest = handed_on(after(rest, low))
            mine = kernel_call(scaled_body, shape(ranges, rows, half, dtype=BF16), [], [scales, *blocks])
            code = functools.partial(later_code_body, ranges, per_group)
            scalars, given = [], [mine, swap(mine, "tok", 1), low, rest, mixing, *packed]
        middle, own, other = kernel_call(
            code,
            [
                shape(width, rows),
                shape(share, rows, block_len),
                shape(share, rows, block_len, dtype=BF16),
            ],
            [],
            [*given, out_weight, enc_rows, mlp_scale],
            scratch=[pltpu.VMEM((ranges, rows, block_len), F32)],
            flops=2 * rows * (out_weight.size + width * block_len * ranges),
        )
        got = swap(other, "tok", 1)
        if layer == 0:
            sends = kernel_call(
                functools.partial(sums_body, ranges, width, 2 * rows),
                [shape(share * rows + INFO, block_len, dtype=BF16)] * ranges,
                [],
                [own, got, value_rows, info],
            )
            blocks = facts = exchange(sends)
            carried += blocks[1:]
        else:
            blocks = spread((own + got.astype(F32)).astype(BF16).reshape(-1, block_len))
        mine = kernel_call(
            clamp_body,
            shape(share, rows, block_len, dtype=BF16),
            [],
            [*blocks, *facts, live],
        )
        also = swap(mine, "tok", 1)
        more = layer + 1 < layers
        added = [middle, error_cols]
        links = [rest] if layer > 0 else []
        outs = [shape(width, rows), shape(rows, block_len, dtype=BF16)]
        if more:
            outs += [shape(width, rows, dtype=BF16)] * 2
        made = kernel_call(
            functools.partial(decode_body, layer, len(added), len(links), more, kept is not None),
            outs,
            [],
            [mine, also, dec_cols, *added, *links, *(kept or ())],
            flops=2 * rows * dec_cols.size // layers,
        )
        kept = made[:2]
        if more:
            low = handed_on(made[2])
            rest = kernel_call(
                functools.partial(writes_body, layer, len(links)),
                shape(layers - layer, width, rows, dtype=BF16),
                [],
                [mine, also, dec_cols, made[3], *links],
                flops=2 * rows * dec_cols.size,
            )
    return kept[0].T[None, :, None, :], kept[1][None]


def local(residual_in, attn_scale, mlp_scale, patterns, lengths, value_proj, out_proj, enc_weight, enc_bias, *others):
    whole = (
        residual_in.shape[0] % LANES == 0
        and residual_in.shape[2] % 32 == 0
        and value_proj.shape[3] == out_proj.shape[2]
        and value_proj.shape[3] == 2 * enc_bias.shape[1] == 2 * residual_in.shape[0]
        and residual_in.shape[2] <= residual_in.shape[0] * (2 + lax.axis_size("feat") // 2)
        and lax.axis_size("feat") % 2 == 0
        and lax.axis_size("tok") == lax.axis_size("groups") == 2
    )
    run = tiled if whole else plain
    return run(
        residual_in, attn_scale, mlp_scale, patterns, lengths, value_proj, out_proj, enc_weight, enc_bias, *others
    )


def solution(mesh):
    return jax.shard_map(
        local,
        mesh=mesh,
        in_specs=(
            P("groups", "tok", "feat"),
            P("layer", "groups"),
            P("layer", "groups"),
            P("layer", None, "groups", None, None),
            P("groups"),
            P("layer", "tok", None, "feat"),
            P("layer", None, None, None, "tok", "feat"),
            P("layer", "tok", None, "feat"),
            P("layer", "feat"),
            P("layer", None, None, "tok", "feat"),
            P("layer", "groups", "tok", "feat"),
            P("layer", "feat"),
            P("layer", "feat"),
            P(),
            P("layer", "feat"),
        ),
        out_specs=(P("layer", "groups", "tok", "feat"), P("layer", "groups", "feat")),
        check_vma=False,
    )
```

```python
import functools

import jax
import jax.numpy as jnp
from jax import lax
from jax.experimental import pallas as pl
from jax.experimental.pallas import tpu as pltpu
from jax.sharding import PartitionSpec as P

BF16 = jnp.bfloat16
F32 = jnp.float32


def peers(axis):
    count = lax.axis_size(axis)
    return range(1, count)


def partner(index, step, count):
    if count & (count - 1) == 0:
        return index ^ (count - step)
    return (step - index) % count


def swap(value, axis, step, first_layer=0):
    count = lax.axis_size(axis)
    if first_layer == 0:
        return lax.ppermute(value, axis, [(s, partner(s, step, count)) for s in range(count)])
    layers = lax.axis_size("layer")
    pairs = [
        (s * layers + n, partner(s, step, count) * layers + n)
        for s in range(count)
        for n in range(first_layer, layers)
    ]
    return lax.ppermute(value, (axis, "layer"), pairs)


def spread(value, axis="feat"):
    return [value] + [swap(value, axis, step) for step in peers(axis)]


def spread_any(value):
    return [value] + [swap(value, "feat", step) for step in reversed(peers("feat"))]


def exchange(sends):
    got = {step: swap(sends[step], "feat", step) for step in reversed(peers("feat"))}
    return [sends[0]] + [got[step] for step in peers("feat")]


def total(blocks):
    result = blocks[0].astype(F32)
    for block in blocks[1:]:
        result = result + block.astype(F32)
    return result


def dot_tn(left, right):
    return lax.dot_general(left, right, (((0,), (0,)), ((), ())), preferred_element_type=F32)


def dot_nt(left, right):
    return lax.dot_general(left, right, (((1,), (1,)), ((), ())), preferred_element_type=F32)


def pick(array, index):
    return lax.dynamic_index_in_dim(array, index, 0, keepdims=False)


def redistribute(weight, ranges, my_range, first_layer):
    blocks = weight.reshape(ranges, -1, weight.shape[1])
    got = [pick(blocks, my_range)]
    for step in peers("feat"):
        other = partner(my_range, step, ranges)
        got.append(swap(pick(blocks, other), "feat", step, first_layer))
    got = jnp.stack(got)
    return [pick(got, partner(my_range, n, ranges)) for n in range(ranges)]


def plain(
    residual_in,
    attn_scale,
    mlp_scale,
    patterns,
    lengths,
    value_proj,
    out_proj,
    enc_weight,
    enc_bias,
    dec_weight,
    errors,
    clamp_mode,
    clamp_index,
    clamp_values,
    active_blocks,
):
    layers = lax.axis_size("layer")
    ranges = lax.axis_size("feat")
    my_layer = lax.axis_index("layer")
    my_range = lax.axis_index("feat")
    my_slab = lax.axis_index("tok")
    prompts, seq = patterns.shape[2:4]
    head_dim, per_group = out_proj.shape[2:4]
    kv_cols = value_proj.shape[3]
    half = kv_cols // 2
    width = residual_in.shape[2]
    block_len = enc_bias.shape[1]
    act = block_len * ranges
    rows = residual_in.shape[0]

    source = residual_in[:, 0, :].T
    error_cols = errors[0, :, 0, :].T
    scale_attn = attn_scale[0]
    scale_mlp = mlp_scale[0]

    chosen = active_blocks[0, 0]
    modes = pick(clamp_mode[0].reshape(-1, block_len), chosen)
    entries = pick(clamp_index[0].reshape(-1, block_len), chosen)
    table_ids = jnp.arange(clamp_values.shape[0], dtype=jnp.int32)
    levels = jnp.sum(jnp.where(entries[:, None] == table_ids[None, :], clamp_values[None, :], 0.0), axis=1)
    gain = jnp.where(modes == 1, 0.0, jnp.where(modes == 2, levels, 1.0))
    shift = jnp.where(modes == 1, levels, 0.0)
    mine = jnp.stack([enc_bias[0], gain, shift])
    got = jnp.stack(spread(mine))
    clamp_all = jnp.stack([pick(got, partner(my_range, n, ranges)) for n in range(ranges)], axis=1).reshape(3, act)
    clamp_half = lax.dynamic_slice_in_dim(clamp_all, my_slab * (act // 2), act // 2, 1)

    positions = jnp.arange(seq, dtype=jnp.int32)
    keep = (positions[None, None, :] <= positions[None, :, None]) & (positions[None, None, :] < lengths[:, None, None])
    masked = jnp.where(keep[None], patterns[0], jnp.zeros_like(patterns[0]))
    zero = jnp.zeros_like(masked[:, 0])
    mixing = jnp.concatenate(
        [
            jnp.concatenate([masked[:, p] if q == p else zero for q in range(prompts)], axis=2)
            for p in range(prompts)
        ],
        axis=1,
    ).reshape(-1, per_group * rows, rows)
    live = (positions[None, :] < lengths[:, None]).reshape(rows)

    value_rows = value_proj[0, 0]
    own_value, other_value = (
        lax.dynamic_slice_in_dim(value_rows, n * half, half, 1) for n in (my_slab, 1 - my_slab)
    )
    out_cols = out_proj[0, :, :, :, 0, :].reshape(ranges, 2, half, per_group, width).transpose(1, 0, 4, 3, 2).reshape(2, ranges, width, per_group * half)
    out_own, out_other = (pick(out_cols, n) for n in (my_slab, 1 - my_slab))
    group_of = [n * kv_cols // head_dim for n in range(ranges)]

    enc_blocks = jnp.concatenate(redistribute(enc_weight[0, 0], ranges, my_range, 0), axis=1)
    enc_own, enc_other = (
        lax.dynamic_slice_in_dim(enc_blocks, n * (act // 2), act // 2, 1) for n in (my_slab, 1 - my_slab)
    )
    value_blocks = redistribute(value_rows, ranges, my_range, 1)
    spread_own, spread_other = (
        jnp.concatenate([lax.dynamic_slice_in_dim(b, n * half, half, 1) for b in value_blocks], axis=1)
        for n in (my_slab, 1 - my_slab)
    )
    dec_cols = dec_weight[0, :, :, 0, :].transpose(0, 2, 1)

    def over_slabs(own, other):
        return own + swap(other, "tok", 1).astype(F32)

    def heads(values, group):
        mixed = jnp.dot(mixing[group] if isinstance(group, int) else pick(mixing, group), values, preferred_element_type=F32)
        return mixed.astype(BF16).reshape(per_group, rows, -1).transpose(1, 0, 2).reshape(rows, -1)

    def first_attention(state):
        normed = (state * scale_attn[None, :]).astype(BF16)
        blocks = spread(normed)
        own_rows, other_rows = (w.reshape(ranges, width, half) for w in (own_value, other_value))
        order = [partner(my_range, n, ranges) if n else my_range for n in range(ranges)]
        other = sum(dot_tn(b, pick(other_rows, n)) for b, n in zip(blocks, order))
        own = sum(dot_tn(b, pick(own_rows, n)) for b, n in zip(blocks, order))
        values = over_slabs(own, other).astype(BF16)
        mine = heads(values, my_range * kv_cols // head_dim)
        got = spread(mine)
        also = [swap(b, "tok", 1) for b in got]
        return sum(
            dot_nt(pick(out_own, n), b) + dot_nt(pick(out_other, n), c) for n, b, c in zip(order, got, also)
        )

    def later_attention(state_low):
        other = dot_tn(state_low, spread_other).astype(BF16)
        own = dot_tn(state_low, spread_own)
        part = over_slabs(own, other).astype(BF16)
        mine = (total(spread(part)) * scale_attn[:, None]).astype(BF16)
        also = swap(mine, "tok", 1)
        result = 0.0
        for n in range(ranges):
            cols = slice(n * half, (n + 1) * half)
            result = (
                result
                + dot_nt(out_own[n], heads(mine[:, cols], group_of[n]))
                + dot_nt(out_other[n], heads(also[:, cols], group_of[n]))
            )
        return result

    def code(middle):
        normed = (middle * scale_mlp[None, :]).astype(BF16)
        other = dot_tn(normed, enc_other).astype(BF16)
        own = dot_tn(normed, enc_own)
        part = over_slabs(own, other).astype(BF16)
        preact = total(spread(part)) + clamp_half[0][None, :]
        clamped = jnp.maximum(preact, 0.0) * clamp_half[1][None, :] + clamp_half[2][None, :]
        mine = jnp.where(live[:, None], clamped, 0.0).astype(BF16)
        also = swap(mine, "tok", 1)
        return jnp.concatenate(
            [jnp.where(my_slab == 0, mine, also), jnp.where(my_slab == 0, also, mine)], axis=1
        )

    def handed_on(value, layer):
        return lax.ppermute(value, "layer", [(layer, layer + 1)])

    states = jnp.zeros_like(source)
    feats = jnp.zeros((rows, block_len), BF16)
    state, links = source, None
    for layer in range(layers):
        if layer == 0:
            middle = state + first_attention(state)
        else:
            middle = low.astype(F32) + later_attention(low) + rest.astype(F32)
        kept = code(middle)
        recon = dot_nt(dec_cols[layer], kept)
        base = middle + error_cols
        if layer > 0:
            base = base + links[0]
        state = base + recon
        states = jnp.where(my_layer == layer, state, states)
        feats = jnp.where(
            my_layer == layer, lax.dynamic_slice_in_dim(kept, my_range * block_len, block_len, 1), feats
        )
        if layer + 1 < layers:
            low = state.astype(BF16)
            left = (state - low.astype(F32)).astype(BF16)
            low = handed_on(low, layer)
            writes = jnp.stack([dot_nt(dec_cols[n], kept) for n in range(layer + 1, layers)])
            if layer > 0:
                writes = writes + links[1:]
            rest = handed_on(left, layer)
            links = handed_on(writes, layer)
    return states.T[None, :, None, :], feats[None]


LANES = 128
INFO = 16


def shape(*sizes, dtype=F32):
    return jax.ShapeDtypeStruct(sizes, dtype)


def kernel_call(body, outs, scalars, arrays, left=(), scratch=(), flops=0, room=16 * 1024 * 1024):
    many = isinstance(outs, (list, tuple))
    kept = list(outs) if many else [outs]
    size = sum(a.size * a.dtype.itemsize for a in arrays) + sum(a.size * a.dtype.itemsize for a in kept)
    return pl.pallas_call(
        body,
        out_shape=tuple(kept) if many else outs,
        in_specs=[pl.BlockSpec(memory_space=pltpu.SMEM)] * len(scalars) + [pl.BlockSpec(memory_space=pltpu.VMEM)] * len(arrays) + [pl.BlockSpec(memory_space=pltpu.HBM)] * len(left),
        out_specs=tuple(pl.BlockSpec(memory_space=pltpu.VMEM) for _ in kept) if many else pl.BlockSpec(memory_space=pltpu.VMEM),
        scratch_shapes=list(scratch),
        compiler_params=pltpu.CompilerParams(vmem_limit_bytes=room),
        cost_estimate=pl.CostEstimate(flops=int(flops), bytes_accessed=int(size), transcendentals=0),
    )(*scalars, *arrays, *left)


def place_of():
    return [lax.axis_index(axis) for axis in ("feat", "tok", "layer", "groups")]


def split_terms(value):
    high = value.astype(BF16)
    left = value - high.astype(F32)
    middle = left.astype(BF16)
    low = (left - middle.astype(F32)).astype(BF16)
    return [high, middle, low]


def facts_body(lengths, chosen, table, mode, index, bias, scale, patterns, info, mixing, scales, lives):
    block = chosen[0, 0]
    modes = mode[pl.ds(block, 1), :]
    entries = index[pl.ds(block, 1), :]
    levels = jnp.zeros(entries.shape, F32)
    for n in range(table.shape[0]):
        levels = jnp.where(entries == n, table[n], levels)
    gain = jnp.where(modes == 1, 0.0, jnp.where(modes == 2, levels, 1.0))
    shift = jnp.where(modes == 1, levels, 0.0)
    terms = [t.astype(F32) for v in (bias[...], gain, shift) for t in split_terms(v)]
    info[...] = jnp.concatenate(terms + [jnp.zeros((INFO - len(terms), bias.shape[1]), F32)], axis=0).astype(BF16)
    heads, prompts, seq, _ = patterns.shape
    query = lax.broadcasted_iota(jnp.int32, (seq, seq), 0)
    key = lax.broadcasted_iota(jnp.int32, (seq, seq), 1)
    for p in range(prompts):
        keep = (key <= query) & (key < lengths[p])
        for head in range(heads):
            pattern = jnp.where(keep, patterns[head, p].astype(F32), 0.0)
            zero = jnp.zeros_like(pattern)
            row = jnp.concatenate([pattern if q == p else zero for q in range(prompts)], axis=1)
            mixing[head, p * seq : (p + 1) * seq, :] = row.astype(BF16)
    rows = scale.shape[1]
    scales[...] = jnp.broadcast_to(scale[...], (rows, rows)).T
    row = lax.broadcasted_iota(jnp.int32, lives.shape, 0)
    end = jnp.full(row.shape, lengths[0], jnp.int32)
    for p in range(1, prompts):
        end = jnp.where(row >= p * seq, p * seq + lengths[p], end)
    lives[...] = jnp.where(row < end, 1.0, 0.0)


def start_body(ranges, state, weight, enc, *refs):
    place = place_of()
    sends, sems = (None, *refs[-2::-1]), refs[-1]
    width, rows = state.shape
    part = width // 2
    low = state[...].astype(BF16)

    def copies(source, first, size, at, group):
        made = []
        for step in range(1, ranges):
            start = pl.multiple_of(partner(place[0], step, ranges) * width + first, 16)
            made.append(
                pltpu.make_async_copy(
                    source.at[pl.ds(start, size), pl.ds(0, rows)],
                    sends[step].at[pl.ds(at, size)],
                    sems.at[group, step - 1],
                )
            )
        return made

    rest = copies(enc, place[3] * part, part, width, 0)
    for copy in rest:
        copy.start()

    @pl.when(place[2] == 0)
    def _():
        for send in sends[1:]:
            send[0:width] = low

    @pl.when(place[2] > 0)
    def _():
        carried = copies(weight, 0, width, 0, 1)
        for copy in carried:
            copy.start()
        for copy in carried:
            copy.wait()

    for copy in rest:
        copy.wait()


def carry(place, ranges, weight, width, first, count, made, sends):
    rows, half = made[0].shape
    for n, block in enumerate(made):
        sends[0][n * rows : (n + 1) * rows] = block
    for step in range(1, ranges):
        other = partner(place[0], step, ranges)
        for n, block in enumerate(made):
            at, size = n * rows, min(max(count - n * rows, 0), rows)
            if size > 0:
                start = pl.multiple_of(other * width + first + at, 16)
                carried = weight[pl.ds(start, size), half:]
                sends[step][at : at + size] = jnp.where(place[2] == 0, block[0:size], carried)
            if size < rows:
                sends[step][at + size : at + rows] = block[size:]


def values_body(ranges, *refs):
    blocks, (weight, own, passed) = refs[:ranges], refs[ranges:]
    width = passed.shape[0] // (ranges - 1) * 2
    place = place_of()
    acc = None
    for step, block in enumerate(blocks):
        n = partner(place[0], step, ranges) if step else place[0]
        if step:
            size = block.shape[0] - width
            passed[(step - 1) * size : step * size] = block[width:]
        part = dot_tn(block[0:width].astype(BF16), weight[pl.ds(pl.multiple_of(n * width, 16), width), :])
        acc = part if acc is None else acc + part
    own[...] = acc


def mix(mixing, head, values):
    return jnp.dot(mixing[head], values, preferred_element_type=F32).astype(BF16)


def whole_values_body(ranges, width, own, got, scales, weight, *sends):
    place = place_of()
    rows, half = scales.shape
    made = [
        ((own[:, n * half : (n + 1) * half] + got[:, n * half : (n + 1) * half]) * scales[...]).astype(BF16)
        for n in range(2)
    ]
    sends = (sends[0], *sends[:0:-1])
    carry(place, ranges, weight, width, 0, 2 * rows, made, sends)


def sums_body(ranges, width, done, own, got, weight, info, *sends):
    place = place_of()
    made = [(own[n] + got[n].astype(F32)).astype(BF16) for n in range(own.shape[0])]
    sends = (sends[0], *sends[:0:-1])
    carry(place, ranges, weight, width, done, width - done, made, sends)
    for send in sends:
        send[send.shape[0] - INFO :] = info[...]


def halves_of(first, mine, theirs):
    return jnp.concatenate([jnp.where(first, mine, theirs), jnp.where(first, theirs, mine)], axis=1)


def spread_values_body(ranges, carried, low, weight, *refs):
    place = place_of()
    others = ranges - 1
    firsts, seconds, thirds = (refs[i * others : (i + 1) * others] for i in range(3))
    own, other = refs[3 * others :]
    width, rows = low.shape
    first = place[1] == 0
    state = low[...]
    for step in range(ranges):
        if step == 0:
            n = place[0]
            both = dot_tn(state, weight[pl.ds(pl.multiple_of(n * width, 16), width), :])
            even, odd = both[:, : own.shape[2]], both[:, own.shape[2] :]
        else:
            n = partner(place[0], step, ranges)
            even = dot_tn(state, firsts[step - 1][0:width])
            odd, at = None, 0
            for piece in (seconds[step - 1], thirds[step - 1]):
                size = min(carried, width - at)
                part = dot_tn(state[at : at + size], piece[0:size])
                odd = part if odd is None else odd + part
                at += size
        own[n] = jnp.where(first, even, odd)
        other[n] = jnp.where(first, odd, even).astype(BF16)


def scaled_body(scales, *refs):
    *blocks, out = refs
    for n in range(out.shape[0]):
        out[n] = (total([b[n] for b in blocks]) * scales[...]).astype(BF16)


def finish(ranges, place, acc, blocks, passed, enc, weight_scale, middle, own, other, parts):
    width = middle.shape[0]
    size = width // 2
    middle[...] = acc
    normed = (acc * weight_scale[...]).astype(BF16)
    here = place[3] == 0
    mine = jnp.where(here, normed[:size], normed[size:])
    theirs = jnp.where(here, normed[size:], normed[:size])
    parts[place[0]] = dot_tn(normed, enc[pl.ds(pl.multiple_of(place[0] * width, 16), width), :])
    for step in range(1, ranges):
        parts[partner(place[0], step, ranges)] = dot_tn(mine, blocks[step - 1][width:]) + dot_tn(
            theirs, passed[(step - 1) * size : step * size]
        )
    share = ranges // 2
    own[...] = parts[pl.ds(place[1] * share, share)]
    other[...] = parts[pl.ds((1 - place[1]) * share, share)].astype(BF16)


def first_code_body(ranges, per_group, *refs):
    place = place_of()
    got, blocks = refs[:ranges], refs[ranges : 2 * ranges - 1]
    passed, state, mixing, weight, *ends = refs[2 * ranges - 1 :]
    rows = state.shape[1]
    acc = state[...]
    for step in range(ranges):
        n = partner(place[0], step, ranges) if step else place[0]
        values = jnp.concatenate([got[step][0:rows], got[step][rows:]], axis=1)
        for u in range(per_group):
            acc = acc + dot_nt(weight[n * per_group + u], mix(mixing, n * per_group + u, values))
    finish(ranges, place, acc, blocks, passed, *ends)


def later_code_body(ranges, per_group, mine, also, low, rest, mixing, *refs):
    place = place_of()
    blocks = refs[: ranges - 1]
    passed, weight, *ends = refs[ranges - 1 :]
    first = place[1] == 0
    acc = low[...].astype(F32) + rest[0].astype(F32)
    for n in range(ranges):
        values = halves_of(first, mine[n], also[n])
        for u in range(per_group):
            acc = acc + dot_nt(weight[n * per_group + u], mix(mixing, n * per_group + u, values))
    finish(ranges, place, acc, blocks, passed, *ends)


def clamp_body(*refs):
    place = place_of()
    *refs, lives, out = refs
    blocks, facts = refs[: len(refs) // 2], refs[len(refs) // 2 :]
    share, rows, _ = out.shape
    ranges = len(blocks)
    live = lives[...] > 0.5
    terms = [f[f.shape[0] - INFO :].astype(F32) for f in facts]
    terms = [
        [t[3 * i : 3 * i + 1] + t[3 * i + 1 : 3 * i + 2] + t[3 * i + 2 : 3 * i + 3] for i in range(3)] for t in terms
    ]
    for n in range(share):
        number = place[1] * share + n
        bias, gain, shift = terms[0]
        for step in range(1, ranges):
            here = partner(place[0], step, ranges) == number
            bias, gain, shift = (jnp.where(here, b, a) for a, b in zip((bias, gain, shift), terms[step]))
        preact = total([b[n * rows : (n + 1) * rows] for b in blocks]) + bias
        clamped = jnp.maximum(preact, 0.0) * gain + shift
        out[n] = jnp.where(live, clamped, 0.0).astype(BF16)


def ordered(place, mine, also):
    first = place[1] == 0
    share = mine.shape[0]
    return [jnp.where(first, mine[n], also[n]) for n in range(share)] + [
        jnp.where(first, also[n], mine[n]) for n in range(share)
    ]


def decode_body(layer, adds, linked, sends, keeps, *refs):
    place = place_of()
    refs = list(refs)
    take = lambda count: [refs.pop(0) for _ in range(count)]
    (mine, also, dec), added, links, before = take(3), take(adds), take(linked), take(2 if keeps else 0)
    state_out, feats_out = take(2)
    feats = ordered(place, mine, also)
    acc = added[0][...]
    for piece in added[1:]:
        acc = acc + piece[...]
    for piece in links:
        acc = acc + piece[1].astype(F32)
    acc = acc + dot_nt(dec[layer], jnp.concatenate(feats, axis=1))
    block = feats[0]
    for n in range(1, len(feats)):
        block = jnp.where(place[0] == n, feats[n], block)
    if sends:
        low = acc.astype(BF16)
        refs[0][...] = low
        refs[1][...] = (acc - low.astype(F32)).astype(BF16)
    if keeps:
        here = place[2] == layer
        state_out[...] = jnp.where(here, acc, before[0][...])
        feats_out[...] = jnp.where(here, block, before[1][...])
    else:
        state_out[...] = acc
        feats_out[...] = block


def writes_body(layer, linked, mine, also, dec, left, *refs):
    place = place_of()
    out = refs[-1]
    feats = jnp.concatenate(ordered(place, mine, also), axis=1)
    out[0] = left[...]
    for n in range(1, out.shape[0]):
        made = dot_nt(dec[layer + n], feats)
        out[n] = (made + refs[0][n + 1].astype(F32) if linked else made).astype(BF16)


def after(value, *others):
    return lax.optimization_barrier((value, *others))[0]


def tiled(
    residual_in,
    attn_scale,
    mlp_scale,
    patterns,
    lengths,
    value_proj,
    out_proj,
    enc_weight,
    enc_bias,
    dec_weight,
    errors,
    clamp_mode,
    clamp_index,
    clamp_values,
    active_blocks,
):
    layers = lax.axis_size("layer")
    ranges = lax.axis_size("feat")
    seq = patterns.shape[3]
    head_dim, per_group = out_proj.shape[2:4]
    kv_cols = value_proj.shape[3]
    half = kv_cols // 2
    width = residual_in.shape[2]
    block_len = enc_bias.shape[1]
    rows = residual_in.shape[0]
    share = ranges // 2

    source = residual_in[:, 0, :].T
    error_cols = errors[0, :, 0, :].T
    out_weight = out_proj[0, :, :, :, 0, :].transpose(0, 2, 3, 1).reshape(-1, width, head_dim)
    dec_cols = dec_weight[0, :, :, 0, :].transpose(0, 2, 1)
    value_rows = value_proj[0, 0]
    enc_rows = enc_weight[0, 0]

    def handed_on(value):
        return lax.ppermute(value, "layer", [(n, (n + 1) % layers) for n in range(layers)])

    packed = carried = rest = low = kept = None
    for layer in range(layers):
        if layer == 0:
            sends = kernel_call(
                functools.partial(start_body, ranges),
                [shape(width + width // 2, rows, dtype=BF16)] * (ranges - 1),
                [],
                [source],
                left=[value_rows, enc_rows],
                scratch=[pltpu.SemaphoreType.DMA((2, ranges - 1))],
                room=60 * 1024 * 1024,
            )
            blocks = exchange([source, *sends[::-1]])
            info, mixing, scales, live = kernel_call(
                facts_body,
                [
                    shape(INFO, block_len, dtype=BF16),
                    shape(patterns.shape[1], rows, rows, dtype=BF16),
                    shape(rows, half),
                    shape(rows, block_len),
                ],
                [lengths, active_blocks, clamp_values],
                [
                    clamp_mode.reshape(-1, block_len),
                    clamp_index.reshape(-1, block_len),
                    enc_bias,
                    attn_scale,
                    patterns[0],
                ],
            )
            blocks[1], info, mixing, scales, live = lax.optimization_barrier((blocks[1], info, mixing, scales, live))
            own, passed = kernel_call(
                functools.partial(values_body, ranges),
                [shape(rows, kv_cols), shape((ranges - 1) * (width // 2), rows, dtype=BF16)],
                [],
                [*blocks, value_rows],
                flops=4 * rows * value_rows.size,
            )
            got = swap(own, "tok", 1)
            passed = swap(passed, "groups", 1)
            packed = [*blocks[1:], passed]
            sends = kernel_call(
                functools.partial(whole_values_body, ranges, width),
                [shape(2 * rows, half, dtype=BF16)] * ranges,
                [],
                [own, got, scales, value_rows],
            )
            got = exchange([sends[0], *sends[:0:-1]])
            carried = [*blocks[1:], *got[1:]]
            code = functools.partial(first_code_body, ranges, per_group)
            given = [*got, *packed, source, mixing]
        else:
            own, other = kernel_call(
                functools.partial(spread_values_body, ranges, 2 * rows),
                [shape(ranges, rows, half), shape(ranges, rows, half, dtype=BF16)],
                [],
                [low, value_rows, *carried],
                flops=2 * rows * value_rows.size,
            )
            part = (own + swap(other, "tok", 1).astype(F32)).astype(BF16)
            blocks = spread_any(part)
            rest = handed_on(after(rest, low))
            mine = kernel_call(scaled_body, shape(ranges, rows, half, dtype=BF16), [], [scales, *blocks])
            code = functools.partial(later_code_body, ranges, per_group)
            scalars, given = [], [mine, swap(mine, "tok", 1), low, rest, mixing, *packed]
        middle, own, other = kernel_call(
            code,
            [
                shape(width, rows),
                shape(share, rows, block_len),
                shape(share, rows, block_len, dtype=BF16),
            ],
            [],
            [*given, out_weight, enc_rows, mlp_scale],
            scratch=[pltpu.VMEM((ranges, rows, block_len), F32)],
            flops=2 * rows * (out_weight.size + width * block_len * ranges),
        )
        got = swap(other, "tok", 1)
        if layer == 0:
            sends = kernel_call(
                functools.partial(sums_body, ranges, width, 2 * rows),
                [shape(share * rows + INFO, block_len, dtype=BF16)] * ranges,
                [],
                [own, got, value_rows, info],
            )
            blocks = facts = exchange([sends[0], *sends[:0:-1]])
            carried += blocks[1:]
        else:
            blocks = spread_any((own + got.astype(F32)).astype(BF16).reshape(-1, block_len))
        mine = kernel_call(
            clamp_body,
            shape(share, rows, block_len, dtype=BF16),
            [],
            [*blocks, *facts, live],
        )
        also = swap(mine, "tok", 1)
        more = layer + 1 < layers
        added = [middle, error_cols]
        links = [rest] if layer > 0 else []
        outs = [shape(width, rows), shape(rows, block_len, dtype=BF16)]
        if more:
            outs += [shape(width, rows, dtype=BF16)] * 2
        made = kernel_call(
            functools.partial(decode_body, layer, len(added), len(links), more, kept is not None),
            outs,
            [],
            [mine, also, dec_cols, *added, *links, *(kept or ())],
            flops=2 * rows * dec_cols.size // layers,
        )
        kept = made[:2]
        if more:
            low = handed_on(made[2])
            rest = kernel_call(
                functools.partial(writes_body, layer, len(links)),
                shape(layers - layer, width, rows, dtype=BF16),
                [],
                [mine, also, dec_cols, made[3], *links],
                flops=2 * rows * dec_cols.size,
            )
    return kept[0].T[None, :, None, :], kept[1][None]


def local(residual_in, attn_scale, mlp_scale, patterns, lengths, value_proj, out_proj, enc_weight, enc_bias, *others):
    whole = (
        residual_in.shape[0] % LANES == 0
        and residual_in.shape[2] % 32 == 0
        and value_proj.shape[3] == out_proj.shape[2]
        and value_proj.shape[3] == 2 * enc_bias.shape[1] == 2 * residual_in.shape[0]
        and residual_in.shape[2] <= residual_in.shape[0] * (2 + lax.axis_size("feat") // 2)
        and lax.axis_size("feat") % 2 == 0
        and lax.axis_size("tok") == lax.axis_size("groups") == 2
    )
    run = tiled if whole else plain
    return run(
        residual_in, attn_scale, mlp_scale, patterns, lengths, value_proj, out_proj, enc_weight, enc_bias, *others
    )


def solution(mesh):
    return jax.shard_map(
        local,
        mesh=mesh,
        in_specs=(
            P("groups", "tok", "feat"),
            P("layer", "groups"),
            P("layer", "groups"),
            P("layer", None, "groups", None, None),
            P("groups"),
            P("layer", "tok", None, "feat"),
            P("layer", None, None, None, "tok", "feat"),
            P("layer", "tok", None, "feat"),
            P("layer", "feat"),
            P("layer", None, None, "tok", "feat"),
            P("layer", "groups", "tok", "feat"),
            P("layer", "feat"),
            P("layer", "feat"),
            P(),
            P("layer", "feat"),
        ),
        out_specs=(P("layer", "groups", "tok", "feat"), P("layer", "groups", "feat")),
        check_vma=False,
    )
```

```python
import functools

import jax
import jax.numpy as jnp
from jax import lax
from jax.experimental import pallas as pl
from jax.experimental.pallas import tpu as pltpu
from jax.sharding import PartitionSpec as P

BF16 = jnp.bfloat16
F32 = jnp.float32


def peers(axis):
    count = lax.axis_size(axis)
    return range(1, count)


def partner(index, step, count):
    if count & (count - 1) == 0:
        return index ^ (count - step)
    return (step - index) % count


def swap(value, axis, step, first_layer=0):
    count = lax.axis_size(axis)
    if first_layer == 0:
        return lax.ppermute(value, axis, [(s, partner(s, step, count)) for s in range(count)])
    layers = lax.axis_size("layer")
    pairs = [
        (s * layers + n, partner(s, step, count) * layers + n)
        for s in range(count)
        for n in range(first_layer, layers)
    ]
    return lax.ppermute(value, (axis, "layer"), pairs)


def spread(value, axis="feat"):
    return [value] + [swap(value, axis, step) for step in peers(axis)]


def spread_any(value):
    return [value] + [swap(value, "feat", step) for step in reversed(peers("feat"))]


def exchange(sends):
    got = {step: swap(sends[step], "feat", step) for step in reversed(peers("feat"))}
    return [sends[0]] + [got[step] for step in peers("feat")]


def total(blocks):
    result = blocks[0].astype(F32)
    for block in blocks[1:]:
        result = result + block.astype(F32)
    return result


def dot_tn(left, right):
    return lax.dot_general(left, right, (((0,), (0,)), ((), ())), preferred_element_type=F32)


def dot_nt(left, right):
    return lax.dot_general(left, right, (((1,), (1,)), ((), ())), preferred_element_type=F32)


def pick(array, index):
    return lax.dynamic_index_in_dim(array, index, 0, keepdims=False)


def redistribute(weight, ranges, my_range, first_layer):
    blocks = weight.reshape(ranges, -1, weight.shape[1])
    got = [pick(blocks, my_range)]
    for step in peers("feat"):
        other = partner(my_range, step, ranges)
        got.append(swap(pick(blocks, other), "feat", step, first_layer))
    got = jnp.stack(got)
    return [pick(got, partner(my_range, n, ranges)) for n in range(ranges)]


def plain(
    residual_in,
    attn_scale,
    mlp_scale,
    patterns,
    lengths,
    value_proj,
    out_proj,
    enc_weight,
    enc_bias,
    dec_weight,
    errors,
    clamp_mode,
    clamp_index,
    clamp_values,
    active_blocks,
):
    layers = lax.axis_size("layer")
    ranges = lax.axis_size("feat")
    my_layer = lax.axis_index("layer")
    my_range = lax.axis_index("feat")
    my_slab = lax.axis_index("tok")
    prompts, seq = patterns.shape[2:4]
    head_dim, per_group = out_proj.shape[2:4]
    kv_cols = value_proj.shape[3]
    half = kv_cols // 2
    width = residual_in.shape[2]
    block_len = enc_bias.shape[1]
    act = block_len * ranges
    rows = residual_in.shape[0]

    source = residual_in[:, 0, :].T
    error_cols = errors[0, :, 0, :].T
    scale_attn = attn_scale[0]
    scale_mlp = mlp_scale[0]

    chosen = active_blocks[0, 0]
    modes = pick(clamp_mode[0].reshape(-1, block_len), chosen)
    entries = pick(clamp_index[0].reshape(-1, block_len), chosen)
    table_ids = jnp.arange(clamp_values.shape[0], dtype=jnp.int32)
    levels = jnp.sum(jnp.where(entries[:, None] == table_ids[None, :], clamp_values[None, :], 0.0), axis=1)
    gain = jnp.where(modes == 1, 0.0, jnp.where(modes == 2, levels, 1.0))
    shift = jnp.where(modes == 1, levels, 0.0)
    mine = jnp.stack([enc_bias[0], gain, shift])
    got = jnp.stack(spread(mine))
    clamp_all = jnp.stack([pick(got, partner(my_range, n, ranges)) for n in range(ranges)], axis=1).reshape(3, act)
    clamp_half = lax.dynamic_slice_in_dim(clamp_all, my_slab * (act // 2), act // 2, 1)

    positions = jnp.arange(seq, dtype=jnp.int32)
    keep = (positions[None, None, :] <= positions[None, :, None]) & (positions[None, None, :] < lengths[:, None, None])
    masked = jnp.where(keep[None], patterns[0], jnp.zeros_like(patterns[0]))
    zero = jnp.zeros_like(masked[:, 0])
    mixing = jnp.concatenate(
        [
            jnp.concatenate([masked[:, p] if q == p else zero for q in range(prompts)], axis=2)
            for p in range(prompts)
        ],
        axis=1,
    ).reshape(-1, per_group * rows, rows)
    live = (positions[None, :] < lengths[:, None]).reshape(rows)

    value_rows = value_proj[0, 0]
    own_value, other_value = (
        lax.dynamic_slice_in_dim(value_rows, n * half, half, 1) for n in (my_slab, 1 - my_slab)
    )
    out_cols = out_proj[0, :, :, :, 0, :].reshape(ranges, 2, half, per_group, width).transpose(1, 0, 4, 3, 2).reshape(2, ranges, width, per_group * half)
    out_own, out_other = (pick(out_cols, n) for n in (my_slab, 1 - my_slab))
    group_of = [n * kv_cols // head_dim for n in range(ranges)]

    enc_blocks = jnp.concatenate(redistribute(enc_weight[0, 0], ranges, my_range, 0), axis=1)
    enc_own, enc_other = (
        lax.dynamic_slice_in_dim(enc_blocks, n * (act // 2), act // 2, 1) for n in (my_slab, 1 - my_slab)
    )
    value_blocks = redistribute(value_rows, ranges, my_range, 1)
    spread_own, spread_other = (
        jnp.concatenate([lax.dynamic_slice_in_dim(b, n * half, half, 1) for b in value_blocks], axis=1)
        for n in (my_slab, 1 - my_slab)
    )
    dec_cols = dec_weight[0, :, :, 0, :].transpose(0, 2, 1)

    def over_slabs(own, other):
        return own + swap(other, "tok", 1).astype(F32)

    def heads(values, group):
        mixed = jnp.dot(mixing[group] if isinstance(group, int) else pick(mixing, group), values, preferred_element_type=F32)
        return mixed.astype(BF16).reshape(per_group, rows, -1).transpose(1, 0, 2).reshape(rows, -1)

    def first_attention(state):
        normed = (state * scale_attn[None, :]).astype(BF16)
        blocks = spread(normed)
        own_rows, other_rows = (w.reshape(ranges, width, half) for w in (own_value, other_value))
        order = [partner(my_range, n, ranges) if n else my_range for n in range(ranges)]
        other = sum(dot_tn(b, pick(other_rows, n)) for b, n in zip(blocks, order))
        own = sum(dot_tn(b, pick(own_rows, n)) for b, n in zip(blocks, order))
        values = over_slabs(own, other).astype(BF16)
        mine = heads(values, my_range * kv_cols // head_dim)
        got = spread(mine)
        also = [swap(b, "tok", 1) for b in got]
        return sum(
            dot_nt(pick(out_own, n), b) + dot_nt(pick(out_other, n), c) for n, b, c in zip(order, got, also)
        )

    def later_attention(state_low):
        other = dot_tn(state_low, spread_other).astype(BF16)
        own = dot_tn(state_low, spread_own)
        part = over_slabs(own, other).astype(BF16)
        mine = (total(spread(part)) * scale_attn[:, None]).astype(BF16)
        also = swap(mine, "tok", 1)
        result = 0.0
        for n in range(ranges):
            cols = slice(n * half, (n + 1) * half)
            result = (
                result
                + dot_nt(out_own[n], heads(mine[:, cols], group_of[n]))
                + dot_nt(out_other[n], heads(also[:, cols], group_of[n]))
            )
        return result

    def code(middle):
        normed = (middle * scale_mlp[None, :]).astype(BF16)
        other = dot_tn(normed, enc_other).astype(BF16)
        own = dot_tn(normed, enc_own)
        part = over_slabs(own, other).astype(BF16)
        preact = total(spread(part)) + clamp_half[0][None, :]
        clamped = jnp.maximum(preact, 0.0) * clamp_half[1][None, :] + clamp_half[2][None, :]
        mine = jnp.where(live[:, None], clamped, 0.0).astype(BF16)
        also = swap(mine, "tok", 1)
        return jnp.concatenate(
            [jnp.where(my_slab == 0, mine, also), jnp.where(my_slab == 0, also, mine)], axis=1
        )

    def handed_on(value, layer):
        return lax.ppermute(value, "layer", [(layer, layer + 1)])

    states = jnp.zeros_like(source)
    feats = jnp.zeros((rows, block_len), BF16)
    state, links = source, None
    for layer in range(layers):
        if layer == 0:
            middle = state + first_attention(state)
        else:
            middle = low.astype(F32) + later_attention(low) + rest.astype(F32)
        kept = code(middle)
        recon = dot_nt(dec_cols[layer], kept)
        base = middle + error_cols
        if layer > 0:
            base = base + links[0]
        state = base + recon
        states = jnp.where(my_layer == layer, state, states)
        feats = jnp.where(
            my_layer == layer, lax.dynamic_slice_in_dim(kept, my_range * block_len, block_len, 1), feats
        )
        if layer + 1 < layers:
            low = state.astype(BF16)
            left = (state - low.astype(F32)).astype(BF16)
            low = handed_on(low, layer)
            writes = jnp.stack([dot_nt(dec_cols[n], kept) for n in range(layer + 1, layers)])
            if layer > 0:
                writes = writes + links[1:]
            rest = handed_on(left, layer)
            links = handed_on(writes, layer)
    return states.T[None, :, None, :], feats[None]


LANES = 128
INFO = 16


def shape(*sizes, dtype=F32):
    return jax.ShapeDtypeStruct(sizes, dtype)


def kernel_call(body, outs, scalars, arrays, scratch=(), flops=0):
    many = isinstance(outs, (list, tuple))
    kept = list(outs) if many else [outs]
    size = sum(a.size * a.dtype.itemsize for a in arrays) + sum(a.size * a.dtype.itemsize for a in kept)
    return pl.pallas_call(
        body,
        out_shape=tuple(kept) if many else outs,
        in_specs=[pl.BlockSpec(memory_space=pltpu.SMEM)] * len(scalars) + [pl.BlockSpec(memory_space=pltpu.VMEM)] * len(arrays),
        out_specs=tuple(pl.BlockSpec(memory_space=pltpu.VMEM) for _ in kept) if many else pl.BlockSpec(memory_space=pltpu.VMEM),
        scratch_shapes=list(scratch),
        compiler_params=pltpu.CompilerParams(vmem_limit_bytes=16 * 1024 * 1024),
        cost_estimate=pl.CostEstimate(flops=int(flops), bytes_accessed=int(size), transcendentals=0),
    )(*scalars, *arrays)


def place_of():
    return [lax.axis_index(axis) for axis in ("feat", "tok", "layer", "groups")]


def split_terms(value):
    high = value.astype(BF16)
    left = value - high.astype(F32)
    middle = left.astype(BF16)
    low = (left - middle.astype(F32)).astype(BF16)
    return [high, middle, low]


def facts_body(lengths, chosen, table, mode, index, bias, scale, patterns, info, mixing, scales, lives):
    block = chosen[0, 0]
    modes = mode[pl.ds(block, 1), :]
    entries = index[pl.ds(block, 1), :]
    levels = jnp.zeros(entries.shape, F32)
    for n in range(table.shape[0]):
        levels = jnp.where(entries == n, table[n], levels)
    gain = jnp.where(modes == 1, 0.0, jnp.where(modes == 2, levels, 1.0))
    shift = jnp.where(modes == 1, levels, 0.0)
    terms = [t.astype(F32) for v in (bias[...], gain, shift) for t in split_terms(v)]
    info[...] = jnp.concatenate(terms + [jnp.zeros((INFO - len(terms), bias.shape[1]), F32)], axis=0).astype(BF16)
    heads, prompts, seq, _ = patterns.shape
    query = lax.broadcasted_iota(jnp.int32, (seq, seq), 0)
    key = lax.broadcasted_iota(jnp.int32, (seq, seq), 1)
    for p in range(prompts):
        keep = (key <= query) & (key < lengths[p])
        for head in range(heads):
            pattern = jnp.where(keep, patterns[head, p].astype(F32), 0.0)
            zero = jnp.zeros_like(pattern)
            row = jnp.concatenate([pattern if q == p else zero for q in range(prompts)], axis=1)
            mixing[head, p * seq : (p + 1) * seq, :] = row.astype(BF16)
    rows = scale.shape[1]
    scales[...] = jnp.broadcast_to(scale[...], (rows, rows)).T
    row = lax.broadcasted_iota(jnp.int32, lives.shape, 0)
    end = jnp.full(row.shape, lengths[0], jnp.int32)
    for p in range(1, prompts):
        end = jnp.where(row >= p * seq, p * seq + lengths[p], end)
    lives[...] = jnp.where(row < end, 1.0, 0.0)


def start_body(ranges, state, weight, enc, *refs):
    place = place_of()
    sends, (wide, load_sem, sems) = refs[: ranges - 1], refs[ranges - 1 :]
    width, rows = state.shape
    part = width // 2

    def copies(source, first, count, at, group):
        made = []
        for step in range(1, ranges):
            start = pl.multiple_of(partner(place[0], step, ranges) * width + first, 16)
            made.append(
                pltpu.make_async_copy(
                    source.at[pl.ds(start, count), pl.ds(0, rows)],
                    sends[step - 1].at[pl.ds(at, count)],
                    sems.at[group, step - 1],
                )
            )
        return made

    load = pltpu.make_async_copy(state, wide, load_sem)
    rest = copies(enc, place[3] * part, part, width, 0)
    carried = copies(weight, 0, width, 0, 1)

    @pl.when(place[2] == 0)
    def _():
        load.start()
        for copy in rest:
            copy.start()
        load.wait()
        low = wide[...].astype(BF16)
        for send in sends:
            send[0:width] = low
        for copy in rest:
            copy.wait()

    @pl.when(place[2] > 0)
    def _():
        for copy in carried + rest:
            copy.start()
        for copy in carried + rest:
            copy.wait()


def carry(place, ranges, weight, width, first, count, made, sends):
    rows, half = made[0].shape
    for n, block in enumerate(made):
        sends[0][n * rows : (n + 1) * rows] = block
    for step in range(1, ranges):
        other = partner(place[0], step, ranges)
        for n, block in enumerate(made):
            at, size = n * rows, min(max(count - n * rows, 0), rows)
            if size > 0:
                start = pl.multiple_of(other * width + first + at, 16)
                carried = weight[pl.ds(start, size), half:]
                sends[step][at : at + size] = jnp.where(place[2] == 0, block[0:size], carried)
            if size < rows:
                sends[step][at + size : at + rows] = block[size:]


def values_body(ranges, *refs):
    blocks, (weight, own, passed) = refs[:ranges], refs[ranges:]
    width = passed.shape[0] // (ranges - 1) * 2
    place = place_of()
    acc = None
    for step, block in enumerate(blocks):
        n = partner(place[0], step, ranges) if step else place[0]
        if step:
            size = block.shape[0] - width
            passed[(step - 1) * size : step * size] = block[width:]
        part = dot_tn(block[0:width].astype(BF16), weight[pl.ds(pl.multiple_of(n * width, 16), width), :])
        acc = part if acc is None else acc + part
    own[...] = acc


def mix(mixing, head, values):
    return jnp.dot(mixing[head], values, preferred_element_type=F32).astype(BF16)


def whole_values_body(ranges, width, own, got, scales, weight, *sends):
    place = place_of()
    rows, half = scales.shape
    made = [
        ((own[:, n * half : (n + 1) * half] + got[:, n * half : (n + 1) * half]) * scales[...]).astype(BF16)
        for n in range(2)
    ]
    sends = (sends[0], *sends[:0:-1])
    carry(place, ranges, weight, width, 0, 2 * rows, made, sends)


def sums_body(ranges, width, done, own, got, weight, info, *sends):
    place = place_of()
    made = [(own[n] + got[n].astype(F32)).astype(BF16) for n in range(own.shape[0])]
    sends = (sends[0], *sends[:0:-1])
    carry(place, ranges, weight, width, done, width - done, made, sends)
    for send in sends:
        send[send.shape[0] - INFO :] = info[...]


def halves_of(first, mine, theirs):
    return jnp.concatenate([jnp.where(first, mine, theirs), jnp.where(first, theirs, mine)], axis=1)


def spread_values_body(ranges, carried, low, weight, *refs):
    place = place_of()
    others = ranges - 1
    firsts, seconds, thirds = (refs[i * others : (i + 1) * others] for i in range(3))
    own, other = refs[3 * others :]
    width, rows = low.shape
    first = place[1] == 0
    state = low[...]
    for step in range(ranges):
        if step == 0:
            n = place[0]
            both = dot_tn(state, weight[pl.ds(pl.multiple_of(n * width, 16), width), :])
            even, odd = both[:, : own.shape[2]], both[:, own.shape[2] :]
        else:
            n = partner(place[0], step, ranges)
            even = dot_tn(state, firsts[step - 1][0:width])
            odd, at = None, 0
            for piece in (seconds[step - 1], thirds[step - 1]):
                size = min(carried, width - at)
                part = dot_tn(state[at : at + size], piece[0:size])
                odd = part if odd is None else odd + part
                at += size
        own[n] = jnp.where(first, even, odd)
        other[n] = jnp.where(first, odd, even).astype(BF16)


def scaled_body(scales, *refs):
    *blocks, out = refs
    for n in range(out.shape[0]):
        out[n] = (total([b[n] for b in blocks]) * scales[...]).astype(BF16)


def finish(ranges, place, acc, blocks, passed, enc, weight_scale, middle, own, other, parts):
    width = middle.shape[0]
    size = width // 2
    middle[...] = acc
    normed = (acc * weight_scale[...]).astype(BF16)
    here = place[3] == 0
    mine = jnp.where(here, normed[:size], normed[size:])
    theirs = jnp.where(here, normed[size:], normed[:size])
    parts[place[0]] = dot_tn(normed, enc[pl.ds(pl.multiple_of(place[0] * width, 16), width), :])
    for step in range(1, ranges):
        parts[partner(place[0], step, ranges)] = dot_tn(mine, blocks[step - 1][width:]) + dot_tn(
            theirs, passed[(step - 1) * size : step * size]
        )
    share = ranges // 2
    own[...] = parts[pl.ds(place[1] * share, share)]
    other[...] = parts[pl.ds((1 - place[1]) * share, share)].astype(BF16)


def first_code_body(ranges, per_group, *refs):
    place = place_of()
    got, blocks = refs[:ranges], refs[ranges : 2 * ranges - 1]
    passed, state, mixing, weight, *ends = refs[2 * ranges - 1 :]
    rows = state.shape[1]
    acc = state[...]
    for step in range(ranges):
        n = partner(place[0], step, ranges) if step else place[0]
        values = jnp.concatenate([got[step][0:rows], got[step][rows:]], axis=1)
        for u in range(per_group):
            acc = acc + dot_nt(weight[n * per_group + u], mix(mixing, n * per_group + u, values))
    finish(ranges, place, acc, blocks, passed, *ends)


def later_code_body(ranges, per_group, mine, also, low, rest, mixing, *refs):
    place = place_of()
    blocks = refs[: ranges - 1]
    passed, weight, *ends = refs[ranges - 1 :]
    first = place[1] == 0
    acc = low[...].astype(F32) + rest[0].astype(F32)
    for n in range(ranges):
        values = halves_of(first, mine[n], also[n])
        for u in range(per_group):
            acc = acc + dot_nt(weight[n * per_group + u], mix(mixing, n * per_group + u, values))
    finish(ranges, place, acc, blocks, passed, *ends)


def clamp_body(*refs):
    place = place_of()
    *refs, lives, out = refs
    blocks, facts = refs[: len(refs) // 2], refs[len(refs) // 2 :]
    share, rows, _ = out.shape
    ranges = len(blocks)
    live = lives[...] > 0.5
    terms = [f[f.shape[0] - INFO :].astype(F32) for f in facts]
    terms = [
        [t[3 * i : 3 * i + 1] + t[3 * i + 1 : 3 * i + 2] + t[3 * i + 2 : 3 * i + 3] for i in range(3)] for t in terms
    ]
    for n in range(share):
        number = place[1] * share + n
        bias, gain, shift = terms[0]
        for step in range(1, ranges):
            here = partner(place[0], step, ranges) == number
            bias, gain, shift = (jnp.where(here, b, a) for a, b in zip((bias, gain, shift), terms[step]))
        preact = total([b[n * rows : (n + 1) * rows] for b in blocks]) + bias
        clamped = jnp.maximum(preact, 0.0) * gain + shift
        out[n] = jnp.where(live, clamped, 0.0).astype(BF16)


def ordered(place, mine, also):
    first = place[1] == 0
    share = mine.shape[0]
    return [jnp.where(first, mine[n], also[n]) for n in range(share)] + [
        jnp.where(first, also[n], mine[n]) for n in range(share)
    ]


def decode_body(layer, adds, linked, sends, keeps, *refs):
    place = place_of()
    refs = list(refs)
    take = lambda count: [refs.pop(0) for _ in range(count)]
    (mine, also, dec), added, links, before = take(3), take(adds), take(linked), take(2 if keeps else 0)
    state_out, feats_out = take(2)
    feats = ordered(place, mine, also)
    acc = added[0][...]
    for piece in added[1:]:
        acc = acc + piece[...]
    for piece in links:
        acc = acc + piece[1].astype(F32)
    acc = acc + dot_nt(dec[layer], jnp.concatenate(feats, axis=1))
    block = feats[0]
    for n in range(1, len(feats)):
        block = jnp.where(place[0] == n, feats[n], block)
    if sends:
        low = acc.astype(BF16)
        refs[0][...] = low
        refs[1][...] = (acc - low.astype(F32)).astype(BF16)
    if keeps:
        here = place[2] == layer
        state_out[...] = jnp.where(here, acc, before[0][...])
        feats_out[...] = jnp.where(here, block, before[1][...])
    else:
        state_out[...] = acc
        feats_out[...] = block


def writes_body(layer, linked, mine, also, dec, left, *refs):
    place = place_of()
    out = refs[-1]
    feats = jnp.concatenate(ordered(place, mine, also), axis=1)
    out[0] = left[...]
    for n in range(1, out.shape[0]):
        made = dot_nt(dec[layer + n], feats)
        out[n] = (made + refs[0][n + 1].astype(F32) if linked else made).astype(BF16)


def after(value, *others):
    return lax.optimization_barrier((value, *others))[0]


def tiled(
    residual_in,
    attn_scale,
    mlp_scale,
    patterns,
    lengths,
    value_proj,
    out_proj,
    enc_weight,
    enc_bias,
    dec_weight,
    errors,
    clamp_mode,
    clamp_index,
    clamp_values,
    active_blocks,
):
    layers = lax.axis_size("layer")
    ranges = lax.axis_size("feat")
    seq = patterns.shape[3]
    head_dim, per_group = out_proj.shape[2:4]
    kv_cols = value_proj.shape[3]
    half = kv_cols // 2
    width = residual_in.shape[2]
    block_len = enc_bias.shape[1]
    rows = residual_in.shape[0]
    share = ranges // 2

    source = residual_in[:, 0, :].T
    error_cols = errors[0, :, 0, :].T
    out_weight = out_proj[0, :, :, :, 0, :].transpose(0, 2, 3, 1).reshape(-1, width, head_dim)
    dec_cols = dec_weight[0, :, :, 0, :].transpose(0, 2, 1)
    value_rows = value_proj[0, 0]
    enc_rows = enc_weight[0, 0]

    def handed_on(value):
        return lax.ppermute(value, "layer", [(n, (n + 1) % layers) for n in range(layers)])

    packed = carried = rest = low = kept = None
    for layer in range(layers):
        if layer == 0:
            sends = pl.pallas_call(
                functools.partial(start_body, ranges),
                out_shape=(shape(width + width // 2, rows, dtype=BF16),) * (ranges - 1),
                in_specs=[pl.BlockSpec(memory_space=pltpu.HBM)] * 3,
                out_specs=(pl.BlockSpec(memory_space=pltpu.VMEM),) * (ranges - 1),
                scratch_shapes=[
                    pltpu.VMEM((width, rows), F32),
                    pltpu.SemaphoreType.DMA,
                    pltpu.SemaphoreType.DMA((2, ranges - 1)),
                ],
                compiler_params=pltpu.CompilerParams(vmem_limit_bytes=60 * 1024 * 1024),
            )(source, value_rows, enc_rows)
            blocks = exchange([source, *sends])
            info, mixing, scales, live = kernel_call(
                facts_body,
                [
                    shape(INFO, block_len, dtype=BF16),
                    shape(patterns.shape[1], rows, rows, dtype=BF16),
                    shape(rows, half),
                    shape(rows, block_len),
                ],
                [lengths, active_blocks, clamp_values],
                [
                    clamp_mode.reshape(-1, block_len),
                    clamp_index.reshape(-1, block_len),
                    enc_bias,
                    attn_scale,
                    patterns[0],
                ],
            )
            blocks[1], info, mixing, scales, live = lax.optimization_barrier((blocks[1], info, mixing, scales, live))
            own, passed = kernel_call(
                functools.partial(values_body, ranges),
                [shape(rows, kv_cols), shape((ranges - 1) * (width // 2), rows, dtype=BF16)],
                [],
                [*blocks, value_rows],
                flops=4 * rows * value_rows.size,
            )
            got = swap(own, "tok", 1)
            passed = swap(passed, "groups", 1)
            packed = [*blocks[1:], passed]
            sends = kernel_call(
                functools.partial(whole_values_body, ranges, width),
                [shape(2 * rows, half, dtype=BF16)] * ranges,
                [],
                [own, got, scales, value_rows],
            )
            got = exchange([sends[0], *sends[:0:-1]])
            carried = [*blocks[1:], *got[1:]]
            code = functools.partial(first_code_body, ranges, per_group)
            given = [*got, *packed, source, mixing]
        else:
            own, other = kernel_call(
                functools.partial(spread_values_body, ranges, 2 * rows),
                [shape(ranges, rows, half), shape(ranges, rows, half, dtype=BF16)],
                [],
                [low, value_rows, *carried],
                flops=2 * rows * value_rows.size,
            )
            part = (own + swap(other, "tok", 1).astype(F32)).astype(BF16)
            blocks = spread_any(part)
            rest = handed_on(after(rest, low))
            mine = kernel_call(scaled_body, shape(ranges, rows, half, dtype=BF16), [], [scales, *blocks])
            code = functools.partial(later_code_body, ranges, per_group)
            scalars, given = [], [mine, swap(mine, "tok", 1), low, rest, mixing, *packed]
        middle, own, other = kernel_call(
            code,
            [
                shape(width, rows),
                shape(share, rows, block_len),
                shape(share, rows, block_len, dtype=BF16),
            ],
            [],
            [*given, out_weight, enc_rows, mlp_scale],
            scratch=[pltpu.VMEM((ranges, rows, block_len), F32)],
            flops=2 * rows * (out_weight.size + width * block_len * ranges),
        )
        got = swap(other, "tok", 1)
        if layer == 0:
            sends = kernel_call(
                functools.partial(sums_body, ranges, width, 2 * rows),
                [shape(share * rows + INFO, block_len, dtype=BF16)] * ranges,
                [],
                [own, got, value_rows, info],
            )
            blocks = facts = exchange([sends[0], *sends[:0:-1]])
            carried += blocks[1:]
        else:
            blocks = spread_any((own + got.astype(F32)).astype(BF16).reshape(-1, block_len))
        mine = kernel_call(
            clamp_body,
            shape(share, rows, block_len, dtype=BF16),
            [],
            [*blocks, *facts, live],
        )
        also = swap(mine, "tok", 1)
        more = layer + 1 < layers
        added = [middle, error_cols]
        links = [rest] if layer > 0 else []
        outs = [shape(width, rows), shape(rows, block_len, dtype=BF16)]
        if more:
            outs += [shape(width, rows, dtype=BF16)] * 2
        made = kernel_call(
            functools.partial(decode_body, layer, len(added), len(links), more, kept is not None),
            outs,
            [],
            [mine, also, dec_cols, *added, *links, *(kept or ())],
            flops=2 * rows * dec_cols.size // layers,
        )
        kept = made[:2]
        if more:
            low = handed_on(made[2])
            rest = kernel_call(
                functools.partial(writes_body, layer, len(links)),
                shape(layers - layer, width, rows, dtype=BF16),
                [],
                [mine, also, dec_cols, made[3], *links],
                flops=2 * rows * dec_cols.size,
            )
    return kept[0].T[None, :, None, :], kept[1][None]


def local(residual_in, attn_scale, mlp_scale, patterns, lengths, value_proj, out_proj, enc_weight, enc_bias, *others):
    whole = (
        residual_in.shape[0] % LANES == 0
        and residual_in.shape[2] % 32 == 0
        and value_proj.shape[3] == out_proj.shape[2]
        and value_proj.shape[3] == 2 * enc_bias.shape[1] == 2 * residual_in.shape[0]
        and residual_in.shape[2] <= residual_in.shape[0] * (2 + lax.axis_size("feat") // 2)
        and lax.axis_size("feat") % 2 == 0
        and lax.axis_size("tok") == lax.axis_size("groups") == 2
    )
    run = tiled if whole else plain
    return run(
        residual_in, attn_scale, mlp_scale, patterns, lengths, value_proj, out_proj, enc_weight, enc_bias, *others
    )


def solution(mesh):
    return jax.shard_map(
        local,
        mesh=mesh,
        in_specs=(
            P("groups", "tok", "feat"),
            P("layer", "groups"),
            P("layer", "groups"),
            P("layer", None, "groups", None, None),
            P("groups"),
            P("layer", "tok", None, "feat"),
            P("layer", None, None, None, "tok", "feat"),
            P("layer", "tok", None, "feat"),
            P("layer", "feat"),
            P("layer", None, None, "tok", "feat"),
            P("layer", "groups", "tok", "feat"),
            P("layer", "feat"),
            P("layer", "feat"),
            P(),
            P("layer", "feat"),
        ),
        out_specs=(P("layer", "groups", "tok", "feat"), P("layer", "groups", "feat")),
        check_vma=False,
    )
```

```python
import functools

import jax
import jax.numpy as jnp
from jax import lax
from jax.experimental import pallas as pl
from jax.experimental.pallas import tpu as pltpu
from jax.sharding import PartitionSpec as P

BF16 = jnp.bfloat16
F32 = jnp.float32


def peers(axis):
    count = lax.axis_size(axis)
    return range(1, count)


def partner(index, step, count):
    if count & (count - 1) == 0:
        return index ^ (count - step)
    return (step - index) % count


def swap(value, axis, step, first_layer=0):
    count = lax.axis_size(axis)
    if first_layer == 0:
        return lax.ppermute(value, axis, [(s, partner(s, step, count)) for s in range(count)])
    layers = lax.axis_size("layer")
    pairs = [
        (s * layers + n, partner(s, step, count) * layers + n)
        for s in range(count)
        for n in range(first_layer, layers)
    ]
    return lax.ppermute(value, (axis, "layer"), pairs)


def spread(value, axis="feat"):
    return [value] + [swap(value, axis, step) for step in peers(axis)]


def spread_any(value):
    return [value] + [swap(value, "feat", step) for step in reversed(peers("feat"))]


def halving(pairs):
    count = lax.axis_size("feat")
    bits = [1 << n for n in range(count.bit_length() - 1)]
    for near, far in zip(bits, reversed(bits)):
        sums = [(a.astype(F32) + b.astype(F32)).astype(BF16) for a, b in pairs]
        got = [swap(value, "feat", count - bit) for value, bit in zip(sums, (near, far))]
        pairs = list(zip(sums, got))
    return pairs


def exchange(sends):
    got = {step: swap(sends[step], "feat", step) for step in reversed(peers("feat"))}
    return [sends[0]] + [got[step] for step in peers("feat")]


def total(blocks):
    result = blocks[0].astype(F32)
    for block in blocks[1:]:
        result = result + block.astype(F32)
    return result


def dot_tn(left, right):
    return lax.dot_general(left, right, (((0,), (0,)), ((), ())), preferred_element_type=F32)


def dot_nt(left, right):
    return lax.dot_general(left, right, (((1,), (1,)), ((), ())), preferred_element_type=F32)


def pick(array, index):
    return lax.dynamic_index_in_dim(array, index, 0, keepdims=False)


def redistribute(weight, ranges, my_range, first_layer):
    blocks = weight.reshape(ranges, -1, weight.shape[1])
    got = [pick(blocks, my_range)]
    for step in peers("feat"):
        other = partner(my_range, step, ranges)
        got.append(swap(pick(blocks, other), "feat", step, first_layer))
    got = jnp.stack(got)
    return [pick(got, partner(my_range, n, ranges)) for n in range(ranges)]


def plain(
    residual_in,
    attn_scale,
    mlp_scale,
    patterns,
    lengths,
    value_proj,
    out_proj,
    enc_weight,
    enc_bias,
    dec_weight,
    errors,
    clamp_mode,
    clamp_index,
    clamp_values,
    active_blocks,
):
    layers = lax.axis_size("layer")
    ranges = lax.axis_size("feat")
    my_layer = lax.axis_index("layer")
    my_range = lax.axis_index("feat")
    my_slab = lax.axis_index("tok")
    prompts, seq = patterns.shape[2:4]
    head_dim, per_group = out_proj.shape[2:4]
    kv_cols = value_proj.shape[3]
    half = kv_cols // 2
    width = residual_in.shape[2]
    block_len = enc_bias.shape[1]
    act = block_len * ranges
    rows = residual_in.shape[0]

    source = residual_in[:, 0, :].T
    error_cols = errors[0, :, 0, :].T
    scale_attn = attn_scale[0]
    scale_mlp = mlp_scale[0]

    chosen = active_blocks[0, 0]
    modes = pick(clamp_mode[0].reshape(-1, block_len), chosen)
    entries = pick(clamp_index[0].reshape(-1, block_len), chosen)
    table_ids = jnp.arange(clamp_values.shape[0], dtype=jnp.int32)
    levels = jnp.sum(jnp.where(entries[:, None] == table_ids[None, :], clamp_values[None, :], 0.0), axis=1)
    gain = jnp.where(modes == 1, 0.0, jnp.where(modes == 2, levels, 1.0))
    shift = jnp.where(modes == 1, levels, 0.0)
    mine = jnp.stack([enc_bias[0], gain, shift])
    got = jnp.stack(spread(mine))
    clamp_all = jnp.stack([pick(got, partner(my_range, n, ranges)) for n in range(ranges)], axis=1).reshape(3, act)
    clamp_half = lax.dynamic_slice_in_dim(clamp_all, my_slab * (act // 2), act // 2, 1)

    positions = jnp.arange(seq, dtype=jnp.int32)
    keep = (positions[None, None, :] <= positions[None, :, None]) & (positions[None, None, :] < lengths[:, None, None])
    masked = jnp.where(keep[None], patterns[0], jnp.zeros_like(patterns[0]))
    zero = jnp.zeros_like(masked[:, 0])
    mixing = jnp.concatenate(
        [
            jnp.concatenate([masked[:, p] if q == p else zero for q in range(prompts)], axis=2)
            for p in range(prompts)
        ],
        axis=1,
    ).reshape(-1, per_group * rows, rows)
    live = (positions[None, :] < lengths[:, None]).reshape(rows)

    value_rows = value_proj[0, 0]
    own_value, other_value = (
        lax.dynamic_slice_in_dim(value_rows, n * half, half, 1) for n in (my_slab, 1 - my_slab)
    )
    out_cols = out_proj[0, :, :, :, 0, :].reshape(ranges, 2, half, per_group, width).transpose(1, 0, 4, 3, 2).reshape(2, ranges, width, per_group * half)
    out_own, out_other = (pick(out_cols, n) for n in (my_slab, 1 - my_slab))
    group_of = [n * kv_cols // head_dim for n in range(ranges)]

    enc_blocks = jnp.concatenate(redistribute(enc_weight[0, 0], ranges, my_range, 0), axis=1)
    enc_own, enc_other = (
        lax.dynamic_slice_in_dim(enc_blocks, n * (act // 2), act // 2, 1) for n in (my_slab, 1 - my_slab)
    )
    value_blocks = redistribute(value_rows, ranges, my_range, 1)
    spread_own, spread_other = (
        jnp.concatenate([lax.dynamic_slice_in_dim(b, n * half, half, 1) for b in value_blocks], axis=1)
        for n in (my_slab, 1 - my_slab)
    )
    dec_cols = dec_weight[0, :, :, 0, :].transpose(0, 2, 1)

    def over_slabs(own, other):
        return own + swap(other, "tok", 1).astype(F32)

    def heads(values, group):
        mixed = jnp.dot(mixing[group] if isinstance(group, int) else pick(mixing, group), values, preferred_element_type=F32)
        return mixed.astype(BF16).reshape(per_group, rows, -1).transpose(1, 0, 2).reshape(rows, -1)

    def first_attention(state):
        normed = (state * scale_attn[None, :]).astype(BF16)
        blocks = spread(normed)
        own_rows, other_rows = (w.reshape(ranges, width, half) for w in (own_value, other_value))
        order = [partner(my_range, n, ranges) if n else my_range for n in range(ranges)]
        other = sum(dot_tn(b, pick(other_rows, n)) for b, n in zip(blocks, order))
        own = sum(dot_tn(b, pick(own_rows, n)) for b, n in zip(blocks, order))
        values = over_slabs(own, other).astype(BF16)
        mine = heads(values, my_range * kv_cols // head_dim)
        got = spread(mine)
        also = [swap(b, "tok", 1) for b in got]
        return sum(
            dot_nt(pick(out_own, n), b) + dot_nt(pick(out_other, n), c) for n, b, c in zip(order, got, also)
        )

    def later_attention(state_low):
        other = dot_tn(state_low, spread_other).astype(BF16)
        own = dot_tn(state_low, spread_own)
        part = over_slabs(own, other).astype(BF16)
        mine = (total(spread(part)) * scale_attn[:, None]).astype(BF16)
        also = swap(mine, "tok", 1)
        result = 0.0
        for n in range(ranges):
            cols = slice(n * half, (n + 1) * half)
            result = (
                result
                + dot_nt(out_own[n], heads(mine[:, cols], group_of[n]))
                + dot_nt(out_other[n], heads(also[:, cols], group_of[n]))
            )
        return result

    def code(middle):
        normed = (middle * scale_mlp[None, :]).astype(BF16)
        other = dot_tn(normed, enc_other).astype(BF16)
        own = dot_tn(normed, enc_own)
        part = over_slabs(own, other).astype(BF16)
        preact = total(spread(part)) + clamp_half[0][None, :]
        clamped = jnp.maximum(preact, 0.0) * clamp_half[1][None, :] + clamp_half[2][None, :]
        mine = jnp.where(live[:, None], clamped, 0.0).astype(BF16)
        also = swap(mine, "tok", 1)
        return jnp.concatenate(
            [jnp.where(my_slab == 0, mine, also), jnp.where(my_slab == 0, also, mine)], axis=1
        )

    def handed_on(value, layer):
        return lax.ppermute(value, "layer", [(layer, layer + 1)])

    states = jnp.zeros_like(source)
    feats = jnp.zeros((rows, block_len), BF16)
    state, links = source, None
    for layer in range(layers):
        if layer == 0:
            middle = state + first_attention(state)
        else:
            middle = low.astype(F32) + later_attention(low) + rest.astype(F32)
        kept = code(middle)
        recon = dot_nt(dec_cols[layer], kept)
        base = middle + error_cols
        if layer > 0:
            base = base + links[0]
        state = base + recon
        states = jnp.where(my_layer == layer, state, states)
        feats = jnp.where(
            my_layer == layer, lax.dynamic_slice_in_dim(kept, my_range * block_len, block_len, 1), feats
        )
        if layer + 1 < layers:
            low = state.astype(BF16)
            left = (state - low.astype(F32)).astype(BF16)
            low = handed_on(low, layer)
            writes = jnp.stack([dot_nt(dec_cols[n], kept) for n in range(layer + 1, layers)])
            if layer > 0:
                writes = writes + links[1:]
            rest = handed_on(left, layer)
            links = handed_on(writes, layer)
    return states.T[None, :, None, :], feats[None]


LANES = 128
INFO = 16


def shape(*sizes, dtype=F32):
    return jax.ShapeDtypeStruct(sizes, dtype)


def kernel_call(body, outs, scalars, arrays, scratch=(), flops=0):
    many = isinstance(outs, (list, tuple))
    kept = list(outs) if many else [outs]
    size = sum(a.size * a.dtype.itemsize for a in arrays) + sum(a.size * a.dtype.itemsize for a in kept)
    return pl.pallas_call(
        body,
        out_shape=tuple(kept) if many else outs,
        in_specs=[pl.BlockSpec(memory_space=pltpu.SMEM)] * len(scalars) + [pl.BlockSpec(memory_space=pltpu.VMEM)] * len(arrays),
        out_specs=tuple(pl.BlockSpec(memory_space=pltpu.VMEM) for _ in kept) if many else pl.BlockSpec(memory_space=pltpu.VMEM),
        scratch_shapes=list(scratch),
        compiler_params=pltpu.CompilerParams(vmem_limit_bytes=16 * 1024 * 1024),
        cost_estimate=pl.CostEstimate(flops=int(flops), bytes_accessed=int(size), transcendentals=0),
    )(*scalars, *arrays)


def place_of():
    return [lax.axis_index(axis) for axis in ("feat", "tok", "layer", "groups")]


def split_terms(value):
    high = value.astype(BF16)
    left = value - high.astype(F32)
    middle = left.astype(BF16)
    low = (left - middle.astype(F32)).astype(BF16)
    return [high, middle, low]


def facts_body(lengths, chosen, table, mode, index, bias, scale, patterns, info, mixing, scales, lives):
    block = chosen[0, 0]
    modes = mode[pl.ds(block, 1), :]
    entries = index[pl.ds(block, 1), :]
    levels = jnp.zeros(entries.shape, F32)
    for n in range(table.shape[0]):
        levels = jnp.where(entries == n, table[n], levels)
    gain = jnp.where(modes == 1, 0.0, jnp.where(modes == 2, levels, 1.0))
    shift = jnp.where(modes == 1, levels, 0.0)
    terms = [t.astype(F32) for v in (bias[...], gain, shift) for t in split_terms(v)]
    info[...] = jnp.concatenate(terms + [jnp.zeros((INFO - len(terms), bias.shape[1]), F32)], axis=0).astype(BF16)
    heads, prompts, seq, _ = patterns.shape
    query = lax.broadcasted_iota(jnp.int32, (seq, seq), 0)
    key = lax.broadcasted_iota(jnp.int32, (seq, seq), 1)
    for p in range(prompts):
        keep = (key <= query) & (key < lengths[p])
        for head in range(heads):
            pattern = jnp.where(keep, patterns[head, p].astype(F32), 0.0)
            zero = jnp.zeros_like(pattern)
            row = jnp.concatenate([pattern if q == p else zero for q in range(prompts)], axis=1)
            mixing[head, p * seq : (p + 1) * seq, :] = row.astype(BF16)
    rows = scale.shape[1]
    scales[...] = jnp.broadcast_to(scale[...], (rows, rows)).T
    row = lax.broadcasted_iota(jnp.int32, lives.shape, 0)
    end = jnp.full(row.shape, lengths[0], jnp.int32)
    for p in range(1, prompts):
        end = jnp.where(row >= p * seq, p * seq + lengths[p], end)
    lives[...] = jnp.where(row < end, 1.0, 0.0)


def start_body(ranges, state, weight, enc, *refs):
    place = place_of()
    sends, (wide, load_sem, sems) = refs[: ranges - 1], refs[ranges - 1 :]
    width, rows = state.shape
    part = width // 2

    def copies(source, first, count, at, group):
        made = []
        for step in range(1, ranges):
            start = pl.multiple_of(partner(place[0], step, ranges) * width + first, 16)
            made.append(
                pltpu.make_async_copy(
                    source.at[pl.ds(start, count), pl.ds(0, rows)],
                    sends[step - 1].at[pl.ds(at, count)],
                    sems.at[group, step - 1],
                )
            )
        return made

    load = pltpu.make_async_copy(state, wide, load_sem)
    rest = copies(enc, place[3] * part, part, width, 0)
    carried = copies(weight, 0, width, 0, 1)

    @pl.when(place[2] == 0)
    def _():
        load.start()
        for copy in rest:
            copy.start()
        load.wait()
        low = wide[...].astype(BF16)
        for send in sends:
            send[0:width] = low
        for copy in rest:
            copy.wait()

    @pl.when(place[2] > 0)
    def _():
        for copy in carried + rest:
            copy.start()
        for copy in carried + rest:
            copy.wait()


def carry(place, ranges, weight, width, first, count, made, sends):
    rows, half = made[0].shape
    for n, block in enumerate(made):
        sends[0][n * rows : (n + 1) * rows] = block
    for step in range(1, ranges):
        other = partner(place[0], step, ranges)
        for n, block in enumerate(made):
            at, size = n * rows, min(max(count - n * rows, 0), rows)
            if size > 0:
                start = pl.multiple_of(other * width + first + at, 16)
                carried = weight[pl.ds(start, size), half:]
                sends[step][at : at + size] = jnp.where(place[2] == 0, block[0:size], carried)
            if size < rows:
                sends[step][at + size : at + rows] = block[size:]


def values_body(ranges, *refs):
    blocks, (weight, own, passed) = refs[:ranges], refs[ranges:]
    width = passed.shape[0] // (ranges - 1) * 2
    place = place_of()
    acc = None
    for step, block in enumerate(blocks):
        n = partner(place[0], step, ranges) if step else place[0]
        if step:
            size = block.shape[0] - width
            passed[(step - 1) * size : step * size] = block[width:]
        part = dot_tn(block[0:width].astype(BF16), weight[pl.ds(pl.multiple_of(n * width, 16), width), :])
        acc = part if acc is None else acc + part
    own[...] = acc


def mix(mixing, head, values):
    return jnp.dot(mixing[head], values, preferred_element_type=F32).astype(BF16)


def whole_values_body(ranges, width, own, got, scales, weight, *sends):
    place = place_of()
    rows, half = scales.shape
    made = [
        ((own[:, n * half : (n + 1) * half] + got[:, n * half : (n + 1) * half]) * scales[...]).astype(BF16)
        for n in range(2)
    ]
    sends = (sends[0], *sends[:0:-1])
    carry(place, ranges, weight, width, 0, 2 * rows, made, sends)


def sums_body(ranges, width, done, own, got, weight, info, *sends):
    place = place_of()
    made = [(own[n] + got[n].astype(F32)).astype(BF16) for n in range(own.shape[0])]
    sends = (sends[0], *sends[:0:-1])
    carry(place, ranges, weight, width, done, width - done, made, sends)
    for send in sends:
        send[send.shape[0] - INFO :] = info[...]


def halves_of(first, mine, theirs):
    return jnp.concatenate([jnp.where(first, mine, theirs), jnp.where(first, theirs, mine)], axis=1)


def spread_values_body(ranges, carried, low, weight, *refs):
    place = place_of()
    others = ranges - 1
    firsts, seconds, thirds = (refs[i * others : (i + 1) * others] for i in range(3))
    own, other = refs[3 * others :]
    width, rows = low.shape
    first = place[1] == 0
    state = low[...]
    for step in range(ranges):
        if step == 0:
            n = place[0]
            both = dot_tn(state, weight[pl.ds(pl.multiple_of(n * width, 16), width), :])
            even, odd = both[:, : own.shape[2]], both[:, own.shape[2] :]
        else:
            n = partner(place[0], step, ranges)
            even = dot_tn(state, firsts[step - 1][0:width])
            odd, at = None, 0
            for piece in (seconds[step - 1], thirds[step - 1]):
                size = min(carried, width - at)
                part = dot_tn(state[at : at + size], piece[0:size])
                odd = part if odd is None else odd + part
                at += size
        own[n] = jnp.where(first, even, odd)
        other[n] = jnp.where(first, odd, even).astype(BF16)


def scaled_body(scales, even, even_got, odd, odd_got, out):
    count = even.shape[0]
    for at, pair in ((0, (even, even_got)), (count, (odd, odd_got))):
        for n in range(count):
            out[at + n] = (total([b[n] for b in pair]) * scales[...]).astype(BF16)


def finish(ranges, place, acc, blocks, passed, enc, weight_scale, middle, own, other, parts):
    width = middle.shape[0]
    size = width // 2
    middle[...] = acc
    normed = (acc * weight_scale[...]).astype(BF16)
    here = place[3] == 0
    mine = jnp.where(here, normed[:size], normed[size:])
    theirs = jnp.where(here, normed[size:], normed[:size])
    parts[place[0]] = dot_tn(normed, enc[pl.ds(pl.multiple_of(place[0] * width, 16), width), :])
    for step in range(1, ranges):
        parts[partner(place[0], step, ranges)] = dot_tn(mine, blocks[step - 1][width:]) + dot_tn(
            theirs, passed[(step - 1) * size : step * size]
        )
    share = ranges // 2
    own[...] = parts[pl.ds(place[1] * share, share)]
    other[...] = parts[pl.ds((1 - place[1]) * share, share)].astype(BF16)


def first_code_body(ranges, per_group, *refs):
    place = place_of()
    got, blocks = refs[:ranges], refs[ranges : 2 * ranges - 1]
    passed, state, mixing, weight, *ends = refs[2 * ranges - 1 :]
    rows = state.shape[1]
    acc = state[...]
    for step in range(ranges):
        n = partner(place[0], step, ranges) if step else place[0]
        values = jnp.concatenate([got[step][0:rows], got[step][rows:]], axis=1)
        for u in range(per_group):
            acc = acc + dot_nt(weight[n * per_group + u], mix(mixing, n * per_group + u, values))
    finish(ranges, place, acc, blocks, passed, *ends)


def later_code_body(ranges, per_group, mine, also, low, rest, mixing, *refs):
    place = place_of()
    blocks = refs[: ranges - 1]
    passed, weight, *ends = refs[ranges - 1 :]
    first = place[1] == 0
    acc = low[...].astype(F32) + rest[0].astype(F32)
    for n in range(ranges):
        values = halves_of(first, mine[n], also[n])
        for u in range(per_group):
            acc = acc + dot_nt(weight[n * per_group + u], mix(mixing, n * per_group + u, values))
    finish(ranges, place, acc, blocks, passed, *ends)


def clamp_body(*refs):
    place = place_of()
    *refs, lives, out = refs
    blocks, facts = refs[: len(refs) // 2], refs[len(refs) // 2 :]
    share, rows, _ = out.shape
    ranges = len(blocks)
    live = lives[...] > 0.5
    terms = [f[f.shape[0] - INFO :].astype(F32) for f in facts]
    terms = [
        [t[3 * i : 3 * i + 1] + t[3 * i + 1 : 3 * i + 2] + t[3 * i + 2 : 3 * i + 3] for i in range(3)] for t in terms
    ]
    for n in range(share):
        number = place[1] * share + n
        bias, gain, shift = terms[0]
        for step in range(1, ranges):
            here = partner(place[0], step, ranges) == number
            bias, gain, shift = (jnp.where(here, b, a) for a, b in zip((bias, gain, shift), terms[step]))
        preact = total([b[n * rows : (n + 1) * rows] for b in blocks]) + bias
        clamped = jnp.maximum(preact, 0.0) * gain + shift
        out[n] = jnp.where(live, clamped, 0.0).astype(BF16)


def ordered(place, mine, also):
    first = place[1] == 0
    share = mine.shape[0]
    return [jnp.where(first, mine[n], also[n]) for n in range(share)] + [
        jnp.where(first, also[n], mine[n]) for n in range(share)
    ]


def decode_body(layer, adds, linked, sends, keeps, *refs):
    place = place_of()
    refs = list(refs)
    take = lambda count: [refs.pop(0) for _ in range(count)]
    (mine, also, dec), added, links, before = take(3), take(adds), take(linked), take(2 if keeps else 0)
    state_out, feats_out = take(2)
    feats = ordered(place, mine, also)
    acc = added[0][...]
    for piece in added[1:]:
        acc = acc + piece[...]
    for piece in links:
        acc = acc + piece[1].astype(F32)
    acc = acc + dot_nt(dec[layer], jnp.concatenate(feats, axis=1))
    block = feats[0]
    for n in range(1, len(feats)):
        block = jnp.where(place[0] == n, feats[n], block)
    if sends:
        low = acc.astype(BF16)
        refs[0][...] = low
        refs[1][...] = (acc - low.astype(F32)).astype(BF16)
    if keeps:
        here = place[2] == layer
        state_out[...] = jnp.where(here, acc, before[0][...])
        feats_out[...] = jnp.where(here, block, before[1][...])
    else:
        state_out[...] = acc
        feats_out[...] = block


def writes_body(layer, linked, mine, also, dec, left, *refs):
    place = place_of()
    out = refs[-1]
    feats = jnp.concatenate(ordered(place, mine, also), axis=1)
    out[0] = left[...]
    for n in range(1, out.shape[0]):
        made = dot_nt(dec[layer + n], feats)
        out[n] = (made + refs[0][n + 1].astype(F32) if linked else made).astype(BF16)


def after(value, *others):
    return lax.optimization_barrier((value, *others))[0]


def tiled(
    residual_in,
    attn_scale,
    mlp_scale,
    patterns,
    lengths,
    value_proj,
    out_proj,
    enc_weight,
    enc_bias,
    dec_weight,
    errors,
    clamp_mode,
    clamp_index,
    clamp_values,
    active_blocks,
):
    layers = lax.axis_size("layer")
    ranges = lax.axis_size("feat")
    seq = patterns.shape[3]
    head_dim, per_group = out_proj.shape[2:4]
    kv_cols = value_proj.shape[3]
    half = kv_cols // 2
    width = residual_in.shape[2]
    block_len = enc_bias.shape[1]
    rows = residual_in.shape[0]
    share = ranges // 2

    source = residual_in[:, 0, :].T
    error_cols = errors[0, :, 0, :].T
    out_weight = out_proj[0, :, :, :, 0, :].transpose(0, 2, 3, 1).reshape(-1, width, head_dim)
    dec_cols = dec_weight[0, :, :, 0, :].transpose(0, 2, 1)
    value_rows = value_proj[0, 0]
    enc_rows = enc_weight[0, 0]

    def handed_on(value):
        return lax.ppermute(value, "layer", [(n, (n + 1) % layers) for n in range(layers)])

    packed = carried = rest = low = kept = None
    for layer in range(layers):
        if layer == 0:
            sends = pl.pallas_call(
                functools.partial(start_body, ranges),
                out_shape=(shape(width + width // 2, rows, dtype=BF16),) * (ranges - 1),
                in_specs=[pl.BlockSpec(memory_space=pltpu.HBM)] * 3,
                out_specs=(pl.BlockSpec(memory_space=pltpu.VMEM),) * (ranges - 1),
                scratch_shapes=[
                    pltpu.VMEM((width, rows), F32),
                    pltpu.SemaphoreType.DMA,
                    pltpu.SemaphoreType.DMA((2, ranges - 1)),
                ],
                compiler_params=pltpu.CompilerParams(vmem_limit_bytes=60 * 1024 * 1024),
            )(source, value_rows, enc_rows)
            blocks = exchange([source, *sends])
            info, mixing, scales, live = kernel_call(
                facts_body,
                [
                    shape(INFO, block_len, dtype=BF16),
                    shape(patterns.shape[1], rows, rows, dtype=BF16),
                    shape(rows, half),
                    shape(rows, block_len),
                ],
                [lengths, active_blocks, clamp_values],
                [
                    clamp_mode.reshape(-1, block_len),
                    clamp_index.reshape(-1, block_len),
                    enc_bias,
                    attn_scale,
                    patterns[0],
                ],
            )
            blocks[1], info, mixing, scales, live = lax.optimization_barrier((blocks[1], info, mixing, scales, live))
            own, passed = kernel_call(
                functools.partial(values_body, ranges),
                [shape(rows, kv_cols), shape((ranges - 1) * (width // 2), rows, dtype=BF16)],
                [],
                [*blocks, value_rows],
                flops=4 * rows * value_rows.size,
            )
            got = swap(own, "tok", 1)
            passed = swap(passed, "groups", 1)
            packed = [*blocks[1:], passed]
            sends = kernel_call(
                functools.partial(whole_values_body, ranges, width),
                [shape(2 * rows, half, dtype=BF16)] * ranges,
                [],
                [own, got, scales, value_rows],
            )
            got = exchange([sends[0], *sends[:0:-1]])
            carried = [*blocks[1:], *got[1:]]
            code = functools.partial(first_code_body, ranges, per_group)
            given = [*got, *packed, source, mixing]
        else:
            own, other = kernel_call(
                functools.partial(spread_values_body, ranges, 2 * rows),
                [shape(ranges, rows, half), shape(ranges, rows, half, dtype=BF16)],
                [],
                [low, value_rows, *carried],
                flops=2 * rows * value_rows.size,
            )
            got = swap(other, "tok", 1).astype(F32)
            parts = halving([(own[: ranges // 2], got[: ranges // 2]), (own[ranges // 2 :], got[ranges // 2 :])])
            mine = kernel_call(
                scaled_body, shape(ranges, rows, half, dtype=BF16), [], [scales, *parts[0], *parts[1]]
            )
            code = functools.partial(later_code_body, ranges, per_group)
            scalars, given = [], [mine, swap(mine, "tok", 1), low, rest, mixing, *packed]
        middle, own, other = kernel_call(
            code,
            [
                shape(width, rows),
                shape(share, rows, block_len),
                shape(share, rows, block_len, dtype=BF16),
            ],
            [],
            [*given, out_weight, enc_rows, mlp_scale],
            scratch=[pltpu.VMEM((ranges, rows, block_len), F32)],
            flops=2 * rows * (out_weight.size + width * block_len * ranges),
        )
        got = swap(other, "tok", 1)
        if layer == 0:
            sends = kernel_call(
                functools.partial(sums_body, ranges, width, 2 * rows),
                [shape(share * rows + INFO, block_len, dtype=BF16)] * ranges,
                [],
                [own, got, value_rows, info],
            )
            blocks = facts = exchange([sends[0], *sends[:0:-1]])
            carried += blocks[1:]
        else:
            blocks = spread_any((own + got.astype(F32)).astype(BF16).reshape(-1, block_len))
        mine = kernel_call(
            clamp_body,
            shape(share, rows, block_len, dtype=BF16),
            [],
            [*blocks, *facts, live],
        )
        also = swap(mine, "tok", 1)
        more = layer + 1 < layers
        added = [middle, error_cols]
        links = [rest] if layer > 0 else []
        outs = [shape(width, rows), shape(rows, block_len, dtype=BF16)]
        if more:
            outs += [shape(width, rows, dtype=BF16)] * 2
        made = kernel_call(
            functools.partial(decode_body, layer, len(added), len(links), more, kept is not None),
            outs,
            [],
            [mine, also, dec_cols, *added, *links, *(kept or ())],
            flops=2 * rows * dec_cols.size // layers,
        )
        kept = made[:2]
        if more:
            low = handed_on(made[2])
            rest = kernel_call(
                functools.partial(writes_body, layer, len(links)),
                shape(layers - layer, width, rows, dtype=BF16),
                [],
                [mine, also, dec_cols, made[3], *links],
                flops=2 * rows * dec_cols.size,
            )
            rest = handed_on(rest)
    return kept[0].T[None, :, None, :], kept[1][None]


def local(residual_in, attn_scale, mlp_scale, patterns, lengths, value_proj, out_proj, enc_weight, enc_bias, *others):
    whole = (
        residual_in.shape[0] % LANES == 0
        and residual_in.shape[2] % 32 == 0
        and value_proj.shape[3] == out_proj.shape[2]
        and value_proj.shape[3] == 2 * enc_bias.shape[1] == 2 * residual_in.shape[0]
        and residual_in.shape[2] <= residual_in.shape[0] * (2 + lax.axis_size("feat") // 2)
        and lax.axis_size("feat") in (1 << n for n in range(1, 16))
        and lax.axis_size("tok") == lax.axis_size("groups") == 2
    )
    run = tiled if whole else plain
    return run(
        residual_in, attn_scale, mlp_scale, patterns, lengths, value_proj, out_proj, enc_weight, enc_bias, *others
    )


def solution(mesh):
    return jax.shard_map(
        local,
        mesh=mesh,
        in_specs=(
            P("groups", "tok", "feat"),
            P("layer", "groups"),
            P("layer", "groups"),
            P("layer", None, "groups", None, None),
            P("groups"),
            P("layer", "tok", None, "feat"),
            P("layer", None, None, None, "tok", "feat"),
            P("layer", "tok", None, "feat"),
            P("layer", "feat"),
            P("layer", None, None, "tok", "feat"),
            P("layer", "groups", "tok", "feat"),
            P("layer", "feat"),
            P("layer", "feat"),
            P(),
            P("layer", "feat"),
        ),
        out_specs=(P("layer", "groups", "tok", "feat"), P("layer", "groups", "feat")),
        check_vma=False,
    )
```

```python
import functools

import jax
import jax.numpy as jnp
from jax import lax
from jax.experimental import pallas as pl
from jax.experimental.pallas import tpu as pltpu
from jax.sharding import PartitionSpec as P

BF16 = jnp.bfloat16
F32 = jnp.float32


def peers(axis):
    count = lax.axis_size(axis)
    return range(1, count)


def partner(index, step, count):
    if count & (count - 1) == 0:
        return index ^ (count - step)
    return (step - index) % count


def swap(value, axis, step, first_layer=0):
    count = lax.axis_size(axis)
    if first_layer == 0:
        return lax.ppermute(value, axis, [(s, partner(s, step, count)) for s in range(count)])
    layers = lax.axis_size("layer")
    pairs = [
        (s * layers + n, partner(s, step, count) * layers + n)
        for s in range(count)
        for n in range(first_layer, layers)
    ]
    return lax.ppermute(value, (axis, "layer"), pairs)


def spread(value, axis="feat"):
    return [value] + [swap(value, axis, step) for step in peers(axis)]


def spread_any(value):
    return [value] + [swap(value, "feat", step) for step in reversed(peers("feat"))]


def halving(pairs):
    count = lax.axis_size("feat")
    bits = [1 << n for n in range(count.bit_length() - 1)]
    for near, far in zip(bits, reversed(bits)):
        sums = [(a.astype(F32) + b.astype(F32)).astype(BF16) for a, b in pairs]
        got = [swap(value, "feat", count - bit) for value, bit in zip(sums, (near, far))]
        pairs = list(zip(sums, got))
    return pairs


def exchange(sends):
    got = {step: swap(sends[step], "feat", step) for step in reversed(peers("feat"))}
    return [sends[0]] + [got[step] for step in peers("feat")]


def total(blocks):
    result = blocks[0].astype(F32)
    for block in blocks[1:]:
        result = result + block.astype(F32)
    return result


def dot_tn(left, right):
    return lax.dot_general(left, right, (((0,), (0,)), ((), ())), preferred_element_type=F32)


def dot_nt(left, right):
    return lax.dot_general(left, right, (((1,), (1,)), ((), ())), preferred_element_type=F32)


def pick(array, index):
    return lax.dynamic_index_in_dim(array, index, 0, keepdims=False)


def redistribute(weight, ranges, my_range, first_layer):
    blocks = weight.reshape(ranges, -1, weight.shape[1])
    got = [pick(blocks, my_range)]
    for step in peers("feat"):
        other = partner(my_range, step, ranges)
        got.append(swap(pick(blocks, other), "feat", step, first_layer))
    got = jnp.stack(got)
    return [pick(got, partner(my_range, n, ranges)) for n in range(ranges)]


def plain(
    residual_in,
    attn_scale,
    mlp_scale,
    patterns,
    lengths,
    value_proj,
    out_proj,
    enc_weight,
    enc_bias,
    dec_weight,
    errors,
    clamp_mode,
    clamp_index,
    clamp_values,
    active_blocks,
):
    layers = lax.axis_size("layer")
    ranges = lax.axis_size("feat")
    my_layer = lax.axis_index("layer")
    my_range = lax.axis_index("feat")
    my_slab = lax.axis_index("tok")
    prompts, seq = patterns.shape[2:4]
    head_dim, per_group = out_proj.shape[2:4]
    kv_cols = value_proj.shape[3]
    half = kv_cols // 2
    width = residual_in.shape[2]
    block_len = enc_bias.shape[1]
    act = block_len * ranges
    rows = residual_in.shape[0]

    source = residual_in[:, 0, :].T
    error_cols = errors[0, :, 0, :].T
    scale_attn = attn_scale[0]
    scale_mlp = mlp_scale[0]

    chosen = active_blocks[0, 0]
    modes = pick(clamp_mode[0].reshape(-1, block_len), chosen)
    entries = pick(clamp_index[0].reshape(-1, block_len), chosen)
    table_ids = jnp.arange(clamp_values.shape[0], dtype=jnp.int32)
    levels = jnp.sum(jnp.where(entries[:, None] == table_ids[None, :], clamp_values[None, :], 0.0), axis=1)
    gain = jnp.where(modes == 1, 0.0, jnp.where(modes == 2, levels, 1.0))
    shift = jnp.where(modes == 1, levels, 0.0)
    mine = jnp.stack([enc_bias[0], gain, shift])
    got = jnp.stack(spread(mine))
    clamp_all = jnp.stack([pick(got, partner(my_range, n, ranges)) for n in range(ranges)], axis=1).reshape(3, act)
    clamp_half = lax.dynamic_slice_in_dim(clamp_all, my_slab * (act // 2), act // 2, 1)

    positions = jnp.arange(seq, dtype=jnp.int32)
    keep = (positions[None, None, :] <= positions[None, :, None]) & (positions[None, None, :] < lengths[:, None, None])
    masked = jnp.where(keep[None], patterns[0], jnp.zeros_like(patterns[0]))
    zero = jnp.zeros_like(masked[:, 0])
    mixing = jnp.concatenate(
        [
            jnp.concatenate([masked[:, p] if q == p else zero for q in range(prompts)], axis=2)
            for p in range(prompts)
        ],
        axis=1,
    ).reshape(-1, per_group * rows, rows)
    live = (positions[None, :] < lengths[:, None]).reshape(rows)

    value_rows = value_proj[0, 0]
    own_value, other_value = (
        lax.dynamic_slice_in_dim(value_rows, n * half, half, 1) for n in (my_slab, 1 - my_slab)
    )
    out_cols = out_proj[0, :, :, :, 0, :].reshape(ranges, 2, half, per_group, width).transpose(1, 0, 4, 3, 2).reshape(2, ranges, width, per_group * half)
    out_own, out_other = (pick(out_cols, n) for n in (my_slab, 1 - my_slab))
    group_of = [n * kv_cols // head_dim for n in range(ranges)]

    enc_blocks = jnp.concatenate(redistribute(enc_weight[0, 0], ranges, my_range, 0), axis=1)
    enc_own, enc_other = (
        lax.dynamic_slice_in_dim(enc_blocks, n * (act // 2), act // 2, 1) for n in (my_slab, 1 - my_slab)
    )
    value_blocks = redistribute(value_rows, ranges, my_range, 1)
    spread_own, spread_other = (
        jnp.concatenate([lax.dynamic_slice_in_dim(b, n * half, half, 1) for b in value_blocks], axis=1)
        for n in (my_slab, 1 - my_slab)
    )
    dec_cols = dec_weight[0, :, :, 0, :].transpose(0, 2, 1)

    def over_slabs(own, other):
        return own + swap(other, "tok", 1).astype(F32)

    def heads(values, group):
        mixed = jnp.dot(mixing[group] if isinstance(group, int) else pick(mixing, group), values, preferred_element_type=F32)
        return mixed.astype(BF16).reshape(per_group, rows, -1).transpose(1, 0, 2).reshape(rows, -1)

    def first_attention(state):
        normed = (state * scale_attn[None, :]).astype(BF16)
        blocks = spread(normed)
        own_rows, other_rows = (w.reshape(ranges, width, half) for w in (own_value, other_value))
        order = [partner(my_range, n, ranges) if n else my_range for n in range(ranges)]
        other = sum(dot_tn(b, pick(other_rows, n)) for b, n in zip(blocks, order))
        own = sum(dot_tn(b, pick(own_rows, n)) for b, n in zip(blocks, order))
        values = over_slabs(own, other).astype(BF16)
        mine = heads(values, my_range * kv_cols // head_dim)
        got = spread(mine)
        also = [swap(b, "tok", 1) for b in got]
        return sum(
            dot_nt(pick(out_own, n), b) + dot_nt(pick(out_other, n), c) for n, b, c in zip(order, got, also)
        )

    def later_attention(state_low):
        other = dot_tn(state_low, spread_other).astype(BF16)
        own = dot_tn(state_low, spread_own)
        part = over_slabs(own, other).astype(BF16)
        mine = (total(spread(part)) * scale_attn[:, None]).astype(BF16)
        also = swap(mine, "tok", 1)
        result = 0.0
        for n in range(ranges):
            cols = slice(n * half, (n + 1) * half)
            result = (
                result
                + dot_nt(out_own[n], heads(mine[:, cols], group_of[n]))
                + dot_nt(out_other[n], heads(also[:, cols], group_of[n]))
            )
        return result

    def code(middle):
        normed = (middle * scale_mlp[None, :]).astype(BF16)
        other = dot_tn(normed, enc_other).astype(BF16)
        own = dot_tn(normed, enc_own)
        part = over_slabs(own, other).astype(BF16)
        preact = total(spread(part)) + clamp_half[0][None, :]
        clamped = jnp.maximum(preact, 0.0) * clamp_half[1][None, :] + clamp_half[2][None, :]
        mine = jnp.where(live[:, None], clamped, 0.0).astype(BF16)
        also = swap(mine, "tok", 1)
        return jnp.concatenate(
            [jnp.where(my_slab == 0, mine, also), jnp.where(my_slab == 0, also, mine)], axis=1
        )

    def handed_on(value, layer):
        return lax.ppermute(value, "layer", [(layer, layer + 1)])

    states = jnp.zeros_like(source)
    feats = jnp.zeros((rows, block_len), BF16)
    state, links = source, None
    for layer in range(layers):
        if layer == 0:
            middle = state + first_attention(state)
        else:
            middle = low.astype(F32) + later_attention(low) + rest.astype(F32)
        kept = code(middle)
        recon = dot_nt(dec_cols[layer], kept)
        base = middle + error_cols
        if layer > 0:
            base = base + links[0]
        state = base + recon
        states = jnp.where(my_layer == layer, state, states)
        feats = jnp.where(
            my_layer == layer, lax.dynamic_slice_in_dim(kept, my_range * block_len, block_len, 1), feats
        )
        if layer + 1 < layers:
            low = state.astype(BF16)
            left = (state - low.astype(F32)).astype(BF16)
            low = handed_on(low, layer)
            writes = jnp.stack([dot_nt(dec_cols[n], kept) for n in range(layer + 1, layers)])
            if layer > 0:
                writes = writes + links[1:]
            rest = handed_on(left, layer)
            links = handed_on(writes, layer)
    return states.T[None, :, None, :], feats[None]


LANES = 128
INFO = 16


def shape(*sizes, dtype=F32):
    return jax.ShapeDtypeStruct(sizes, dtype)


def kernel_call(body, outs, scalars, arrays, scratch=(), flops=0):
    many = isinstance(outs, (list, tuple))
    kept = list(outs) if many else [outs]
    size = sum(a.size * a.dtype.itemsize for a in arrays) + sum(a.size * a.dtype.itemsize for a in kept)
    return pl.pallas_call(
        body,
        out_shape=tuple(kept) if many else outs,
        in_specs=[pl.BlockSpec(memory_space=pltpu.SMEM)] * len(scalars) + [pl.BlockSpec(memory_space=pltpu.VMEM)] * len(arrays),
        out_specs=tuple(pl.BlockSpec(memory_space=pltpu.VMEM) for _ in kept) if many else pl.BlockSpec(memory_space=pltpu.VMEM),
        scratch_shapes=list(scratch),
        compiler_params=pltpu.CompilerParams(vmem_limit_bytes=16 * 1024 * 1024),
        cost_estimate=pl.CostEstimate(flops=int(flops), bytes_accessed=int(size), transcendentals=0),
    )(*scalars, *arrays)


def place_of():
    return [lax.axis_index(axis) for axis in ("feat", "tok", "layer", "groups")]


def split_terms(value):
    high = value.astype(BF16)
    left = value - high.astype(F32)
    middle = left.astype(BF16)
    low = (left - middle.astype(F32)).astype(BF16)
    return [high, middle, low]


def facts_body(lengths, chosen, table, mode, index, bias, scale, patterns, info, mixing, scales, lives):
    block = chosen[0, 0]
    modes = mode[pl.ds(block, 1), :]
    entries = index[pl.ds(block, 1), :]
    levels = jnp.zeros(entries.shape, F32)
    for n in range(table.shape[0]):
        levels = jnp.where(entries == n, table[n], levels)
    gain = jnp.where(modes == 1, 0.0, jnp.where(modes == 2, levels, 1.0))
    shift = jnp.where(modes == 1, levels, 0.0)
    terms = [t.astype(F32) for v in (bias[...], gain, shift) for t in split_terms(v)]
    info[...] = jnp.concatenate(terms + [jnp.zeros((INFO - len(terms), bias.shape[1]), F32)], axis=0).astype(BF16)
    heads, prompts, seq, _ = patterns.shape
    query = lax.broadcasted_iota(jnp.int32, (seq, seq), 0)
    key = lax.broadcasted_iota(jnp.int32, (seq, seq), 1)
    for p in range(prompts):
        keep = (key <= query) & (key < lengths[p])
        for head in range(heads):
            pattern = jnp.where(keep, patterns[head, p].astype(F32), 0.0)
            zero = jnp.zeros_like(pattern)
            row = jnp.concatenate([pattern if q == p else zero for q in range(prompts)], axis=1)
            mixing[head, p * seq : (p + 1) * seq, :] = row.astype(BF16)
    rows = scale.shape[1]
    scales[...] = jnp.broadcast_to(scale[...], (rows, rows)).T
    row = lax.broadcasted_iota(jnp.int32, lives.shape, 0)
    end = jnp.full(row.shape, lengths[0], jnp.int32)
    for p in range(1, prompts):
        end = jnp.where(row >= p * seq, p * seq + lengths[p], end)
    lives[...] = jnp.where(row < end, 1.0, 0.0)


def start_body(ranges, state, weight, enc, *refs):
    place = place_of()
    sends, (wide, load_sem, sems) = refs[: ranges - 1], refs[ranges - 1 :]
    width, rows = state.shape
    part = width // 2

    def copies(source, first, count, at, group):
        made = []
        for step in range(1, ranges):
            start = pl.multiple_of(partner(place[0], step, ranges) * width + first, 16)
            made.append(
                pltpu.make_async_copy(
                    source.at[pl.ds(start, count), pl.ds(0, rows)],
                    sends[step - 1].at[pl.ds(at, count)],
                    sems.at[group, step - 1],
                )
            )
        return made

    load = pltpu.make_async_copy(state, wide, load_sem)
    rest = copies(enc, place[3] * part, part, width, 0)
    carried = copies(weight, 0, width, 0, 1)

    @pl.when(place[2] == 0)
    def _():
        load.start()
        for copy in rest:
            copy.start()
        load.wait()
        low = wide[...].astype(BF16)
        for send in sends:
            send[0:width] = low
        for copy in rest:
            copy.wait()

    @pl.when(place[2] > 0)
    def _():
        for copy in carried + rest:
            copy.start()
        for copy in carried + rest:
            copy.wait()


def carry(place, ranges, weight, width, first, count, made, sends):
    rows, half = made[0].shape
    for n, block in enumerate(made):
        sends[0][n * rows : (n + 1) * rows] = block
    for step in range(1, ranges):
        other = partner(place[0], step, ranges)
        for n, block in enumerate(made):
            at, size = n * rows, min(max(count - n * rows, 0), rows)
            if size > 0:
                start = pl.multiple_of(other * width + first + at, 16)
                carried = weight[pl.ds(start, size), half:]
                sends[step][at : at + size] = jnp.where(place[2] == 0, block[0:size], carried)
            if size < rows:
                sends[step][at + size : at + rows] = block[size:]


def values_body(ranges, *refs):
    blocks, (weight, own, passed) = refs[:ranges], refs[ranges:]
    width = passed.shape[0] // (ranges - 1) * 2
    place = place_of()
    acc = None
    for step, block in enumerate(blocks):
        n = partner(place[0], step, ranges) if step else place[0]
        if step:
            size = block.shape[0] - width
            passed[(step - 1) * size : step * size] = block[width:]
        part = dot_tn(block[0:width].astype(BF16), weight[pl.ds(pl.multiple_of(n * width, 16), width), :])
        acc = part if acc is None else acc + part
    own[...] = acc


def mix(mixing, head, values):
    return jnp.dot(mixing[head], values, preferred_element_type=F32).astype(BF16)


def whole_values_body(ranges, width, own, got, scales, weight, *sends):
    place = place_of()
    rows, half = scales.shape
    made = [
        ((own[:, n * half : (n + 1) * half] + got[:, n * half : (n + 1) * half]) * scales[...]).astype(BF16)
        for n in range(2)
    ]
    sends = (sends[0], *sends[:0:-1])
    carry(place, ranges, weight, width, 0, 2 * rows, made, sends)


def sums_body(ranges, width, done, own, got, weight, info, *sends):
    place = place_of()
    made = [(own[n] + got[n].astype(F32)).astype(BF16) for n in range(own.shape[0])]
    sends = (sends[0], *sends[:0:-1])
    carry(place, ranges, weight, width, done, width - done, made, sends)
    for send in sends:
        send[send.shape[0] - INFO :] = info[...]


def halves_of(first, mine, theirs):
    return jnp.concatenate([jnp.where(first, mine, theirs), jnp.where(first, theirs, mine)], axis=1)


def spread_values_body(ranges, carried, low, weight, *refs):
    place = place_of()
    others = ranges - 1
    firsts, seconds, thirds = (refs[i * others : (i + 1) * others] for i in range(3))
    own, other = refs[3 * others :]
    width, rows = low.shape
    first = place[1] == 0
    state = low[...]
    for step in range(ranges):
        if step == 0:
            n = place[0]
            both = dot_tn(state, weight[pl.ds(pl.multiple_of(n * width, 16), width), :])
            even, odd = both[:, : own.shape[2]], both[:, own.shape[2] :]
        else:
            n = partner(place[0], step, ranges)
            even = dot_tn(state, firsts[step - 1][0:width])
            odd, at = None, 0
            for piece in (seconds[step - 1], thirds[step - 1]):
                size = min(carried, width - at)
                part = dot_tn(state[at : at + size], piece[0:size])
                odd = part if odd is None else odd + part
                at += size
        own[n] = jnp.where(first, even, odd)
        other[n] = jnp.where(first, odd, even).astype(BF16)


def scaled_body(scales, even, even_got, odd, odd_got, out):
    count = even.shape[0]
    for at, pair in ((0, (even, even_got)), (count, (odd, odd_got))):
        for n in range(count):
            out[at + n] = (total([b[n] for b in pair]) * scales[...]).astype(BF16)


def finish(ranges, place, acc, blocks, passed, enc, weight_scale, middle, own, other, parts):
    width = middle.shape[0]
    size = width // 2
    middle[...] = acc
    normed = (acc * weight_scale[...]).astype(BF16)
    here = place[3] == 0
    mine = jnp.where(here, normed[:size], normed[size:])
    theirs = jnp.where(here, normed[size:], normed[:size])
    parts[place[0]] = dot_tn(normed, enc[pl.ds(pl.multiple_of(place[0] * width, 16), width), :])
    for step in range(1, ranges):
        parts[partner(place[0], step, ranges)] = dot_tn(mine, blocks[step - 1][width:]) + dot_tn(
            theirs, passed[(step - 1) * size : step * size]
        )
    share = ranges // 2
    own[...] = parts[pl.ds(place[1] * share, share)]
    other[...] = parts[pl.ds((1 - place[1]) * share, share)].astype(BF16)


def first_code_body(ranges, per_group, *refs):
    place = place_of()
    got, blocks = refs[:ranges], refs[ranges : 2 * ranges - 1]
    passed, state, mixing, weight, *ends = refs[2 * ranges - 1 :]
    rows = state.shape[1]
    acc = state[...]
    for step in range(ranges):
        n = partner(place[0], step, ranges) if step else place[0]
        values = jnp.concatenate([got[step][0:rows], got[step][rows:]], axis=1)
        for u in range(per_group):
            acc = acc + dot_nt(weight[n * per_group + u], mix(mixing, n * per_group + u, values))
    finish(ranges, place, acc, blocks, passed, *ends)


def later_code_body(ranges, per_group, mine, also, low, rest, mixing, *refs):
    place = place_of()
    blocks = refs[: ranges - 1]
    passed, weight, *ends = refs[ranges - 1 :]
    first = place[1] == 0
    acc = low[...].astype(F32) + rest[0].astype(F32)
    for n in range(ranges):
        values = halves_of(first, mine[n], also[n])
        for u in range(per_group):
            acc = acc + dot_nt(weight[n * per_group + u], mix(mixing, n * per_group + u, values))
    finish(ranges, place, acc, blocks, passed, *ends)


def clamp_body(*refs):
    place = place_of()
    *refs, lives, out = refs
    blocks, facts = refs[: len(refs) // 2], refs[len(refs) // 2 :]
    share, rows, _ = out.shape
    ranges = len(blocks)
    live = lives[...] > 0.5
    terms = [f[f.shape[0] - INFO :].astype(F32) for f in facts]
    terms = [
        [t[3 * i : 3 * i + 1] + t[3 * i + 1 : 3 * i + 2] + t[3 * i + 2 : 3 * i + 3] for i in range(3)] for t in terms
    ]
    for n in range(share):
        number = place[1] * share + n
        bias, gain, shift = terms[0]
        for step in range(1, ranges):
            here = partner(place[0], step, ranges) == number
            bias, gain, shift = (jnp.where(here, b, a) for a, b in zip((bias, gain, shift), terms[step]))
        preact = total([b[n * rows : (n + 1) * rows] for b in blocks]) + bias
        clamped = jnp.maximum(preact, 0.0) * gain + shift
        out[n] = jnp.where(live, clamped, 0.0).astype(BF16)


def ordered(place, mine, also):
    first = place[1] == 0
    share = mine.shape[0]
    return [jnp.where(first, mine[n], also[n]) for n in range(share)] + [
        jnp.where(first, also[n], mine[n]) for n in range(share)
    ]


def decode_body(layer, adds, linked, sends, keeps, *refs):
    place = place_of()
    refs = list(refs)
    take = lambda count: [refs.pop(0) for _ in range(count)]
    (mine, also, dec), added, links, before = take(3), take(adds), take(linked), take(2 if keeps else 0)
    state_out, feats_out = take(2)
    feats = ordered(place, mine, also)
    acc = added[0][...]
    for piece in added[1:]:
        acc = acc + piece[...]
    for piece in links:
        acc = acc + piece[1].astype(F32)
    acc = acc + dot_nt(dec[layer], jnp.concatenate(feats, axis=1))
    block = feats[0]
    for n in range(1, len(feats)):
        block = jnp.where(place[0] == n, feats[n], block)
    if sends:
        low = acc.astype(BF16)
        refs[0][...] = low
        refs[1][...] = (acc - low.astype(F32)).astype(BF16)
    if keeps:
        here = place[2] == layer
        state_out[...] = jnp.where(here, acc, before[0][...])
        feats_out[...] = jnp.where(here, block, before[1][...])
    else:
        state_out[...] = acc
        feats_out[...] = block


def writes_body(layer, linked, mine, also, dec, left, *refs):
    place = place_of()
    out = refs[-1]
    feats = jnp.concatenate(ordered(place, mine, also), axis=1)
    out[0] = left[...]
    for n in range(1, out.shape[0]):
        made = dot_nt(dec[layer + n], feats)
        out[n] = (made + refs[0][n + 1].astype(F32) if linked else made).astype(BF16)


def after(value, *others):
    return lax.optimization_barrier((value, *others))[0]


def tiled(
    residual_in,
    attn_scale,
    mlp_scale,
    patterns,
    lengths,
    value_proj,
    out_proj,
    enc_weight,
    enc_bias,
    dec_weight,
    errors,
    clamp_mode,
    clamp_index,
    clamp_values,
    active_blocks,
):
    layers = lax.axis_size("layer")
    ranges = lax.axis_size("feat")
    seq = patterns.shape[3]
    head_dim, per_group = out_proj.shape[2:4]
    kv_cols = value_proj.shape[3]
    half = kv_cols // 2
    width = residual_in.shape[2]
    block_len = enc_bias.shape[1]
    rows = residual_in.shape[0]
    share = ranges // 2

    source = residual_in[:, 0, :].T
    error_cols = errors[0, :, 0, :].T
    out_weight = out_proj[0, :, :, :, 0, :].transpose(0, 2, 3, 1).reshape(-1, width, head_dim)
    dec_cols = dec_weight[0, :, :, 0, :].transpose(0, 2, 1)
    value_rows = value_proj[0, 0]
    enc_rows = enc_weight[0, 0]

    def handed_on(value):
        return lax.ppermute(value, "layer", [(n, (n + 1) % layers) for n in range(layers)])

    packed = carried = rest = low = kept = None
    for layer in range(layers):
        if layer == 0:
            sends = pl.pallas_call(
                functools.partial(start_body, ranges),
                out_shape=(shape(width + width // 2, rows, dtype=BF16),) * (ranges - 1),
                in_specs=[pl.BlockSpec(memory_space=pltpu.HBM)] * 3,
                out_specs=(pl.BlockSpec(memory_space=pltpu.VMEM),) * (ranges - 1),
                scratch_shapes=[
                    pltpu.VMEM((width, rows), F32),
                    pltpu.SemaphoreType.DMA,
                    pltpu.SemaphoreType.DMA((2, ranges - 1)),
                ],
                compiler_params=pltpu.CompilerParams(vmem_limit_bytes=60 * 1024 * 1024),
            )(source, value_rows, enc_rows)
            blocks = exchange([source, *sends])
            info, mixing, scales, live = kernel_call(
                facts_body,
                [
                    shape(INFO, block_len, dtype=BF16),
                    shape(patterns.shape[1], rows, rows, dtype=BF16),
                    shape(rows, half),
                    shape(rows, block_len),
                ],
                [lengths, active_blocks, clamp_values],
                [
                    clamp_mode.reshape(-1, block_len),
                    clamp_index.reshape(-1, block_len),
                    enc_bias,
                    attn_scale,
                    patterns[0],
                ],
            )
            blocks[1], info, mixing, scales, live = lax.optimization_barrier((blocks[1], info, mixing, scales, live))
            own, passed = kernel_call(
                functools.partial(values_body, ranges),
                [shape(rows, kv_cols), shape((ranges - 1) * (width // 2), rows, dtype=BF16)],
                [],
                [*blocks, value_rows],
                flops=4 * rows * value_rows.size,
            )
            got = swap(own, "tok", 1)
            passed = swap(passed, "groups", 1)
            packed = [*blocks[1:], passed]
            sends = kernel_call(
                functools.partial(whole_values_body, ranges, width),
                [shape(2 * rows, half, dtype=BF16)] * ranges,
                [],
                [own, got, scales, value_rows],
            )
            got = exchange([sends[0], *sends[:0:-1]])
            carried = [*blocks[1:], *got[1:]]
            code = functools.partial(first_code_body, ranges, per_group)
            given = [*got, *packed, source, mixing]
        else:
            own, other = kernel_call(
                functools.partial(spread_values_body, ranges, 2 * rows),
                [shape(ranges, rows, half), shape(ranges, rows, half, dtype=BF16)],
                [],
                [low, value_rows, *carried],
                flops=2 * rows * value_rows.size,
            )
            got = swap(other, "tok", 1).astype(F32)
            parts = halving([(own[: ranges // 2], got[: ranges // 2]), (own[ranges // 2 :], got[ranges // 2 :])])
            mine = kernel_call(
                scaled_body, shape(ranges, rows, half, dtype=BF16), [], [scales, *parts[0], *parts[1]]
            )
            code = functools.partial(later_code_body, ranges, per_group)
            scalars, given = [], [mine, swap(mine, "tok", 1), low, rest, mixing, *packed]
        middle, own, other = kernel_call(
            code,
            [
                shape(width, rows),
                shape(share, rows, block_len),
                shape(share, rows, block_len, dtype=BF16),
            ],
            [],
            [*given, out_weight, enc_rows, mlp_scale],
            scratch=[pltpu.VMEM((ranges, rows, block_len), F32)],
            flops=2 * rows * (out_weight.size + width * block_len * ranges),
        )
        got = swap(other, "tok", 1)
        if layer == 0:
            sends = kernel_call(
                functools.partial(sums_body, ranges, width, 2 * rows),
                [shape(share * rows + INFO, block_len, dtype=BF16)] * ranges,
                [],
                [own, got, value_rows, info],
            )
            blocks = facts = exchange([sends[0], *sends[:0:-1]])
            carried += blocks[1:]
        else:
            blocks = spread_any((own + got.astype(F32)).astype(BF16).reshape(-1, block_len))
        mine = kernel_call(
            clamp_body,
            shape(share, rows, block_len, dtype=BF16),
            [],
            [*blocks, *facts, live],
        )
        also = swap(mine, "tok", 1)
        more = layer + 1 < layers
        added = [middle, error_cols]
        links = [rest] if layer > 0 else []
        outs = [shape(width, rows), shape(rows, block_len, dtype=BF16)]
        if more:
            outs += [shape(width, rows, dtype=BF16)] * 2
        made = kernel_call(
            functools.partial(decode_body, layer, len(added), len(links), more, kept is not None),
            outs,
            [],
            [mine, also, dec_cols, *added, *links, *(kept or ())],
            flops=2 * rows * dec_cols.size // layers,
        )
        kept = made[:2]
        if more:
            low = handed_on(made[2])
            rest = kernel_call(
                functools.partial(writes_body, layer, len(links)),
                shape(layers - layer, width, rows, dtype=BF16),
                [],
                [mine, also, dec_cols, made[3], *links],
                flops=2 * rows * dec_cols.size,
            )
            low, rest = lax.optimization_barrier((low, rest))
            rest = handed_on(rest)
    return kept[0].T[None, :, None, :], kept[1][None]


def local(residual_in, attn_scale, mlp_scale, patterns, lengths, value_proj, out_proj, enc_weight, enc_bias, *others):
    whole = (
        residual_in.shape[0] % LANES == 0
        and residual_in.shape[2] % 32 == 0
        and value_proj.shape[3] == out_proj.shape[2]
        and value_proj.shape[3] == 2 * enc_bias.shape[1] == 2 * residual_in.shape[0]
        and residual_in.shape[2] <= residual_in.shape[0] * (2 + lax.axis_size("feat") // 2)
        and lax.axis_size("feat") in (1 << n for n in range(1, 16))
        and lax.axis_size("tok") == lax.axis_size("groups") == 2
    )
    run = tiled if whole else plain
    return run(
        residual_in, attn_scale, mlp_scale, patterns, lengths, value_proj, out_proj, enc_weight, enc_bias, *others
    )


def solution(mesh):
    return jax.shard_map(
        local,
        mesh=mesh,
        in_specs=(
            P("groups", "tok", "feat"),
            P("layer", "groups"),
            P("layer", "groups"),
            P("layer", None, "groups", None, None),
            P("groups"),
            P("layer", "tok", None, "feat"),
            P("layer", None, None, None, "tok", "feat"),
            P("layer", "tok", None, "feat"),
            P("layer", "feat"),
            P("layer", None, None, "tok", "feat"),
            P("layer", "groups", "tok", "feat"),
            P("layer", "feat"),
            P("layer", "feat"),
            P(),
            P("layer", "feat"),
        ),
        out_specs=(P("layer", "groups", "tok", "feat"), P("layer", "groups", "feat")),
        check_vma=False,
    )
```
